32 devices in a mesh: groups: 2 (over y), row: 8 (over z, x), col: 2 (over core).
Axes of the slice: x: 2, y: 2, z: 4, core: 2. Of those that a mesh axis runs over, the one named last changes fastest.
Arguments:
- gram_old: bfloat16 [28672, 14336], P(('groups', 'row'), 'col'), parts along dimension 0, may hold values from -10 to 256, as said below
- activations: bfloat16 [256, 14336], P('groups', 'row'), parts along dimension 0, may hold values from -0.5 to 0.5
- weights: float32 [14336, 512], P('row', ('groups', 'col')), parts along dimension 1, may hold values from -6 to 6
- block_mask: int32 [112, 4], P(None, 'groups'), parts along dimension 1, may hold values 0 or 1
Outputs:
- pruned: float32 [14336, 512], P('row', ('groups', 'col')), parts along dimension 1
The draws below stay inside these ranges and needn't reach their ends.
There are 2 independent parts, one for each index of `groups`. The reference program is written for one: setup_inputs(seed, part) draws one part's arguments, and reference() takes and returns one part's arrays. A program takes and returns all parts, laid end to end along the dimension named above; each array names one. Nothing has to cross between parts.
Inputs may be any that keep to these rules, and one draw needn't show every extreme that they name: `gram_old`: symmetric and positive definite.
All inputs are finite; a program needn't handle non-finite values.
Results may differ from the reference program's by a relative error of at most 0.00076.
Values may be sent and summed in bfloat16 or wider, within the bound.
No kernel may reach another device: no remote copies, remote signals or barrier semaphores. Data moves between devices by JAX's collectives and lax.ppermute only.
A program may use at most 128 MiB of HBM per device.

```python
import math
import jax
import jax.numpy as jnp

K = 14336
BLK = 128
NCOL = 256
ROWS = 128
KB = 112
NB = 2


def draw_gram_old(key, part):
    key_noise = jax.random.fold_in(key, 11)
    key_scale = jax.random.fold_in(key, 23)
    noise = jax.random.normal(key_noise, (K, K), jnp.float32)
    symmetric = (noise + noise.T) * (1.0 / math.sqrt(2.0 * K))
    base = 3.0 * jnp.eye(K, dtype=jnp.float32) + symmetric
    position = jnp.arange(K, dtype=jnp.float32) / K
    uniform_draw = jax.random.uniform(key_scale, (K,), jnp.float32)
    squares = jnp.exp(uniform_draw * math.log(10.0)) * (1.0 + 2.0 * position)
    scales = jnp.sqrt(squares)
    return (scales[:, None] * base * scales[None, :]).astype(jnp.bfloat16)


def place_ends(values, stream_key, least, largest):
    shape = values.shape
    spot = [jax.random.randint(jax.random.fold_in(stream_key, axis), (), 0, shape[axis]) for axis in range(len(shape))]
    values = values.at[tuple(spot)].set(least)
    longest = shape.index(max(shape))
    spot[longest] = (spot[longest] + 1) % shape[longest]
    return values.at[tuple(spot)].set(largest)


def block_scale(stream_key, dims, split, smallest, largest):
    level, own = 1.0, jax.random.fold_in(stream_key, 6)
    for dim, parts in split:
        steps = jnp.exp(jax.random.uniform(jax.random.fold_in(own, dim), (parts,), jnp.float32, smallest / len(split), largest / len(split)))
        level = level * jnp.repeat(steps, dims[dim] // parts).reshape([-1 if axis == dim else 1 for axis in range(len(dims))])
    return level


def bell_draw(key, dims, deviation, limit, cuts=(), kind=jnp.bfloat16):
    factor_of = block_scale(key, dims, cuts, -0.22, 0.18) if cuts else 1.0
    result = jax.random.normal(key, dims, jnp.float32) * deviation * factor_of
    return jnp.minimum(jnp.maximum(result, -limit), limit).astype(kind)


def setup_inputs(seed: int = 0, part: int = 0) -> dict:
    splits = jax.random.split(jax.random.key(seed), 5)
    part_keys = jax.random.split(jax.random.fold_in(splits[4], part), 5)
    gram_old = draw_gram_old(jax.random.fold_in(jax.random.fold_in(splits[4], part), 71), part)
    activations = bell_draw(part_keys[1], (ROWS, K), ROWS ** -0.5, 0.5, ((1, 8),))
    weights = bell_draw(part_keys[2], (K, NCOL), 1.0, 6.0, ((0, 8), (1, 2)), jnp.float32)
    block_mask = place_ends((jax.random.randint(part_keys[3], (KB, NB), 0, 2) < 1).astype(jnp.int32), jax.random.fold_in(part_keys[3], 1), 0, 1)
    return {"gram_old": gram_old, "activations": activations, "weights": weights, "block_mask": block_mask}


damping_ratio = 0.3
epsilon = 1e-6


def expand_mask(block_mask):
    widened = jnp.repeat(block_mask.astype(jnp.float32), BLK, axis=0)
    return jnp.repeat(widened, BLK, axis=1)


def reference(gram_old, activations, weights, block_mask):
    gram_update = jnp.dot(activations.T, activations, preferred_element_type=jnp.float32)
    gram_new = (gram_old.astype(jnp.float32) + gram_update).astype(jnp.bfloat16)
    trace_total = jnp.sum(jnp.diagonal(gram_new).astype(jnp.float32))
    damping = damping_ratio * trace_total / K
    mask_full = expand_mask(block_mask)
    kept_weights = mask_full * weights
    pruned_diff = kept_weights - weights
    grad_first = jnp.dot(gram_new, pruned_diff.astype(jnp.bfloat16), preferred_element_type=jnp.float32)
    step_dir = mask_full * grad_first
    curvature = jnp.dot(gram_new, step_dir.astype(jnp.bfloat16), preferred_element_type=jnp.float32)
    masked_curve = mask_full * curvature
    grad_square = jnp.sum(step_dir * step_dir)
    grad_curve = jnp.sum(step_dir * curvature)
    curve_square = jnp.sum(masked_curve * masked_curve)
    step_first = grad_square / (grad_curve + damping * grad_square + epsilon)
    step_second = (grad_curve + damping * grad_square) / (curve_square + 2.0 * damping * grad_curve + damping * damping * grad_square + epsilon)
    grad_second = grad_first - step_first * curvature
    return kept_weights - step_first * step_dir - step_second * (mask_full * grad_second)
```

```python
import functools

import jax
import jax.numpy as jnp
from jax import lax
from jax.experimental import pallas as pl
from jax.experimental.pallas import tpu as pltpu
from jax.sharding import PartitionSpec as P

BLK = 128
TILE = 256

damping_ratio = 0.3
epsilon = 1e-06


def swap(value, axis, distance):
    return lax.ppermute(value, axis, [(i, i ^ distance) for i in range(lax.axis_size(axis))])


def expand_local(block_mask, row_index, row_block, col_index, width_cols):
    if width_cols != BLK:
        row_ids = (row_index * row_block + jnp.arange(row_block, dtype=jnp.int32)) // BLK
        col_ids = (col_index * width_cols + jnp.arange(width_cols, dtype=jnp.int32)) // BLK
        return block_mask[row_ids][:, col_ids].astype(jnp.float32)
    piece = BLK
    while row_block % piece:
        piece //= 2
    column = lax.dynamic_index_in_dim(block_mask, col_index, 1, keepdims=False)
    column = jnp.repeat(column, BLK // piece) if piece != BLK else column
    count = row_block // piece
    own = lax.dynamic_slice_in_dim(column, row_index * count, count, 0).astype(jnp.float32)
    return jnp.broadcast_to(own[:, None, None], (count, piece, width_cols)).reshape(
        row_block, width_cols
    )


class Ring:
    def __init__(self, count):
        self.count = count
        self.order = list(range(0, count, 2)) + list(range(count - 1, 0, -2))

    def half(self, place):
        return self.order[place % self.count] * 2 // self.count

    def device(self, place, core):
        return self.order[place % self.count] * 2 + core

    def shift(self, step, sign):
        pairs = []
        for place in range(self.count):
            core = self.half(place - sign * step)
            pairs.append((self.device(place, core), self.device(place + sign, core)))
        return pairs

    def collect(self):
        pairs = []
        for place in range(self.count):
            core = self.half(place)
            pairs.append((self.device(place, 1 - core), self.device(place, core)))
        return pairs

    def source(self, row_index, distance):
        place = jnp.where(
            row_index % 2 == 0, row_index // 2, self.count - 1 - row_index // 2
        )
        place = (place + distance) % self.count
        return jnp.where(place < self.count // 2, 2 * place, 2 * (self.count - 1 - place) + 1)


def product_kernel(parts, first, with_diag, scalars, *refs):
    refs = list(refs)
    operands = [tuple(refs[3 * k : 3 * k + 3]) for k in range(parts)]
    refs = refs[3 * parts :]
    if first:
        own_ref, other_ref = refs[:2]
        own_ref[...] = jnp.zeros_like(own_ref)
        other_ref[...] = jnp.zeros_like(other_ref)
    else:
        own_in, other_in, own_ref, other_ref = refs[:4]
        own_ref[...] = own_in[...]
        other_ref[...] = other_in[...]
    for k, (gram, own_panel, other_panel) in enumerate(operands):

        @pl.when(scalars[2 * k + 1] == 1)
        def _():
            panel = jnp.concatenate([own_panel[...], other_panel[...]], axis=1)
            result = jnp.dot(gram[...], panel, preferred_element_type=jnp.float32)
            width = own_panel.shape[1]
            own_ref[...] += result[:, :width]
            other_ref[...] += result[:, width:]

    if with_diag:
        diag_ref = refs[-1]
        gram = operands[0][0]
        start = pl.multiple_of(pl.program_id(0) * TILE, TILE)
        square = gram[:, pl.ds(start, TILE)].astype(jnp.float32)
        rows = lax.broadcasted_iota(jnp.int32, (TILE, TILE), 0)
        cols = lax.broadcasted_iota(jnp.int32, (TILE, TILE), 1)
        picked = jnp.sum(jnp.where(rows == cols, square, 0.0), axis=0, keepdims=True)
        diag_ref[...] = jnp.broadcast_to(picked, diag_ref.shape)


def product(gram, parts, acc, with_diag=False):
    rows, _ = gram.shape
    depth, width = parts[0][2].shape
    steps = rows // TILE
    scalars = jnp.stack([jnp.asarray(v, jnp.int32) for part in parts for v in part[:2]])
    in_specs, operands = [], []
    for k, part in enumerate(parts):
        in_specs.append(pl.BlockSpec((TILE, depth), lambda i, s, k=k: (i * s[2 * k + 1], s[2 * k])))
        in_specs += [pl.BlockSpec((depth, width), lambda i, s: (0, 0))] * 2
        operands += [gram, part[2], part[3]]
    tile = pl.BlockSpec((TILE, width), lambda i, s: (i, 0))
    aliases = {}
    if acc is not None:
        aliases = {1 + len(operands): 0, 2 + len(operands): 1}
        in_specs += [tile, tile]
        operands += list(acc)
    out_specs = [tile, tile]
    out_shape = [jax.ShapeDtypeStruct((rows, width), jnp.float32)] * 2
    if with_diag:
        out_specs.append(pl.BlockSpec((8, TILE), lambda i, s: (0, i)))
        out_shape.append(jax.ShapeDtypeStruct((8, rows), jnp.float32))
    return pl.pallas_call(
        functools.partial(product_kernel, len(parts), acc is None, with_diag),
        grid_spec=pltpu.PrefetchScalarGridSpec(
            num_scalar_prefetch=1, grid=(steps,), in_specs=in_specs, out_specs=out_specs
        ),
        out_shape=out_shape,
        input_output_aliases=aliases,
        compiler_params=pltpu.CompilerParams(vmem_limit_bytes=32 * 1024 * 1024),
        cost_estimate=pl.CostEstimate(
            flops=len(parts) * 4 * rows * depth * width,
            bytes_accessed=len(parts) * 2 * rows * depth,
            transcendentals=0,
        ),
    )(scalars, *operands)


def sum_rows(value, count):
    distance = 1
    while distance < count:
        value = value + swap(value, "row", distance)
        distance *= 2
    return value


def ring_apply(ring, gram, activations, panel, row_index, col_index, with_diag):
    axes = ("row", "col")
    count = ring.count
    half = count // 2

    def part(distance, own, other):
        source = ring.source(row_index, distance)
        active = (source // half == col_index).astype(jnp.int32)
        return (source % half, active, own, other)

    low = jnp.dot(activations, panel, preferred_element_type=jnp.float32)
    ahead = [panel, None]
    back = [panel, None]
    other = lax.ppermute(panel, axes, ring.collect())
    ahead[1] = back[1] = other
    acc = product(gram, [part(0, panel, other)], None, with_diag)
    diag = acc[2] if with_diag else None
    acc = acc[:2]
    for step in range(half - 1):
        for chunk in range(2):
            ahead[chunk] = lax.ppermute(ahead[chunk], axes, ring.shift(step, 1))
            back[chunk] = lax.ppermute(back[chunk], axes, ring.shift(step, -1))
        acc = product(gram, [part(-1 - step, *ahead), part(1 + step, *back)], acc)
    last_own = lax.ppermute(ahead[0], axes, ring.shift(half - 1, 1))
    last_other = lax.ppermute(back[1], axes, ring.shift(half - 1, -1))
    own, partial = product(gram, [part(half, last_own, last_other)], acc)
    low = sum_rows(low, count)
    low_high = low.astype(jnp.bfloat16)
    low_rest = (low - low_high.astype(jnp.float32)).astype(jnp.bfloat16)
    contract = (((0,), (0,)), ((), ()))
    update = lax.dot_general(
        activations, low_high, contract, preferred_element_type=jnp.float32
    ) + lax.dot_general(activations, low_rest, contract, preferred_element_type=jnp.float32)
    return own + swap(partial, "col", 1) + update, diag


def gather_apply(gram, activations, panel, col_index):
    half = gram.shape[1]
    full = lax.all_gather(panel, "row", axis=0, tiled=True)
    own_half = lax.dynamic_slice_in_dim(full, col_index * half, half, 0)
    need = lax.dynamic_slice_in_dim(full, (1 - col_index) * half, half, 0)
    other_half = swap(need, "col", 1)
    own = jnp.dot(gram, own_half, preferred_element_type=jnp.float32)
    partial = jnp.dot(gram, other_half, preferred_element_type=jnp.float32)
    low = lax.psum(jnp.dot(activations, panel, preferred_element_type=jnp.float32), "row")
    update = lax.dot_general(
        activations.astype(jnp.float32),
        low,
        (((0,), (0,)), ((), ())),
        precision=lax.Precision.HIGHEST,
        preferred_element_type=jnp.float32,
    )
    return own + swap(partial, "col", 1) + update


def per_device(gram_old, activations, weights, block_mask):
    row_block, half_width = gram_old.shape
    width_cols = weights.shape[1]
    count = lax.axis_size("row")
    units = count * row_block
    row_index = lax.axis_index("row")
    col_index = lax.axis_index("col")
    ringed = row_block % TILE == 0 and count in (4, 8, 16) and width_cols % BLK == 0
    mask_local = expand_local(block_mask, row_index, row_block, col_index, width_cols)
    kept_weights = mask_local * weights
    diff_low = (kept_weights - weights).astype(jnp.bfloat16)
    acts = activations.astype(jnp.float32)
    column_squares = jnp.sum(acts * acts, axis=0)
    if ringed:
        ring = Ring(count)
        grad_first, diag = ring_apply(
            ring, gram_old, activations, diff_low, row_index, col_index, True
        )
        holds = (row_index * 2 // count == col_index).astype(jnp.float32)
        new_diag = (diag[0] + column_squares).astype(jnp.bfloat16).astype(jnp.float32)
        trace_part = holds * jnp.sum(new_diag)
    else:
        grad_first = gather_apply(gram_old, activations, diff_low, col_index)
        place = row_index * row_block + jnp.arange(row_block, dtype=jnp.int32)
        place = place - col_index * half_width
        on_diagonal = jnp.arange(half_width, dtype=jnp.int32)[None, :] == place[:, None]
        new_gram = gram_old.astype(jnp.float32) + column_squares[:, None]
        new_gram = new_gram.astype(jnp.bfloat16).astype(jnp.float32)
        trace_part = jnp.sum(jnp.where(on_diagonal, new_gram, 0.0))
    step_dir = mask_local * grad_first
    step_low = step_dir.astype(jnp.bfloat16)
    if ringed:
        curvature, _ = ring_apply(
            ring, gram_old, activations, step_low, row_index, col_index, False
        )
    else:
        curvature = gather_apply(gram_old, activations, step_low, col_index)
    masked_curve = mask_local * curvature
    sums = jnp.stack(
        [
            trace_part,
            jnp.sum(step_dir * step_dir),
            jnp.sum(step_dir * curvature),
            jnp.sum(masked_curve * masked_curve),
        ]
    )
    if ringed:
        sums = sum_rows(sums + swap(sums, "col", 1), count)
    else:
        sums = lax.psum(sums, ("row", "col"))
    trace_total, grad_square, grad_curve, curve_square = sums[0], sums[1], sums[2], sums[3]
    damping = damping_ratio * trace_total / units
    step_first = grad_square / (grad_curve + damping * grad_square + epsilon)
    step_second = (grad_curve + damping * grad_square) / (
        curve_square + 2.0 * damping * grad_curve + damping * damping * grad_square + epsilon
    )
    grad_second = grad_first - step_first * curvature
    return kept_weights - step_first * step_dir - step_second * (mask_local * grad_second)


def solution(mesh):
    placed = (
        P(("groups", "row"), "col"),
        P("groups", "row"),
        P("row", ("groups", "col")),
        P(None, "groups"),
    )
    return jax.shard_map(
        per_device,
        mesh=mesh,
        in_specs=placed,
        out_specs=P("row", ("groups", "col")),
        check_vma=False,
    )
```

```python
import functools

import jax
import jax.numpy as jnp
from jax import lax
from jax.experimental import pallas as pl
from jax.experimental.pallas import tpu as pltpu
from jax.sharding import PartitionSpec as P

BLK = 128
TILE = 256
LIMIT = 48 * 1024 * 1024

damping_ratio = 0.3
epsilon = 1e-06


def swap(value, axis, distance):
    return lax.ppermute(value, axis, [(i, i ^ distance) for i in range(lax.axis_size(axis))])


def sum_rows(value, count):
    distance = 1
    while distance < count:
        value = value + swap(value, "row", distance)
        distance *= 2
    return value


def expand_local(block_mask, row_index, row_block, col_index, width_cols):
    if width_cols != BLK:
        row_ids = (row_index * row_block + jnp.arange(row_block, dtype=jnp.int32)) // BLK
        col_ids = (col_index * width_cols + jnp.arange(width_cols, dtype=jnp.int32)) // BLK
        return block_mask[row_ids][:, col_ids].astype(jnp.float32)
    piece = BLK
    while row_block % piece:
        piece //= 2
    column = lax.dynamic_index_in_dim(block_mask, col_index, 1, keepdims=False)
    column = jnp.repeat(column, BLK // piece) if piece != BLK else column
    count = row_block // piece
    own = lax.dynamic_slice_in_dim(column, row_index * count, count, 0).astype(jnp.float32)
    return jnp.broadcast_to(own[:, None, None], (count, piece, width_cols)).reshape(
        row_block, width_cols
    )


def gather_two_ways(panel, count):
    groups = [
        [2 * row for row in range(count)],
        [2 * row + 1 for row in range(count - 1, -1, -1)],
    ]
    return lax.all_gather(
        panel, ("row", "col"), axis=0, tiled=True, axis_index_groups=groups
    )


def product_kernel(scalars, gram, own_panel, other_panel, own_ref, other_ref, *rest):
    step = pl.program_id(0)
    rows, depth = gram.shape
    width = own_panel.shape[1]

    @pl.when(step == 0)
    def _():
        own_ref[...] = jnp.zeros_like(own_ref)
        other_ref[...] = jnp.zeros_like(other_ref)

    @pl.loop(0, rows // TILE)
    def _(tile):
        here = pl.ds(pl.multiple_of(tile * TILE, TILE), TILE)
        panel = jnp.concatenate([own_panel[...], other_panel[...]], axis=1)
        result = jnp.dot(gram[here, :], panel, preferred_element_type=jnp.float32)
        own_ref[here, :] += result[:, :width]
        other_ref[here, :] += result[:, width:]

    if rest:
        (diag_ref,) = rest
        pieces = rows // depth
        first = scalars[1]

        @pl.when(step == 0)
        def _():
            diag_ref[...] = jnp.zeros_like(diag_ref)

        @pl.when((step >= first) & (step < first + pieces))
        def _():
            piece = step - first
            lanes = lax.broadcasted_iota(jnp.int32, (BLK, BLK), 0)
            same = lanes == lax.broadcasted_iota(jnp.int32, (BLK, BLK), 1)
            for block in range(depth // BLK):
                start = pl.multiple_of(piece * depth + block * BLK, BLK)
                square = gram[pl.ds(start, BLK), block * BLK : (block + 1) * BLK]
                picked = jnp.where(same, square.astype(jnp.float32), 0.0)
                diag_ref[:, pl.ds(start, BLK)] = jnp.broadcast_to(
                    jnp.sum(picked, axis=0, keepdims=True), (8, BLK)
                )


def product(gram, own_panel, other_panel, row_index, col_index, count, with_diag):
    rows, cols = gram.shape
    width = own_panel.shape[1]
    half = count // 2
    pieces = 2
    depth = rows // pieces
    first = jnp.where(row_index // half == col_index, (row_index % half) * pieces, 2 * half * pieces)
    scalars = jnp.stack([col_index, first]).astype(jnp.int32)

    def place(flip):
        def index(k, s):
            block, piece = k // pieces, k % pieces
            turned = jnp.where(s[0] == flip, half - 1 - block, block)
            return turned * pieces + piece, 0

        return index

    whole = pl.BlockSpec((rows, width), lambda k, s: (0, 0))
    out_specs = [whole, whole]
    out_shape = [jax.ShapeDtypeStruct((rows, width), jnp.float32)] * 2
    if with_diag:
        out_specs.append(pl.BlockSpec((8, rows), lambda k, s: (0, 0)))
        out_shape.append(jax.ShapeDtypeStruct((8, rows), jnp.float32))
    return pl.pallas_call(
        product_kernel,
        grid_spec=pltpu.PrefetchScalarGridSpec(
            num_scalar_prefetch=1,
            grid=(half * pieces,),
            in_specs=[
                pl.BlockSpec((rows, depth), lambda k, s: (0, k)),
                pl.BlockSpec((depth, width), place(1)),
                pl.BlockSpec((depth, width), place(0)),
            ],
            out_specs=out_specs,
        ),
        out_shape=out_shape,
        compiler_params=pltpu.CompilerParams(vmem_limit_bytes=LIMIT),
        cost_estimate=pl.CostEstimate(
            flops=4 * rows * cols * width, bytes_accessed=2 * rows * cols, transcendentals=0
        ),
    )(scalars, gram, own_panel, other_panel)


def low_update(activations, panel, count):
    low = jnp.dot(activations, panel, preferred_element_type=jnp.float32)
    low = sum_rows(low, count)
    low_high = low.astype(jnp.bfloat16)
    low_rest = (low - low_high.astype(jnp.float32)).astype(jnp.bfloat16)
    contract = (((0,), (0,)), ((), ()))
    return lax.dot_general(
        activations, low_high, contract, preferred_element_type=jnp.float32
    ) + lax.dot_general(activations, low_rest, contract, preferred_element_type=jnp.float32)


def ring_apply(gram, activations, panel, row_index, col_index, count, with_diag):
    full = gather_two_ways(panel, count)
    half = full.shape[0] // 2
    other = swap(full[half:], "col", 1)
    results = product(gram, full[:half], other, row_index, col_index, count, with_diag)
    update = low_update(activations, panel, count)
    return results[0], swap(results[1], "col", 1), update, results[2:]


def lane_sums(value):
    return jnp.sum(value, axis=0, keepdims=True)


def curve_kernel(scalars, trace, grad, own, received, update, blocks, curve_ref, sums_ref):
    rows = grad.shape[0]
    sums_ref[...] = jnp.zeros_like(sums_ref)
    sums_ref[0:1, :] = trace[0:1, :]
    for block in range(rows // BLK):
        here = slice(block * BLK, (block + 1) * BLK)
        kept = blocks[block : block + 1, :]
        curve = own[here, :] + received[here, :] + update[here, :]
        curve_ref[here, :] = curve
        step_dir = kept * grad[here, :]
        masked = kept * curve
        sums_ref[1:2, :] += lane_sums(step_dir * step_dir)
        sums_ref[2:3, :] += lane_sums(step_dir * curve)
        sums_ref[3:4, :] += lane_sums(masked * masked)


def last_kernel(units, sums, grad, curve, weights, blocks, out_ref):
    totals = jnp.sum(sums[...], axis=1, keepdims=True)
    trace_total, grad_square = totals[0:1, :], totals[1:2, :]
    grad_curve, curve_square = totals[2:3, :], totals[3:4, :]
    damping = damping_ratio * trace_total / units
    step_first = grad_square / (grad_curve + damping * grad_square + epsilon)
    step_second = (grad_curve + damping * grad_square) / (
        curve_square + 2.0 * damping * grad_curve + damping * damping * grad_square + epsilon
    )
    rows = grad.shape[0]
    for block in range(rows // BLK):
        here = slice(block * BLK, (block + 1) * BLK)
        kept = blocks[block : block + 1, :]
        grad_first = grad[here, :]
        step_dir = kept * grad_first
        grad_second = grad_first - step_first * curve[here, :]
        out_ref[here, :] = (
            kept * weights[here, :] - step_first * step_dir - step_second * (kept * grad_second)
        )


def gather_apply(gram, activations, panel, col_index):
    half = gram.shape[1]
    full = lax.all_gather(panel, "row", axis=0, tiled=True)
    own_half = lax.dynamic_slice_in_dim(full, col_index * half, half, 0)
    need = lax.dynamic_slice_in_dim(full, (1 - col_index) * half, half, 0)
    other_half = swap(need, "col", 1)
    own = jnp.dot(gram, own_half, preferred_element_type=jnp.float32)
    partial = jnp.dot(gram, other_half, preferred_element_type=jnp.float32)
    low = lax.psum(jnp.dot(activations, panel, preferred_element_type=jnp.float32), "row")
    update = lax.dot_general(
        activations.astype(jnp.float32),
        low,
        (((0,), (0,)), ((), ())),
        precision=lax.Precision.HIGHEST,
        preferred_element_type=jnp.float32,
    )
    return own + swap(partial, "col", 1) + update


def per_device_general(gram_old, activations, weights, block_mask):
    row_block, half_width = gram_old.shape
    width_cols = weights.shape[1]
    units = lax.axis_size("row") * row_block
    row_index = lax.axis_index("row")
    col_index = lax.axis_index("col")
    mask_local = expand_local(block_mask, row_index, row_block, col_index, width_cols)
    kept_weights = mask_local * weights
    diff_low = (kept_weights - weights).astype(jnp.bfloat16)
    acts = activations.astype(jnp.float32)
    column_squares = jnp.sum(acts * acts, axis=0)
    grad_first = gather_apply(gram_old, activations, diff_low, col_index)
    place = row_index * row_block + jnp.arange(row_block, dtype=jnp.int32)
    place = place - col_index * half_width
    on_diagonal = jnp.arange(half_width, dtype=jnp.int32)[None, :] == place[:, None]
    new_gram = gram_old.astype(jnp.float32) + column_squares[:, None]
    new_gram = new_gram.astype(jnp.bfloat16).astype(jnp.float32)
    trace_part = jnp.sum(jnp.where(on_diagonal, new_gram, 0.0))
    step_dir = mask_local * grad_first
    curvature = gather_apply(gram_old, activations, step_dir.astype(jnp.bfloat16), col_index)
    masked_curve = mask_local * curvature
    sums = jnp.stack(
        [
            trace_part,
            jnp.sum(step_dir * step_dir),
            jnp.sum(step_dir * curvature),
            jnp.sum(masked_curve * masked_curve),
        ]
    )
    sums = lax.psum(sums, ("row", "col"))
    trace_total, grad_square, grad_curve, curve_square = sums[0], sums[1], sums[2], sums[3]
    damping = damping_ratio * trace_total / units
    step_first = grad_square / (grad_curve + damping * grad_square + epsilon)
    step_second = (grad_curve + damping * grad_square) / (
        curve_square + 2.0 * damping * grad_curve + damping * damping * grad_square + epsilon
    )
    grad_second = grad_first - step_first * curvature
    return kept_weights - step_first * step_dir - step_second * (mask_local * grad_second)


def per_device(gram_old, activations, weights, block_mask):
    row_block, _ = gram_old.shape
    width_cols = weights.shape[1]
    count = lax.axis_size("row")
    if row_block % (2 * BLK) or count not in (4, 8, 16) or width_cols != BLK:
        return per_device_general(gram_old, activations, weights, block_mask)
    row_index = lax.axis_index("row")
    col_index = lax.axis_index("col")
    per_block = row_block // BLK
    own_mask = lax.dynamic_slice(block_mask, (row_index * per_block, col_index), (per_block, 1))
    blocks = jnp.broadcast_to(own_mask.astype(jnp.float32), (per_block, width_cols))
    mask_local = jnp.broadcast_to(blocks[:, None, :], (per_block, BLK, width_cols))
    mask_local = mask_local.reshape(row_block, width_cols)
    diff_low = (mask_local * weights - weights).astype(jnp.bfloat16)
    own, received, update, (diag,) = ring_apply(
        gram_old, activations, diff_low, row_index, col_index, count, True
    )
    acts = activations.astype(jnp.float32)
    holds = (row_index * 2 // count == col_index).astype(jnp.float32)
    new_diag = (diag[0] + jnp.sum(acts * acts, axis=0)).astype(jnp.bfloat16).astype(jnp.float32)
    trace = holds * jnp.sum(new_diag.reshape(per_block, BLK), axis=0)
    trace = jnp.broadcast_to(trace[None, :], (8, BLK))
    grad_first = own + received + update
    step_low = (mask_local * grad_first).astype(jnp.bfloat16)
    own, received, update, _ = ring_apply(
        gram_old, activations, step_low, row_index, col_index, count, False
    )
    whole = pl.BlockSpec(memory_space=pltpu.VMEM)
    params = pltpu.CompilerParams(vmem_limit_bytes=LIMIT)
    panel_shape = jax.ShapeDtypeStruct((row_block, width_cols), jnp.float32)
    curve, sums = pl.pallas_call(
        functools.partial(curve_kernel, None),
        in_specs=[whole] * 6,
        out_specs=[whole] * 2,
        out_shape=[panel_shape, jax.ShapeDtypeStruct((8, BLK), jnp.float32)],
        compiler_params=params,
    )(trace, grad_first, own, received, update, blocks)
    sums = sum_rows(sums + swap(sums, "col", 1), count)
    return pl.pallas_call(
        functools.partial(last_kernel, float(count * row_block)),
        in_specs=[whole] * 5,
        out_specs=whole,
        out_shape=panel_shape,
        compiler_params=params,
    )(sums, grad_first, curve, weights, blocks)


def solution(mesh):
    placed = (
        P(("groups", "row"), "col"),
        P("groups", "row"),
        P("row", ("groups", "col")),
        P(None, "groups"),
    )
    return jax.shard_map(
        per_device,
        mesh=mesh,
        in_specs=placed,
        out_specs=P("row", ("groups", "col")),
        check_vma=False,
    )
```

```python
import functools

import jax
import jax.numpy as jnp
from jax import lax
from jax.experimental import pallas as pl
from jax.experimental.pallas import tpu as pltpu
from jax.sharding import PartitionSpec as P

BLK = 128
TILE = 256
LIMIT = 48 * 1024 * 1024
AXES = ("row", "col")

damping_ratio = 0.3
epsilon = 1e-06


def swap(value, axis, distance):
    return lax.ppermute(value, axis, [(i, i ^ distance) for i in range(lax.axis_size(axis))])


def sum_rows(value, count):
    distance = 1
    while distance < count:
        value = value + swap(value, "row", distance)
        distance *= 2
    return value


def expand_local(block_mask, row_index, row_block, col_index, width_cols):
    if width_cols != BLK:
        row_ids = (row_index * row_block + jnp.arange(row_block, dtype=jnp.int32)) // BLK
        col_ids = (col_index * width_cols + jnp.arange(width_cols, dtype=jnp.int32)) // BLK
        return block_mask[row_ids][:, col_ids].astype(jnp.float32)
    piece = BLK
    while row_block % piece:
        piece //= 2
    column = lax.dynamic_index_in_dim(block_mask, col_index, 1, keepdims=False)
    column = jnp.repeat(column, BLK // piece) if piece != BLK else column
    count = row_block // piece
    own = lax.dynamic_slice_in_dim(column, row_index * count, count, 0).astype(jnp.float32)
    return jnp.broadcast_to(own[:, None, None], (count, piece, width_cols)).reshape(
        row_block, width_cols
    )


class Ring:
    def __init__(self, count):
        self.count = count
        self.order = list(range(0, count, 2)) + list(range(count - 1, 0, -2))
        self.last = count // 2 - 1

    def row(self, place):
        return self.order[place % self.count]

    def half(self, place):
        return self.row(place) * 2 // self.count

    def ahead(self, place):
        return int(place % self.count >= self.count // 2)

    def device(self, place, core):
        return self.row(place) * 2 + core

    def source(self, place, core, step):
        return place - 1 - step if core == self.ahead(place) else place + 1 + step

    def first_column(self, place, core, step):
        origin = self.ahead(self.source(place, core, step))
        return origin if core == self.ahead(place) else 1 - origin

    def places(self):
        return [(place, core) for place in range(self.count) for core in range(2)]

    def shift(self):
        pairs = []
        for place in range(self.count):
            pairs.append(
                (self.device(place, self.ahead(place)), self.device(place + 1, self.ahead(place + 1)))
            )
            pairs.append(
                (
                    self.device(place, 1 - self.ahead(place)),
                    self.device(place - 1, 1 - self.ahead(place - 1)),
                )
            )
        return pairs

    def hand_over(self, step):
        return [
            (self.device(place, core), self.device(place, 1 - core))
            for place, core in self.places()
            if self.half(self.source(place, core, step)) != core
        ]

    def close(self, sign):
        pairs = []
        for place in range(self.count):
            core = self.ahead(place - sign)
            core = core if sign > 0 else 1 - core
            target = self.half(place + self.count // 2)
            pairs.append((self.device(place - sign, core), self.device(place, target)))
        return pairs

    def table(self):
        half = self.count // 2
        lines = [None] * (2 * self.count)
        for place, core in self.places():
            line = [self.row(place) % half, int(self.half(place) == core), 0]
            for step in range(self.last):
                for carrier in (core, 1 - core):
                    source = self.source(place, carrier, step)
                    line += [
                        self.row(source) % half,
                        int(self.half(source) == core),
                        int(self.first_column(place, carrier, step) != core),
                    ]
            far = place + half
            line += [
                self.row(far) % half,
                int(self.half(far) == core),
                int(self.ahead(far) != core),
            ]
            lines[self.device(place, core)] = line
        return lines


def product_kernel(
    slot, with_trace, scalars, gram, first, second, across, acts, own_in, other_in, *refs
):
    if with_trace:
        own, other, trace, tiles, sems = refs
        trace[...] = jnp.zeros_like(trace)
    else:
        own, other, tiles, sems = refs
    rows, width = own.shape
    depth = tiles.shape[2]
    steps = rows // TILE
    block, flip = scalars[3 * slot], scalars[3 * slot + 2]
    if with_trace:
        own[...] = jnp.zeros_like(own)
        other[...] = jnp.zeros_like(other)

    def fetch(step, buffer):
        return pltpu.make_async_copy(
            gram.at[
                pl.ds(pl.multiple_of(step * TILE, TILE), TILE),
                pl.ds(pl.multiple_of(block * depth, BLK), depth),
            ],
            tiles.at[buffer],
            sems.at[buffer],
        )

    @pl.when(scalars[3 * slot + 1] == 1)
    def _():
        fetch(0, 0).start()

        @pl.loop(0, steps)
        def _(step):
            buffer = lax.rem(step, 2)

            @pl.when(step + 1 < steps)
            def _():
                fetch(step + 1, 1 - buffer).start()

            fetch(step, buffer).wait()
            here = pl.ds(pl.multiple_of(step * TILE, TILE), TILE)
            panel = jnp.concatenate([first[:depth, :], second[:depth, :]], axis=1)
            low = jnp.concatenate([first[depth:, :], second[depth:, :]], axis=1)
            result = jnp.dot(tiles[buffer], panel, preferred_element_type=jnp.float32)
            result += jnp.dot(across[here, :], low, preferred_element_type=jnp.float32)
            left, right = result[:, :width], result[:, width:]
            own[here, :] += jnp.where(flip == 1, right, left)
            other[here, :] += jnp.where(flip == 1, left, right)
            if with_trace:
                square = tiles[buffer, :, here].astype(jnp.float32)
                lines = lax.broadcasted_iota(jnp.int32, (TILE, TILE), 0)
                same = lines == lax.broadcasted_iota(jnp.int32, (TILE, TILE), 1)
                diag = jnp.sum(jnp.where(same, square, 0.0), axis=0, keepdims=True)
                part = acts[:, here].astype(jnp.float32)
                diag += jnp.sum(part * part, axis=0, keepdims=True)
                diag = diag.astype(jnp.bfloat16).astype(jnp.float32)
                for start in range(0, TILE, BLK):
                    trace[0:1, :] += diag[:, start : start + BLK]


def product(slot, scalars, gram, message, across, acts, acc):
    rows = gram.shape[0]
    width = message[0].shape[1]
    whole = pl.BlockSpec(memory_space=pltpu.VMEM)
    panel = jax.ShapeDtypeStruct((rows, width), jnp.float32)
    with_trace = acc is None
    operands = [scalars, gram, *message, across, acts]
    in_specs = [pl.BlockSpec(memory_space=pltpu.SMEM), pl.BlockSpec(memory_space=pl.ANY)]
    in_specs += [whole] * 4
    kernel = product_kernel
    aliases = {}
    if with_trace:

        def kernel(slot, with_trace, scalars, gram, first, second, across, acts, *refs):
            product_kernel(
                slot, with_trace, scalars, gram, first, second, across, acts, None, None, *refs
            )

    else:
        aliases = {6: 0, 7: 1}
        operands += acc
        in_specs += [whole] * 2
    out_shape = [panel, panel]
    if with_trace:
        out_shape.append(jax.ShapeDtypeStruct((8, width), jnp.float32))
    return pl.pallas_call(
        functools.partial(kernel, slot, with_trace),
        in_specs=in_specs,
        out_specs=[whole] * len(out_shape),
        out_shape=out_shape,
        scratch_shapes=[
            pltpu.VMEM((2, TILE, rows), jnp.bfloat16),
            pltpu.SemaphoreType.DMA((2,)),
        ],
        input_output_aliases=aliases,
        compiler_params=pltpu.CompilerParams(vmem_limit_bytes=LIMIT),
        cost_estimate=pl.CostEstimate(
            flops=4 * rows * rows * width, bytes_accessed=2 * rows * rows, transcendentals=0
        ),
    )(*operands)


def ring_apply(ring, scalars, gram, message, across, acts):
    first = message
    second = swap(message, "col", 1)
    held = [(first, second)]
    for step in range(ring.last):
        first = lax.ppermute(first, AXES, ring.shift())
        second = lax.ppermute(second, AXES, ring.shift())
        held.append((first, second))
    close = (
        lax.ppermute(first, AXES, ring.close(1)),
        lax.ppermute(first, AXES, ring.close(-1)),
    )
    own, other, trace = product(0, scalars, gram, held[0], across, acts, None)
    acc = [own, other]
    for step in range(ring.last):
        acc = product(1 + 2 * step, scalars, gram, held[step + 1], across, acts, acc)
        pairs = ring.hand_over(step)
        if pairs:
            handed = tuple(lax.ppermute(part, AXES, pairs) for part in held[step + 1])
            acc = product(2 + 2 * step, scalars, gram, handed, across, acts, acc)
    own, other = product(1 + 2 * ring.last, scalars, gram, close, across, acts, acc)
    return own, swap(other, "col", 1), trace


def put_message(message, acts, rows):
    message[rows:, :] = jnp.dot(
        acts[...], message[:rows, :], preferred_element_type=jnp.float32
    ).astype(message.dtype)


def head_kernel(weights, blocks, acts, message):
    rows = weights.shape[0]
    for block in range(rows // BLK):
        here = slice(block * BLK, (block + 1) * BLK)
        dense = weights[here, :]
        message[here, :] = (blocks[block : block + 1, :] * dense - dense).astype(message.dtype)
    put_message(message, acts, rows)


def turn_kernel(own, received, blocks, acts, grad, message):
    rows = own.shape[0]
    for block in range(rows // BLK):
        here = slice(block * BLK, (block + 1) * BLK)
        grad_first = own[here, :] + received[here, :]
        grad[here, :] = grad_first
        message[here, :] = (blocks[block : block + 1, :] * grad_first).astype(message.dtype)
    put_message(message, acts, rows)


def lane_sums(value):
    return jnp.sum(value, axis=0, keepdims=True)


def curve_kernel(trace, grad, own, received, blocks, curve_ref, sums_ref):
    rows = grad.shape[0]
    sums_ref[...] = jnp.zeros_like(sums_ref)
    sums_ref[0:1, :] = trace[0:1, :]
    for block in range(rows // BLK):
        here = slice(block * BLK, (block + 1) * BLK)
        kept = blocks[block : block + 1, :]
        curve = own[here, :] + received[here, :]
        curve_ref[here, :] = curve
        step_dir = kept * grad[here, :]
        masked = kept * curve
        sums_ref[1:2, :] += lane_sums(step_dir * step_dir)
        sums_ref[2:3, :] += lane_sums(step_dir * curve)
        sums_ref[3:4, :] += lane_sums(masked * masked)


def last_kernel(units, sums, grad, curve, weights, blocks, out_ref):
    totals = jnp.sum(sums[...], axis=1, keepdims=True)
    trace_total, grad_square = totals[0:1, :], totals[1:2, :]
    grad_curve, curve_square = totals[2:3, :], totals[3:4, :]
    damping = damping_ratio * trace_total / units
    step_first = grad_square / (grad_curve + damping * grad_square + epsilon)
    step_second = (grad_curve + damping * grad_square) / (
        curve_square + 2.0 * damping * grad_curve + damping * damping * grad_square + epsilon
    )
    rows = grad.shape[0]
    for block in range(rows // BLK):
        here = slice(block * BLK, (block + 1) * BLK)
        kept = blocks[block : block + 1, :]
        grad_first = grad[here, :]
        step_dir = kept * grad_first
        grad_second = grad_first - step_first * curve[here, :]
        out_ref[here, :] = (
            kept * weights[here, :] - step_first * step_dir - step_second * (kept * grad_second)
        )


def gather_apply(gram, activations, panel, col_index):
    half = gram.shape[1]
    full = lax.all_gather(panel, "row", axis=0, tiled=True)
    own_half = lax.dynamic_slice_in_dim(full, col_index * half, half, 0)
    need = lax.dynamic_slice_in_dim(full, (1 - col_index) * half, half, 0)
    other_half = swap(need, "col", 1)
    own = jnp.dot(gram, own_half, preferred_element_type=jnp.float32)
    partial = jnp.dot(gram, other_half, preferred_element_type=jnp.float32)
    low = lax.psum(jnp.dot(activations, panel, preferred_element_type=jnp.float32), "row")
    update = lax.dot_general(
        activations.astype(jnp.float32),
        low,
        (((0,), (0,)), ((), ())),
        precision=lax.Precision.HIGHEST,
        preferred_element_type=jnp.float32,
    )
    return own + swap(partial, "col", 1) + update


def per_device_general(gram_old, activations, weights, block_mask):
    row_block, half_width = gram_old.shape
    width_cols = weights.shape[1]
    units = lax.axis_size("row") * row_block
    row_index = lax.axis_index("row")
    col_index = lax.axis_index("col")
    mask_local = expand_local(block_mask, row_index, row_block, col_index, width_cols)
    kept_weights = mask_local * weights
    diff_low = (kept_weights - weights).astype(jnp.bfloat16)
    acts = activations.astype(jnp.float32)
    column_squares = jnp.sum(acts * acts, axis=0)
    grad_first = gather_apply(gram_old, activations, diff_low, col_index)
    place = row_index * row_block + jnp.arange(row_block, dtype=jnp.int32)
    place = place - col_index * half_width
    on_diagonal = jnp.arange(half_width, dtype=jnp.int32)[None, :] == place[:, None]
    new_gram = gram_old.astype(jnp.float32) + column_squares[:, None]
    new_gram = new_gram.astype(jnp.bfloat16).astype(jnp.float32)
    trace_part = jnp.sum(jnp.where(on_diagonal, new_gram, 0.0))
    step_dir = mask_local * grad_first
    curvature = gather_apply(gram_old, activations, step_dir.astype(jnp.bfloat16), col_index)
    masked_curve = mask_local * curvature
    sums = jnp.stack(
        [
            trace_part,
            jnp.sum(step_dir * step_dir),
            jnp.sum(step_dir * curvature),
            jnp.sum(masked_curve * masked_curve),
        ]
    )
    sums = lax.psum(sums, ("row", "col"))
    trace_total, grad_square, grad_curve, curve_square = sums[0], sums[1], sums[2], sums[3]
    damping = damping_ratio * trace_total / units
    step_first = grad_square / (grad_curve + damping * grad_square + epsilon)
    step_second = (grad_curve + damping * grad_square) / (
        curve_square + 2.0 * damping * grad_curve + damping * damping * grad_square + epsilon
    )
    grad_second = grad_first - step_first * curvature
    return kept_weights - step_first * step_dir - step_second * (mask_local * grad_second)


def call_whole(kernel, out_shape, *operands):
    whole = pl.BlockSpec(memory_space=pltpu.VMEM)
    return pl.pallas_call(
        kernel,
        in_specs=[whole] * len(operands),
        out_specs=[whole] * len(out_shape),
        out_shape=out_shape,
        compiler_params=pltpu.CompilerParams(vmem_limit_bytes=LIMIT),
    )(*operands)


def per_device(gram_old, activations, weights, block_mask):
    row_block, _ = gram_old.shape
    width = weights.shape[1]
    samples = activations.shape[0]
    count = lax.axis_size("row")
    if row_block % TILE or count not in (4, 8, 16) or width != BLK or samples % 16:
        return per_device_general(gram_old, activations, weights, block_mask)
    ring = Ring(count)
    row_index = lax.axis_index("row")
    col_index = lax.axis_index("col")
    table = jnp.asarray(ring.table(), jnp.int32)
    scalars = lax.dynamic_index_in_dim(table, row_index * 2 + col_index, 0, keepdims=False)
    per_block = row_block // BLK
    own_mask = lax.dynamic_slice(block_mask, (row_index * per_block, col_index), (per_block, 1))
    blocks = jnp.broadcast_to(own_mask.astype(jnp.float32), (per_block, width))
    across = activations.T
    panel = jax.ShapeDtypeStruct((row_block, width), jnp.float32)
    letter = jax.ShapeDtypeStruct((row_block + samples, width), jnp.bfloat16)
    eight = jax.ShapeDtypeStruct((8, width), jnp.float32)

    (message,) = call_whole(head_kernel, [letter], weights, blocks, activations)
    own, received, trace = ring_apply(ring, scalars, gram_old, message, across, activations)
    grad, message = call_whole(turn_kernel, [panel, letter], own, received, blocks, activations)
    own, received, _ = ring_apply(ring, scalars, gram_old, message, across, activations)
    curve, sums = call_whole(curve_kernel, [panel, eight], trace, grad, own, received, blocks)
    sums = sum_rows(sums + swap(sums, "col", 1), count)
    last = functools.partial(last_kernel, float(count * row_block))
    return call_whole(last, [panel], sums, grad, curve, weights, blocks)[0]


def solution(mesh):
    placed = (
        P(("groups", "row"), "col"),
        P("groups", "row"),
        P("row", ("groups", "col")),
        P(None, "groups"),
    )
    return jax.shard_map(
        per_device,
        mesh=mesh,
        in_specs=placed,
        out_specs=P("row", ("groups", "col")),
        check_vma=False,
    )
```

```python
import functools

import jax
import jax.numpy as jnp
from jax import lax
from jax.experimental import pallas as pl
from jax.experimental.pallas import tpu as pltpu
from jax.sharding import PartitionSpec as P

BLK = 128
TILE = 256
LIMIT = 8 * 1024 * 1024
AXES = ("row", "col")

damping_ratio = 0.3
epsilon = 1e-06


def swap(value, axis, distance):
    return lax.ppermute(value, axis, [(i, i ^ distance) for i in range(lax.axis_size(axis))])


def sum_rows(value, count):
    distance = 1
    while distance < count:
        value = value + swap(value, "row", distance)
        distance *= 2
    return value


def expand_local(block_mask, row_index, row_block, col_index, width_cols):
    if width_cols != BLK:
        row_ids = (row_index * row_block + jnp.arange(row_block, dtype=jnp.int32)) // BLK
        col_ids = (col_index * width_cols + jnp.arange(width_cols, dtype=jnp.int32)) // BLK
        return block_mask[row_ids][:, col_ids].astype(jnp.float32)
    piece = BLK
    while row_block % piece:
        piece //= 2
    column = lax.dynamic_index_in_dim(block_mask, col_index, 1, keepdims=False)
    column = jnp.repeat(column, BLK // piece) if piece != BLK else column
    count = row_block // piece
    own = lax.dynamic_slice_in_dim(column, row_index * count, count, 0).astype(jnp.float32)
    return jnp.broadcast_to(own[:, None, None], (count, piece, width_cols)).reshape(
        row_block, width_cols
    )


class Ring:
    def __init__(self, count):
        self.count = count
        self.order = list(range(0, count, 2)) + list(range(count - 1, 0, -2))
        self.last = count // 2 - 1

    def row(self, place):
        return self.order[place % self.count]

    def half(self, place):
        return self.row(place) * 2 // self.count

    def ahead(self, place):
        return int(place % self.count >= self.count // 2)

    def device(self, place, core):
        return self.row(place) * 2 + core

    def source(self, place, core, step):
        return place - 1 - step if core == self.ahead(place) else place + 1 + step

    def first_column(self, place, core, step):
        origin = self.ahead(self.source(place, core, step))
        return origin if core == self.ahead(place) else 1 - origin

    def places(self):
        return [(place, core) for place in range(self.count) for core in range(2)]

    def shift(self):
        pairs = []
        for place in range(self.count):
            pairs.append(
                (self.device(place, self.ahead(place)), self.device(place + 1, self.ahead(place + 1)))
            )
            pairs.append(
                (
                    self.device(place, 1 - self.ahead(place)),
                    self.device(place - 1, 1 - self.ahead(place - 1)),
                )
            )
        return pairs

    def hand_over(self, step):
        return [
            (self.device(place, core), self.device(place, 1 - core))
            for place, core in self.places()
            if self.half(self.source(place, core, step)) != core
        ]

    def close(self, sign):
        pairs = []
        for place in range(self.count):
            core = self.ahead(place - sign)
            core = core if sign > 0 else 1 - core
            target = self.half(place + self.count // 2)
            pairs.append((self.device(place - sign, core), self.device(place, target)))
        return pairs

    def entry(self, place, core, carrier, step):
        source = self.source(place, carrier, step)
        return [
            self.row(source) % (self.count // 2),
            int(self.half(source) == core),
            int(self.first_column(place, carrier, step) != core),
        ]

    def table(self):
        half = self.count // 2
        lines = [None] * (2 * self.count)
        for place, core in self.places():
            line = [self.row(place) % half, int(self.half(place) == core), 0]
            for step in range(self.last):
                if step and self.hand_over(step - 1):
                    line += self.entry(place, core, 1 - core, step - 1)
                line += self.entry(place, core, core, step)
            if self.hand_over(self.last - 1):
                line += self.entry(place, core, 1 - core, self.last - 1)
            else:
                line += [0, 0, 0]
            far = place + half
            line += [
                self.row(far) % half,
                int(self.half(far) == core),
                int(self.ahead(far) != core),
            ]
            lines[self.device(place, core)] = line
        return lines


def product_kernel(slot, scalars, gram, first, second, across, own_in, other_in, own, other):
    rows, width = own.shape
    start = pl.multiple_of(scalars[3 * slot] * rows, BLK)
    flip = scalars[3 * slot + 2]
    if slot == 0:
        own[...] = jnp.zeros_like(own)
        other[...] = jnp.zeros_like(other)

    @pl.when(scalars[3 * slot + 1] == 1)
    def _():
        @pl.loop(0, rows // TILE)
        def _(tile):
            here = pl.ds(pl.multiple_of(tile * TILE, TILE), TILE)
            lines = jnp.concatenate([gram[here, pl.ds(start, rows)], across[here, :]], axis=1)
            panel = jnp.concatenate([first[...], second[...]], axis=1)
            result = jnp.dot(lines, panel, preferred_element_type=jnp.float32)
            left, right = result[:, :width], result[:, width:]
            own[here, :] += jnp.where(flip == 1, right, left)
            other[here, :] += jnp.where(flip == 1, left, right)


def first_product_kernel(scalars, gram, first, second, across, own, other):
    product_kernel(0, scalars, gram, first, second, across, None, None, own, other)


def product(slot, scalars, gram, message, across, acc):
    rows = gram.shape[0]
    width = message[0].shape[1]
    whole = pl.BlockSpec(memory_space=pltpu.VMEM)
    operands = [scalars, gram, *message, across, *acc]
    return pl.pallas_call(
        functools.partial(product_kernel, slot) if slot else first_product_kernel,
        in_specs=[pl.BlockSpec(memory_space=pltpu.SMEM)] + [whole] * (len(operands) - 1),
        out_specs=[whole] * 2,
        out_shape=[jax.ShapeDtypeStruct((rows, width), jnp.float32)] * 2,
        input_output_aliases={5: 0, 6: 1} if acc else {},
        compiler_params=pltpu.CompilerParams(vmem_limit_bytes=LIMIT),
        cost_estimate=pl.CostEstimate(
            flops=4 * rows * rows * width, bytes_accessed=2 * rows * rows, transcendentals=0
        ),
    )(*operands)


def after(value, others):
    return lax.optimization_barrier((value, *others))[0]


def ring_apply(ring, scalars, gram, message, across):
    first = message
    second = swap(message, "col", 1)
    slot = 0
    held = (first, second)
    acc = []
    waiting = []
    for step in range(ring.last):
        first = lax.ppermute(after(first, acc), AXES, ring.shift())
        acc = product(slot, scalars, gram, held, across, acc)
        slot += 1
        second = lax.ppermute(after(second, acc), AXES, ring.shift())
        if waiting:
            acc = product(slot, scalars, gram, waiting, across, acc)
            slot += 1
        held = (first, second)
        waiting = []
        if ring.hand_over(step):
            waiting = [swap(first, "col", 1), swap(second, "col", 1)]
    first = after(first, acc)
    close = (
        lax.ppermute(first, AXES, ring.close(1)),
        lax.ppermute(first, AXES, ring.close(-1)),
    )
    acc = product(slot, scalars, gram, held, across, acc)
    if waiting:
        acc = product(slot + 1, scalars, gram, waiting, across, acc)
    own, other = product(slot + 2, scalars, gram, close, across, acc)
    return own, swap(other, "col", 1)


def trace_kernel(scalars, gram, acts, trace, tile, sem):
    rows = acts.shape[1]
    trace[...] = jnp.zeros_like(trace)

    @pl.when(scalars[1] == 1)
    def _():
        start = scalars[0] * rows
        lines = lax.broadcasted_iota(jnp.int32, (BLK, BLK), 0)
        same = lines == lax.broadcasted_iota(jnp.int32, (BLK, BLK), 1)
        copies = [
            pltpu.make_async_copy(
                gram.at[
                    block * BLK : (block + 1) * BLK,
                    pl.ds(pl.multiple_of(start + block * BLK, BLK), BLK),
                ],
                tile.at[block],
                sem.at[block],
            )
            for block in range(rows // BLK)
        ]
        for copy in copies:
            copy.start()
        for block, copy in enumerate(copies):
            copy.wait()
            square = tile[block].astype(jnp.float32)
            diag = jnp.sum(jnp.where(same, square, 0.0), axis=0, keepdims=True)
            part = acts[:, block * BLK : (block + 1) * BLK].astype(jnp.float32)
            diag += jnp.sum(part * part, axis=0, keepdims=True)
            trace[0:1, :] += diag.astype(jnp.bfloat16).astype(jnp.float32)


def trace_part(scalars, gram, acts):
    whole = pl.BlockSpec(memory_space=pltpu.VMEM)
    blocks = acts.shape[1] // BLK
    return pl.pallas_call(
        trace_kernel,
        in_specs=[
            pl.BlockSpec(memory_space=pltpu.SMEM),
            pl.BlockSpec(memory_space=pl.ANY),
            whole,
        ],
        out_specs=whole,
        out_shape=jax.ShapeDtypeStruct((8, BLK), jnp.float32),
        scratch_shapes=[
            pltpu.VMEM((blocks, BLK, BLK), jnp.bfloat16),
            pltpu.SemaphoreType.DMA((blocks,)),
        ],
        compiler_params=pltpu.CompilerParams(vmem_limit_bytes=LIMIT),
    )(scalars, gram, acts)


def put_message(message, acts, rows):
    message[rows:, :] = jnp.dot(
        acts[...], message[:rows, :], preferred_element_type=jnp.float32
    ).astype(message.dtype)


def head_kernel(weights, blocks, acts, message):
    rows = weights.shape[0]
    for block in range(rows // BLK):
        here = slice(block * BLK, (block + 1) * BLK)
        dense = weights[here, :]
        message[here, :] = (blocks[block : block + 1, :] * dense - dense).astype(message.dtype)
    put_message(message, acts, rows)


def turn_kernel(own, received, blocks, acts, grad, message):
    rows = own.shape[0]
    for block in range(rows // BLK):
        here = slice(block * BLK, (block + 1) * BLK)
        grad_first = own[here, :] + received[here, :]
        grad[here, :] = grad_first
        message[here, :] = (blocks[block : block + 1, :] * grad_first).astype(message.dtype)
    put_message(message, acts, rows)


def lane_sums(value):
    return jnp.sum(value, axis=0, keepdims=True)


def curve_kernel(trace, grad, own, received, blocks, curve_ref, sums_ref):
    rows = grad.shape[0]
    sums_ref[...] = jnp.zeros_like(sums_ref)
    sums_ref[0:1, :] = trace[0:1, :]
    for block in range(rows // BLK):
        here = slice(block * BLK, (block + 1) * BLK)
        kept = blocks[block : block + 1, :]
        curve = own[here, :] + received[here, :]
        curve_ref[here, :] = curve
        step_dir = kept * grad[here, :]
        masked = kept * curve
        sums_ref[1:2, :] += lane_sums(step_dir * step_dir)
        sums_ref[2:3, :] += lane_sums(step_dir * curve)
        sums_ref[3:4, :] += lane_sums(masked * masked)


def last_kernel(units, sums, grad, curve, weights, blocks, out_ref):
    totals = jnp.sum(sums[...], axis=1, keepdims=True)
    trace_total, grad_square = totals[0:1, :], totals[1:2, :]
    grad_curve, curve_square = totals[2:3, :], totals[3:4, :]
    damping = damping_ratio * trace_total / units
    step_first = grad_square / (grad_curve + damping * grad_square + epsilon)
    step_second = (grad_curve + damping * grad_square) / (
        curve_square + 2.0 * damping * grad_curve + damping * damping * grad_square + epsilon
    )
    rows = grad.shape[0]
    for block in range(rows // BLK):
        here = slice(block * BLK, (block + 1) * BLK)
        kept = blocks[block : block + 1, :]
        grad_first = grad[here, :]
        step_dir = kept * grad_first
        grad_second = grad_first - step_first * curve[here, :]
        out_ref[here, :] = (
            kept * weights[here, :] - step_first * step_dir - step_second * (kept * grad_second)
        )


def gather_apply(gram, activations, panel, col_index):
    half = gram.shape[1]
    full = lax.all_gather(panel, "row", axis=0, tiled=True)
    own_half = lax.dynamic_slice_in_dim(full, col_index * half, half, 0)
    need = lax.dynamic_slice_in_dim(full, (1 - col_index) * half, half, 0)
    other_half = swap(need, "col", 1)
    own = jnp.dot(gram, own_half, preferred_element_type=jnp.float32)
    partial = jnp.dot(gram, other_half, preferred_element_type=jnp.float32)
    low = lax.psum(jnp.dot(activations, panel, preferred_element_type=jnp.float32), "row")
    update = lax.dot_general(
        activations.astype(jnp.float32),
        low,
        (((0,), (0,)), ((), ())),
        precision=lax.Precision.HIGHEST,
        preferred_element_type=jnp.float32,
    )
    return own + swap(partial, "col", 1) + update


def per_device_general(gram_old, activations, weights, block_mask):
    row_block, half_width = gram_old.shape
    width_cols = weights.shape[1]
    units = lax.axis_size("row") * row_block
    row_index = lax.axis_index("row")
    col_index = lax.axis_index("col")
    mask_local = expand_local(block_mask, row_index, row_block, col_index, width_cols)
    kept_weights = mask_local * weights
    diff_low = (kept_weights - weights).astype(jnp.bfloat16)
    acts = activations.astype(jnp.float32)
    column_squares = jnp.sum(acts * acts, axis=0)
    grad_first = gather_apply(gram_old, activations, diff_low, col_index)
    place = row_index * row_block + jnp.arange(row_block, dtype=jnp.int32)
    place = place - col_index * half_width
    on_diagonal = jnp.arange(half_width, dtype=jnp.int32)[None, :] == place[:, None]
    new_gram = gram_old.astype(jnp.float32) + column_squares[:, None]
    new_gram = new_gram.astype(jnp.bfloat16).astype(jnp.float32)
    trace_part = jnp.sum(jnp.where(on_diagonal, new_gram, 0.0))
    step_dir = mask_local * grad_first
    curvature = gather_apply(gram_old, activations, step_dir.astype(jnp.bfloat16), col_index)
    masked_curve = mask_local * curvature
    sums = jnp.stack(
        [
            trace_part,
            jnp.sum(step_dir * step_dir),
            jnp.sum(step_dir * curvature),
            jnp.sum(masked_curve * masked_curve),
        ]
    )
    sums = lax.psum(sums, ("row", "col"))
    trace_total, grad_square, grad_curve, curve_square = sums[0], sums[1], sums[2], sums[3]
    damping = damping_ratio * trace_total / units
    step_first = grad_square / (grad_curve + damping * grad_square + epsilon)
    step_second = (grad_curve + damping * grad_square) / (
        curve_square + 2.0 * damping * grad_curve + damping * damping * grad_square + epsilon
    )
    grad_second = grad_first - step_first * curvature
    return kept_weights - step_first * step_dir - step_second * (mask_local * grad_second)


def call_whole(kernel, out_shape, *operands):
    whole = pl.BlockSpec(memory_space=pltpu.VMEM)
    return pl.pallas_call(
        kernel,
        in_specs=[whole] * len(operands),
        out_specs=[whole] * len(out_shape),
        out_shape=out_shape,
        compiler_params=pltpu.CompilerParams(vmem_limit_bytes=LIMIT),
    )(*operands)


def per_device(gram_old, activations, weights, block_mask):
    row_block, _ = gram_old.shape
    width = weights.shape[1]
    samples = activations.shape[0]
    count = lax.axis_size("row")
    if row_block % TILE or count not in (4, 8, 16) or width != BLK or samples % 16:
        return per_device_general(gram_old, activations, weights, block_mask)
    ring = Ring(count)
    row_index = lax.axis_index("row")
    col_index = lax.axis_index("col")
    table = jnp.asarray(ring.table(), jnp.int32)
    scalars = lax.dynamic_index_in_dim(table, row_index * 2 + col_index, 0, keepdims=False)
    per_block = row_block // BLK
    own_mask = lax.dynamic_slice(block_mask, (row_index * per_block, col_index), (per_block, 1))
    blocks = jnp.broadcast_to(own_mask.astype(jnp.float32), (per_block, width))
    across = activations.T
    panel = jax.ShapeDtypeStruct((row_block, width), jnp.float32)
    letter = jax.ShapeDtypeStruct((row_block + samples, width), jnp.bfloat16)
    eight = jax.ShapeDtypeStruct((8, width), jnp.float32)

    (message,) = call_whole(head_kernel, [letter], weights, blocks, activations)
    own, received = ring_apply(ring, scalars, gram_old, message, across)
    trace = trace_part(scalars, gram_old, activations)
    grad, message = call_whole(turn_kernel, [panel, letter], own, received, blocks, activations)
    own, received = ring_apply(ring, scalars, gram_old, message, across)
    curve, sums = call_whole(curve_kernel, [panel, eight], trace, grad, own, received, blocks)
    sums = sum_rows(sums + swap(sums, "col", 1), count)
    last = functools.partial(last_kernel, float(count * row_block))
    return call_whole(last, [panel], sums, grad, curve, weights, blocks)[0]


def solution(mesh):
    placed = (
        P(("groups", "row"), "col"),
        P("groups", "row"),
        P("row", ("groups", "col")),
        P(None, "groups"),
    )
    return jax.shard_map(
        per_device,
        mesh=mesh,
        in_specs=placed,
        out_specs=P("row", ("groups", "col")),
        check_vma=False,
    )
```

```python
import functools

import jax
import jax.numpy as jnp
from jax import lax
from jax.experimental import pallas as pl
from jax.experimental.pallas import tpu as pltpu
from jax.sharding import PartitionSpec as P

BLK = 128
TILE = 896
PART = 448
LIMIT = 8 * 1024 * 1024
AXES = ("row", "col")

damping_ratio = 0.3
epsilon = 1e-06


def swap(value, axis, distance):
    return lax.ppermute(value, axis, [(i, i ^ distance) for i in range(lax.axis_size(axis))])


def sum_rows(value, count):
    distance = 1
    while distance < count:
        value = value + swap(value, "row", distance)
        distance *= 2
    return value


def expand_local(block_mask, row_index, row_block, col_index, width_cols):
    if width_cols != BLK:
        row_ids = (row_index * row_block + jnp.arange(row_block, dtype=jnp.int32)) // BLK
        col_ids = (col_index * width_cols + jnp.arange(width_cols, dtype=jnp.int32)) // BLK
        return block_mask[row_ids][:, col_ids].astype(jnp.float32)
    piece = BLK
    while row_block % piece:
        piece //= 2
    column = lax.dynamic_index_in_dim(block_mask, col_index, 1, keepdims=False)
    column = jnp.repeat(column, BLK // piece) if piece != BLK else column
    count = row_block // piece
    own = lax.dynamic_slice_in_dim(column, row_index * count, count, 0).astype(jnp.float32)
    return jnp.broadcast_to(own[:, None, None], (count, piece, width_cols)).reshape(
        row_block, width_cols
    )


class Ring:
    def __init__(self, count):
        self.count = count
        self.order = list(range(0, count, 2)) + list(range(count - 1, 0, -2))
        self.last = count // 2 - 1

    def row(self, place):
        return self.order[place % self.count]

    def half(self, place):
        return self.row(place) * 2 // self.count

    def ahead(self, place):
        return int(place % self.count >= self.count // 2)

    def device(self, place, core):
        return self.row(place) * 2 + core

    def source(self, place, core, step):
        return place - 1 - step if core == self.ahead(place) else place + 1 + step

    def first_column(self, place, core, step):
        origin = self.ahead(self.source(place, core, step))
        return origin if core == self.ahead(place) else 1 - origin

    def places(self):
        return [(place, core) for place in range(self.count) for core in range(2)]

    def shift(self):
        pairs = []
        for place in range(self.count):
            pairs.append(
                (self.device(place, self.ahead(place)), self.device(place + 1, self.ahead(place + 1)))
            )
            pairs.append(
                (
                    self.device(place, 1 - self.ahead(place)),
                    self.device(place - 1, 1 - self.ahead(place - 1)),
                )
            )
        return pairs

    def hand_over(self, step):
        return [
            (self.device(place, core), self.device(place, 1 - core))
            for place, core in self.places()
            if self.half(self.source(place, core, step)) != core
        ]

    def slots(self):
        found = []
        for step in range(self.last):
            found.append((True, step))
            if self.hand_over(step):
                found.append((False, step))
        return found + [(True, self.last)]

    def loads(self, slot):
        base = 3 * (1 + len(self.slots()))
        if slot == 0:
            return [base, base + 1]
        return [base + slot + 1] if slot + 1 < self.count // 2 else []

    def entry(self, place, core, carrier, step):
        source = self.source(place, carrier, step)
        return [
            self.row(source) % (self.count // 2),
            int(self.half(source) == core),
            int(self.first_column(place, carrier, step) != core),
        ]

    def table(self):
        half = self.count // 2
        lines = [None] * (2 * self.count)
        for place, core in self.places():
            line = [self.row(place) % half, int(self.half(place) == core), 0]
            for carrier, step in self.slots():
                line += self.entry(place, core, core if carrier else 1 - core, step)
            needed = [line[k] for k in range(0, len(line), 3) if line[k + 1]]
            line += needed
            lines[self.device(place, core)] = line
        return lines


def product_kernel(slot, loads, scalars, gram, first, second, across, *refs):
    if loads is None:
        store = gram
        own, other = refs[-2:]
    else:
        own, other, store, sems = refs[-4:]
    rows, width = own.shape
    start = pl.multiple_of(scalars[3 * slot] * rows, BLK)
    active = scalars[3 * slot + 1] == 1
    flip = scalars[3 * slot + 2] == 1
    parts = rows // PART

    def fetch(load, part):
        block = pl.multiple_of(scalars[load] * rows, BLK)
        here = pl.ds(part * PART, PART)
        there = pl.ds(block, rows)
        return pltpu.make_async_copy(
            gram.at[here, there], store.at[here, there], sems.at[loads.index(load), part]
        )

    for load in loads or []:
        for part in range(parts):
            fetch(load, part).start()
    if slot == 0:
        own[...] = jnp.zeros_like(own)
        other[...] = jnp.zeros_like(other)
    at_once = slot == 0 and loads is not None

    @pl.when(active)
    def _():
        @pl.loop(0, rows // TILE)
        def _(tile):
            if at_once:
                for part in range(TILE // PART):
                    fetch(loads[0], tile * (TILE // PART) + part).wait()
            here = pl.ds(pl.multiple_of(tile * TILE, TILE), TILE)
            lines = jnp.concatenate([store[here, pl.ds(start, rows)], across[here, :]], axis=1)
            panel = jnp.concatenate([first[...], second[...]], axis=1)
            result = jnp.dot(lines, panel, preferred_element_type=jnp.float32)
            left, right = result[:, :width], result[:, width:]
            own[here, :] += jnp.where(flip, right, left)
            other[here, :] += jnp.where(flip, left, right)

    if at_once:

        @pl.when(jnp.logical_not(active))
        def _():
            for part in range(parts):
                fetch(loads[0], part).wait()

    for load in (loads or [])[int(at_once) :]:
        for part in range(parts):
            fetch(load, part).wait()


def product(slot, loads, scalars, gram, message, across, carried):
    rows = across.shape[0]
    width = message[0].shape[1]
    whole = pl.BlockSpec(memory_space=pltpu.VMEM)
    loading = loads is not None
    operands = [scalars, gram, *message, across, *carried]
    in_specs = [pl.BlockSpec(memory_space=pltpu.SMEM)] + [whole] * (len(operands) - 1)
    out_shape = [jax.ShapeDtypeStruct((rows, width), jnp.float32)] * 2
    scratch = []
    if loading:
        in_specs[1] = pl.BlockSpec(memory_space=pl.ANY)
        out_shape.append(jax.ShapeDtypeStruct(gram.shape, gram.dtype))
        scratch = [pltpu.SemaphoreType.DMA((max(len(loads), 1), rows // PART))]
    return pl.pallas_call(
        functools.partial(product_kernel, slot, loads),
        in_specs=in_specs,
        out_specs=[whole] * len(out_shape),
        out_shape=out_shape,
        scratch_shapes=scratch,
        input_output_aliases={5 + k: k for k in range(len(carried))},
        compiler_params=pltpu.CompilerParams(vmem_limit_bytes=LIMIT),
        cost_estimate=pl.CostEstimate(
            flops=4 * rows * rows * width, bytes_accessed=2 * rows * rows, transcendentals=0
        ),
    )(*operands)


def after(value, others):
    return lax.optimization_barrier((value, *others))[0]


def ring_apply(ring, scalars, gram, message, across, loading):
    first, second = message, swap(message, "col", 1)
    ready = [(first, second)]
    carried = []
    slot = 0

    def work(others=()):
        nonlocal carried, slot
        if not ready:
            return
        parts = ready.pop(0)
        parts = (after(parts[0], others), parts[1])
        loads = ring.loads(slot) if loading else None
        carried = product(slot, loads, scalars, gram, parts, across, carried)
        slot += 1

    def hand_over(step):
        if ring.hand_over(step):
            ready.append(tuple(swap(after(part, carried[:1]), "col", 1) for part in held))

    for step in range(ring.last):
        came = lax.ppermute(after(first, carried[:1]), AXES, ring.shift())
        if step:
            work([first])
        second = lax.ppermute(after(second, carried[:1]), AXES, ring.shift())
        if step:
            hand_over(step - 1)
            work()
        first = came
        held = (first, second)
        ready.append(held)
    first = lax.ppermute(after(first, carried[:1]), AXES, ring.shift())
    hand_over(ring.last - 1)
    work()
    last = (first, swap(after(first, carried[:1]), "col", 1))
    while ready:
        work()
    ready.append(last)
    work()
    return carried[0], swap(carried[1], "col", 1), carried[2:]


def trace_kernel(scalars, gram, acts, trace, tile, sem):
    rows = acts.shape[1]
    trace[...] = jnp.zeros_like(trace)

    @pl.when(scalars[1] == 1)
    def _():
        start = scalars[0] * rows
        lines = lax.broadcasted_iota(jnp.int32, (BLK, BLK), 0)
        same = lines == lax.broadcasted_iota(jnp.int32, (BLK, BLK), 1)
        copies = [
            pltpu.make_async_copy(
                gram.at[
                    block * BLK : (block + 1) * BLK,
                    pl.ds(pl.multiple_of(start + block * BLK, BLK), BLK),
                ],
                tile.at[block],
                sem.at[block],
            )
            for block in range(rows // BLK)
        ]
        for copy in copies:
            copy.start()
        for block, copy in enumerate(copies):
            copy.wait()
            square = tile[block].astype(jnp.float32)
            diag = jnp.sum(jnp.where(same, square, 0.0), axis=0, keepdims=True)
            part = acts[:, block * BLK : (block + 1) * BLK].astype(jnp.float32)
            diag += jnp.sum(part * part, axis=0, keepdims=True)
            trace[0:1, :] += diag.astype(jnp.bfloat16).astype(jnp.float32)


def trace_part(scalars, gram, acts):
    whole = pl.BlockSpec(memory_space=pltpu.VMEM)
    blocks = acts.shape[1] // BLK
    return pl.pallas_call(
        trace_kernel,
        in_specs=[
            pl.BlockSpec(memory_space=pltpu.SMEM),
            pl.BlockSpec(memory_space=pl.ANY),
            whole,
        ],
        out_specs=whole,
        out_shape=jax.ShapeDtypeStruct((8, BLK), jnp.float32),
        scratch_shapes=[
            pltpu.VMEM((blocks, BLK, BLK), jnp.bfloat16),
            pltpu.SemaphoreType.DMA((blocks,)),
        ],
        compiler_params=pltpu.CompilerParams(vmem_limit_bytes=LIMIT),
    )(scalars, gram, acts)


def put_message(message, acts, rows):
    message[rows:, :] = jnp.dot(
        acts[...], message[:rows, :], preferred_element_type=jnp.float32
    ).astype(message.dtype)


def head_kernel(weights, blocks, acts, message):
    rows = weights.shape[0]
    for block in range(rows // BLK):
        here = slice(block * BLK, (block + 1) * BLK)
        dense = weights[here, :]
        message[here, :] = (blocks[block : block + 1, :] * dense - dense).astype(message.dtype)
    put_message(message, acts, rows)


def turn_kernel(own, received, blocks, acts, grad, message):
    rows = own.shape[0]
    for block in range(rows // BLK):
        here = slice(block * BLK, (block + 1) * BLK)
        grad_first = own[here, :] + received[here, :]
        grad[here, :] = grad_first
        message[here, :] = (blocks[block : block + 1, :] * grad_first).astype(message.dtype)
    put_message(message, acts, rows)


def lane_sums(value):
    return jnp.sum(value, axis=0, keepdims=True)


def curve_kernel(trace, grad, own, received, blocks, curve_ref, sums_ref):
    rows = grad.shape[0]
    sums_ref[...] = jnp.zeros_like(sums_ref)
    sums_ref[0:1, :] = trace[0:1, :]
    for block in range(rows // BLK):
        here = slice(block * BLK, (block + 1) * BLK)
        kept = blocks[block : block + 1, :]
        curve = own[here, :] + received[here, :]
        curve_ref[here, :] = curve
        step_dir = kept * grad[here, :]
        masked = kept * curve
        sums_ref[1:2, :] += lane_sums(step_dir * step_dir)
        sums_ref[2:3, :] += lane_sums(step_dir * curve)
        sums_ref[3:4, :] += lane_sums(masked * masked)


def last_kernel(units, sums, grad, curve, weights, blocks, out_ref):
    totals = jnp.sum(sums[...], axis=1, keepdims=True)
    trace_total, grad_square = totals[0:1, :], totals[1:2, :]
    grad_curve, curve_square = totals[2:3, :], totals[3:4, :]
    damping = damping_ratio * trace_total / units
    step_first = grad_square / (grad_curve + damping * grad_square + epsilon)
    step_second = (grad_curve + damping * grad_square) / (
        curve_square + 2.0 * damping * grad_curve + damping * damping * grad_square + epsilon
    )
    rows = grad.shape[0]
    for block in range(rows // BLK):
        here = slice(block * BLK, (block + 1) * BLK)
        kept = blocks[block : block + 1, :]
        grad_first = grad[here, :]
        step_dir = kept * grad_first
        grad_second = grad_first - step_first * curve[here, :]
        out_ref[here, :] = (
            kept * weights[here, :] - step_first * step_dir - step_second * (kept * grad_second)
        )


def gather_apply(gram, activations, panel, col_index):
    half = gram.shape[1]
    full = lax.all_gather(panel, "row", axis=0, tiled=True)
    own_half = lax.dynamic_slice_in_dim(full, col_index * half, half, 0)
    need = lax.dynamic_slice_in_dim(full, (1 - col_index) * half, half, 0)
    other_half = swap(need, "col", 1)
    own = jnp.dot(gram, own_half, preferred_element_type=jnp.float32)
    partial = jnp.dot(gram, other_half, preferred_element_type=jnp.float32)
    low = lax.psum(jnp.dot(activations, panel, preferred_element_type=jnp.float32), "row")
    update = lax.dot_general(
        activations.astype(jnp.float32),
        low,
        (((0,), (0,)), ((), ())),
        precision=lax.Precision.HIGHEST,
        preferred_element_type=jnp.float32,
    )
    return own + swap(partial, "col", 1) + update


def per_device_general(gram_old, activations, weights, block_mask):
    row_block, half_width = gram_old.shape
    width_cols = weights.shape[1]
    units = lax.axis_size("row") * row_block
    row_index = lax.axis_index("row")
    col_index = lax.axis_index("col")
    mask_local = expand_local(block_mask, row_index, row_block, col_index, width_cols)
    kept_weights = mask_local * weights
    diff_low = (kept_weights - weights).astype(jnp.bfloat16)
    acts = activations.astype(jnp.float32)
    column_squares = jnp.sum(acts * acts, axis=0)
    grad_first = gather_apply(gram_old, activations, diff_low, col_index)
    place = row_index * row_block + jnp.arange(row_block, dtype=jnp.int32)
    place = place - col_index * half_width
    on_diagonal = jnp.arange(half_width, dtype=jnp.int32)[None, :] == place[:, None]
    new_gram = gram_old.astype(jnp.float32) + column_squares[:, None]
    new_gram = new_gram.astype(jnp.bfloat16).astype(jnp.float32)
    trace_part = jnp.sum(jnp.where(on_diagonal, new_gram, 0.0))
    step_dir = mask_local * grad_first
    curvature = gather_apply(gram_old, activations, step_dir.astype(jnp.bfloat16), col_index)
    masked_curve = mask_local * curvature
    sums = jnp.stack(
        [
            trace_part,
            jnp.sum(step_dir * step_dir),
            jnp.sum(step_dir * curvature),
            jnp.sum(masked_curve * masked_curve),
        ]
    )
    sums = lax.psum(sums, ("row", "col"))
    trace_total, grad_square, grad_curve, curve_square = sums[0], sums[1], sums[2], sums[3]
    damping = damping_ratio * trace_total / units
    step_first = grad_square / (grad_curve + damping * grad_square + epsilon)
    step_second = (grad_curve + damping * grad_square) / (
        curve_square + 2.0 * damping * grad_curve + damping * damping * grad_square + epsilon
    )
    grad_second = grad_first - step_first * curvature
    return kept_weights - step_first * step_dir - step_second * (mask_local * grad_second)


def call_whole(kernel, out_shape, *operands):
    whole = pl.BlockSpec(memory_space=pltpu.VMEM)
    return pl.pallas_call(
        kernel,
        in_specs=[whole] * len(operands),
        out_specs=[whole] * len(out_shape),
        out_shape=out_shape,
        compiler_params=pltpu.CompilerParams(vmem_limit_bytes=LIMIT),
    )(*operands)


def per_device(gram_old, activations, weights, block_mask):
    row_block, _ = gram_old.shape
    width = weights.shape[1]
    samples = activations.shape[0]
    count = lax.axis_size("row")
    if row_block % TILE or count not in (4, 8, 16) or width != BLK or samples % 16:
        return per_device_general(gram_old, activations, weights, block_mask)
    ring = Ring(count)
    row_index = lax.axis_index("row")
    col_index = lax.axis_index("col")
    table = jnp.asarray(ring.table(), jnp.int32)
    scalars = lax.dynamic_index_in_dim(table, row_index * 2 + col_index, 0, keepdims=False)
    per_block = row_block // BLK
    own_mask = lax.dynamic_slice(block_mask, (row_index * per_block, col_index), (per_block, 1))
    blocks = jnp.broadcast_to(own_mask.astype(jnp.float32), (per_block, width))
    across = activations.T
    panel = jax.ShapeDtypeStruct((row_block, width), jnp.float32)
    letter = jax.ShapeDtypeStruct((row_block + samples, width), jnp.bfloat16)
    eight = jax.ShapeDtypeStruct((8, width), jnp.float32)

    (message,) = call_whole(head_kernel, [letter], weights, blocks, activations)
    own, received, held = ring_apply(ring, scalars, gram_old, message, across, True)
    trace = trace_part(scalars, gram_old, activations)
    grad, message = call_whole(turn_kernel, [panel, letter], own, received, blocks, activations)
    own, received, _ = ring_apply(ring, scalars, held[0], message, across, False)
    curve, sums = call_whole(curve_kernel, [panel, eight], trace, grad, own, received, blocks)
    sums = sum_rows(sums + swap(sums, "col", 1), count)
    last = functools.partial(last_kernel, float(count * row_block))
    return call_whole(last, [panel], sums, grad, curve, weights, blocks)[0]


def solution(mesh):
    placed = (
        P(("groups", "row"), "col"),
        P("groups", "row"),
        P("row", ("groups", "col")),
        P(None, "groups"),
    )
    return jax.shard_map(
        per_device,
        mesh=mesh,
        in_specs=placed,
        out_specs=P("row", ("groups", "col")),
        check_vma=False,
    )
```

```python
import functools

import jax
import jax.numpy as jnp
from jax import lax
from jax.experimental import pallas as pl
from jax.experimental.pallas import tpu as pltpu
from jax.sharding import PartitionSpec as P

BLK = 128
TILE = 896
PART = 448
LIMIT = 8 * 1024 * 1024
HEAD_LIMIT = 60 * 1024 * 1024
AXES = ("row", "col")

damping_ratio = 0.3
epsilon = 1e-06


def swap(value, axis, distance):
    return lax.ppermute(value, axis, [(i, i ^ distance) for i in range(lax.axis_size(axis))])


def sum_part(value, count):
    devices = 2 * count
    shifts = [[(i, i ^ k) for i in range(devices)] for k in (1, 2, 3)]
    value += sum(lax.ppermute(value, AXES, pairs) for pairs in shifts)
    shifts = [[(i, (i + k) % devices) for i in range(devices)] for k in range(4, devices, 4)]
    return value + sum(lax.ppermute(value, AXES, pairs) for pairs in shifts)


def expand_local(block_mask, row_index, row_block, col_index, width_cols):
    if width_cols != BLK:
        row_ids = (row_index * row_block + jnp.arange(row_block, dtype=jnp.int32)) // BLK
        col_ids = (col_index * width_cols + jnp.arange(width_cols, dtype=jnp.int32)) // BLK
        return block_mask[row_ids][:, col_ids].astype(jnp.float32)
    piece = BLK
    while row_block % piece:
        piece //= 2
    column = lax.dynamic_index_in_dim(block_mask, col_index, 1, keepdims=False)
    column = jnp.repeat(column, BLK // piece) if piece != BLK else column
    count = row_block // piece
    own = lax.dynamic_slice_in_dim(column, row_index * count, count, 0).astype(jnp.float32)
    return jnp.broadcast_to(own[:, None, None], (count, piece, width_cols)).reshape(
        row_block, width_cols
    )


class Ring:
    def __init__(self, count):
        self.count = count
        self.order = list(range(0, count, 2)) + list(range(count - 1, 0, -2))
        self.last = count // 2 - 1

    def row(self, place):
        return self.order[place % self.count]

    def half(self, place):
        return self.row(place) * 2 // self.count

    def ahead(self, place):
        return int(place % self.count >= self.count // 2)

    def device(self, place, core):
        return self.row(place) * 2 + core

    def source(self, place, core, step):
        return place - 1 - step if core == self.ahead(place) else place + 1 + step

    def first_column(self, place, core, step):
        origin = self.ahead(self.source(place, core, step))
        return origin if core == self.ahead(place) else 1 - origin

    def places(self):
        return [(place, core) for place in range(self.count) for core in range(2)]

    def shift(self):
        pairs = []
        for place in range(self.count):
            pairs.append(
                (self.device(place, self.ahead(place)), self.device(place + 1, self.ahead(place + 1)))
            )
            pairs.append(
                (
                    self.device(place, 1 - self.ahead(place)),
                    self.device(place - 1, 1 - self.ahead(place - 1)),
                )
            )
        return pairs

    def hand_over(self, step):
        return [
            (self.device(place, core), self.device(place, 1 - core))
            for place, core in self.places()
            if self.half(self.source(place, core, step)) != core
        ]

    def slots(self):
        found = []
        for step in range(self.last):
            found.append((True, step))
            if self.hand_over(step):
                found.append((False, step))
        return found + [(True, self.last)]

    def loads(self, slot):
        base = 3 * (1 + len(self.slots()))
        return [base + slot + 1] if slot + 1 < self.count // 2 else []

    def entry(self, place, core, carrier, step):
        source = self.source(place, carrier, step)
        return [
            self.row(source) % (self.count // 2),
            int(self.half(source) == core),
            int(self.first_column(place, carrier, step) != core),
        ]

    def table(self):
        half = self.count // 2
        lines = [None] * (2 * self.count)
        for place, core in self.places():
            line = [self.row(place) % half, int(self.half(place) == core), 0]
            for carrier, step in self.slots():
                line += self.entry(place, core, core if carrier else 1 - core, step)
            needed = [line[k] for k in range(0, len(line), 3) if line[k + 1]]
            line += needed
            lines[self.device(place, core)] = line
        return lines


def pick(ring, entry):
    device = lax.axis_index("row") * 2 + lax.axis_index("col")
    values = [line[entry] for line in ring.table()]
    picked = jnp.int32(values[0])
    for index, value in enumerate(values):
        if value != values[0]:
            picked = jnp.where(device == index, jnp.int32(value), picked)
    return picked


def block_copies(ring, load, gram, store, sems):
    rows = gram.shape[0]
    there = pl.ds(pl.multiple_of(pick(ring, load) * rows, BLK), rows)
    parts = [pl.ds(part * PART, PART) for part in range(rows // PART)]
    return [
        pltpu.make_async_copy(gram.at[here, there], store.at[here, there], sems.at[part])
        for part, here in enumerate(parts)
    ]


def load_kernel(ring, load, gram, acts, second, store, across, passed, sems):
    copies = block_copies(ring, load, gram, store, sems)
    for copy in copies:
        copy.start()
    across[...] = acts[...].astype(jnp.float32).T.astype(across.dtype)
    for copy in copies:
        copy.wait()


def load_first(ring, gram, acts, second):
    whole = pl.BlockSpec(memory_space=pltpu.VMEM)
    return pl.pallas_call(
        functools.partial(load_kernel, ring, ring.loads(-1)[0]),
        in_specs=[pl.BlockSpec(memory_space=pltpu.HBM), whole, whole],
        out_specs=[whole] * 3,
        out_shape=[
            jax.ShapeDtypeStruct(gram.shape, gram.dtype),
            jax.ShapeDtypeStruct(acts.shape[::-1], acts.dtype),
            jax.ShapeDtypeStruct(second.shape, second.dtype),
        ],
        scratch_shapes=[pltpu.SemaphoreType.DMA((gram.shape[0] // PART,))],
        input_output_aliases={2: 2},
        compiler_params=pltpu.CompilerParams(vmem_limit_bytes=LIMIT),
    )(gram, acts, second)


def product_kernel(ring, slot, loads, gram, first, second, across, *refs):
    copies = []
    if loads:
        own, other, store, sems = refs[-4:]
        copies = block_copies(ring, loads[0], gram, store, sems)
    else:
        store = gram
        own, other = refs[-2:]
    for copy in copies:
        copy.start()
    rows, width = own.shape
    start = pl.multiple_of(pick(ring, 3 * slot) * rows, BLK)
    flip = pick(ring, 3 * slot + 2) == 1
    if slot == 0:
        own[...] = jnp.zeros_like(own)
        other[...] = jnp.zeros_like(other)

    @pl.when(pick(ring, 3 * slot + 1) == 1)
    def _():
        @pl.loop(0, rows // TILE)
        def _(tile):
            here = pl.ds(pl.multiple_of(tile * TILE, TILE), TILE)
            lines = jnp.concatenate([store[here, pl.ds(start, rows)], across[here, :]], axis=1)
            panel = jnp.concatenate([first[...], second[...]], axis=1)
            result = jnp.dot(lines, panel, preferred_element_type=jnp.float32)
            left, right = result[:, :width], result[:, width:]
            own[here, :] += jnp.where(flip, right, left)
            other[here, :] += jnp.where(flip, left, right)

    for copy in copies:
        copy.wait()


def product(ring, slot, loads, gram, store, message, across, acc):
    rows = across.shape[0]
    width = message[0].shape[1]
    whole = pl.BlockSpec(memory_space=pltpu.VMEM)
    out_shape = [jax.ShapeDtypeStruct((rows, width), jnp.float32)] * 2
    in_specs = [whole] * (4 + len(acc))
    operands = [store, *message, across, *acc]
    scratch = []
    if loads:
        operands = [gram, *message, across, *acc, store]
        in_specs[0] = pl.BlockSpec(memory_space=pltpu.HBM)
        in_specs.append(whole)
        out_shape.append(jax.ShapeDtypeStruct(gram.shape, gram.dtype))
        scratch = [pltpu.SemaphoreType.DMA((rows // PART,))]
    given = len(operands) - 4
    results = pl.pallas_call(
        functools.partial(product_kernel, ring, slot, loads),
        in_specs=in_specs,
        out_specs=[whole] * len(out_shape),
        out_shape=out_shape,
        scratch_shapes=scratch,
        input_output_aliases={4 + k: len(out_shape) - given + k for k in range(given)},
        compiler_params=pltpu.CompilerParams(vmem_limit_bytes=LIMIT),
        cost_estimate=pl.CostEstimate(
            flops=4 * rows * rows * width, bytes_accessed=2 * rows * rows, transcendentals=0
        ),
    )(*operands)
    return results[:2], results[2] if loads else store


def after(value, others):
    return lax.optimization_barrier((value, *others))[0]


def ring_apply(ring, gram, message, early):
    first = message
    store, across, second = early(swap(message, "col", 1))
    ready = [(first, second)]
    acc = []
    slot = 0

    def work(others=()):
        nonlocal acc, store, slot
        if not ready:
            return
        parts = ready.pop(0)
        parts = (after(parts[0], others), parts[1])
        loads = [] if gram is None else ring.loads(slot)
        acc, store = product(ring, slot, loads, gram, store, parts, across, acc)
        slot += 1

    def hand_over(step):
        if ring.hand_over(step):
            ready.append(tuple(swap(after(part, acc[:1]), "col", 1) for part in held))

    for step in range(ring.last):
        came = lax.ppermute(after(first, acc[:1]), AXES, ring.shift())
        if step:
            work([first])
        second = lax.ppermute(after(second, acc[:1]), AXES, ring.shift())
        if step:
            hand_over(step - 1)
            work()
        first = came
        held = (first, second)
        ready.append(held)
    first = lax.ppermute(after(first, acc[:1]), AXES, ring.shift())
    hand_over(ring.last - 1)
    work()
    last = (first, swap(after(first, acc[:1]), "col", 1))
    while ready:
        work()
    ready.append(last)
    work()
    return acc[0], swap(acc[1], "col", 1), store


def trace_kernel(ring, store, acts, second, trace):
    trace[...] = jnp.zeros_like(trace)

    @pl.when(pick(ring, 1) == 1)
    def _():
        rows = acts.shape[1]
        start = pick(ring, 0) * rows
        lines = lax.broadcasted_iota(jnp.int32, (BLK, BLK), 0)
        same = lines == lax.broadcasted_iota(jnp.int32, (BLK, BLK), 1)
        for block in range(rows // BLK):
            here = slice(block * BLK, (block + 1) * BLK)
            there = pl.ds(pl.multiple_of(start + block * BLK, BLK), BLK)
            square = store[here, there].astype(jnp.float32)
            diag = jnp.sum(jnp.where(same, square, 0.0), axis=0, keepdims=True)
            part = acts[:, here].astype(jnp.float32)
            diag += jnp.sum(part * part, axis=0, keepdims=True)
            trace[0:1, :] += diag.astype(jnp.bfloat16).astype(jnp.float32)


def trace_part(ring, store, acts, second):
    whole = pl.BlockSpec(memory_space=pltpu.VMEM)
    return pl.pallas_call(
        functools.partial(trace_kernel, ring),
        in_specs=[whole] * 3,
        out_specs=whole,
        out_shape=jax.ShapeDtypeStruct((8, BLK), jnp.float32),
        compiler_params=pltpu.CompilerParams(vmem_limit_bytes=LIMIT),
    )(store, acts, second)


def put_message(message, acts, rows):
    message[rows:, :] = jnp.dot(
        acts[...], message[:rows, :], preferred_element_type=jnp.float32
    ).astype(message.dtype)


def head_kernel(mask, weights, acts, message, dense, samples, sems):
    copies = [
        pltpu.make_async_copy(weights, dense, sems.at[0]),
        pltpu.make_async_copy(acts, samples, sems.at[1]),
    ]
    for copy in copies:
        copy.start()
    copies[0].wait()
    rows = weights.shape[0]
    top, column = lax.axis_index("row") * (rows // BLK), lax.axis_index("col")
    for block in range(rows // BLK):
        here = slice(block * BLK, (block + 1) * BLK)
        kept = mask[column, top + block].astype(jnp.float32)
        message[here, :] = (kept * dense[here, :] - dense[here, :]).astype(message.dtype)
    copies[1].wait()
    put_message(message, samples, rows)


def first_message(block_mask, weights, acts, letter):
    smem = pl.BlockSpec(memory_space=pltpu.SMEM)
    hbm = pl.BlockSpec(memory_space=pltpu.HBM)
    return pl.pallas_call(
        head_kernel,
        in_specs=[smem, hbm, hbm],
        out_specs=pl.BlockSpec(memory_space=pltpu.VMEM),
        out_shape=letter,
        scratch_shapes=[
            pltpu.VMEM(weights.shape, weights.dtype),
            pltpu.VMEM(acts.shape, acts.dtype),
            pltpu.SemaphoreType.DMA((2,)),
        ],
        compiler_params=pltpu.CompilerParams(vmem_limit_bytes=HEAD_LIMIT),
    )(block_mask.T, weights, acts)


def turn_kernel(own, received, blocks, acts, grad, message):
    rows = own.shape[0]
    for block in range(rows // BLK):
        here = slice(block * BLK, (block + 1) * BLK)
        grad_first = own[here, :] + received[here, :]
        grad[here, :] = grad_first
        message[here, :] = (blocks[block : block + 1, :] * grad_first).astype(message.dtype)
    put_message(message, acts, rows)


def lane_sums(value):
    return jnp.sum(value, axis=0, keepdims=True)


def curve_kernel(trace, grad, own, received, blocks, curve_ref, sums_ref):
    rows = grad.shape[0]
    sums_ref[...] = jnp.zeros_like(sums_ref)
    sums_ref[0:1, :] = trace[0:1, :]
    for block in range(rows // BLK):
        here = slice(block * BLK, (block + 1) * BLK)
        kept = blocks[block : block + 1, :]
        curve = own[here, :] + received[here, :]
        curve_ref[here, :] = curve
        step_dir = kept * grad[here, :]
        masked = kept * curve
        sums_ref[1:2, :] += lane_sums(step_dir * step_dir)
        sums_ref[2:3, :] += lane_sums(step_dir * curve)
        sums_ref[3:4, :] += lane_sums(masked * masked)


def last_kernel(units, sums, grad, curve, weights, blocks, out_ref):
    totals = jnp.sum(sums[...], axis=1, keepdims=True)
    trace_total, grad_square = totals[0:1, :], totals[1:2, :]
    grad_curve, curve_square = totals[2:3, :], totals[3:4, :]
    damping = damping_ratio * trace_total / units
    step_first = grad_square / (grad_curve + damping * grad_square + epsilon)
    step_second = (grad_curve + damping * grad_square) / (
        curve_square + 2.0 * damping * grad_curve + damping * damping * grad_square + epsilon
    )
    rows = grad.shape[0]
    for block in range(rows // BLK):
        here = slice(block * BLK, (block + 1) * BLK)
        kept = blocks[block : block + 1, :]
        grad_first = grad[here, :]
        step_dir = kept * grad_first
        grad_second = grad_first - step_first * curve[here, :]
        out_ref[here, :] = (
            kept * weights[here, :] - step_first * step_dir - step_second * (kept * grad_second)
        )


def gather_apply(gram, activations, panel, col_index):
    half = gram.shape[1]
    full = lax.all_gather(panel, "row", axis=0, tiled=True)
    own_half = lax.dynamic_slice_in_dim(full, col_index * half, half, 0)
    need = lax.dynamic_slice_in_dim(full, (1 - col_index) * half, half, 0)
    other_half = swap(need, "col", 1)
    own = jnp.dot(gram, own_half, preferred_element_type=jnp.float32)
    partial = jnp.dot(gram, other_half, preferred_element_type=jnp.float32)
    low = lax.psum(jnp.dot(activations, panel, preferred_element_type=jnp.float32), "row")
    update = lax.dot_general(
        activations.astype(jnp.float32),
        low,
        (((0,), (0,)), ((), ())),
        precision=lax.Precision.HIGHEST,
        preferred_element_type=jnp.float32,
    )
    return own + swap(partial, "col", 1) + update


def per_device_general(gram_old, activations, weights, block_mask):
    row_block, half_width = gram_old.shape
    width_cols = weights.shape[1]
    units = lax.axis_size("row") * row_block
    row_index = lax.axis_index("row")
    col_index = lax.axis_index("col")
    mask_local = expand_local(block_mask, row_index, row_block, col_index, width_cols)
    kept_weights = mask_local * weights
    diff_low = (kept_weights - weights).astype(jnp.bfloat16)
    acts = activations.astype(jnp.float32)
    column_squares = jnp.sum(acts * acts, axis=0)
    grad_first = gather_apply(gram_old, activations, diff_low, col_index)
    place = row_index * row_block + jnp.arange(row_block, dtype=jnp.int32)
    place = place - col_index * half_width
    on_diagonal = jnp.arange(half_width, dtype=jnp.int32)[None, :] == place[:, None]
    new_gram = gram_old.astype(jnp.float32) + column_squares[:, None]
    new_gram = new_gram.astype(jnp.bfloat16).astype(jnp.float32)
    trace_part = jnp.sum(jnp.where(on_diagonal, new_gram, 0.0))
    step_dir = mask_local * grad_first
    curvature = gather_apply(gram_old, activations, step_dir.astype(jnp.bfloat16), col_index)
    masked_curve = mask_local * curvature
    sums = jnp.stack(
        [
            trace_part,
            jnp.sum(step_dir * step_dir),
            jnp.sum(step_dir * curvature),
            jnp.sum(masked_curve * masked_curve),
        ]
    )
    sums = lax.psum(sums, ("row", "col"))
    trace_total, grad_square, grad_curve, curve_square = sums[0], sums[1], sums[2], sums[3]
    damping = damping_ratio * trace_total / units
    step_first = grad_square / (grad_curve + damping * grad_square + epsilon)
    step_second = (grad_curve + damping * grad_square) / (
        curve_square + 2.0 * damping * grad_curve + damping * damping * grad_square + epsilon
    )
    grad_second = grad_first - step_first * curvature
    return kept_weights - step_first * step_dir - step_second * (mask_local * grad_second)


def call_whole(kernel, out_shape, *operands):
    whole = pl.BlockSpec(memory_space=pltpu.VMEM)
    return pl.pallas_call(
        kernel,
        in_specs=[whole] * len(operands),
        out_specs=[whole] * len(out_shape),
        out_shape=out_shape,
        compiler_params=pltpu.CompilerParams(vmem_limit_bytes=LIMIT),
    )(*operands)


def per_device(gram_old, activations, weights, block_mask):
    row_block, _ = gram_old.shape
    width = weights.shape[1]
    samples = activations.shape[0]
    count = lax.axis_size("row")
    if row_block % TILE or count not in (4, 8, 16) or width != BLK or samples % 16:
        return per_device_general(gram_old, activations, weights, block_mask)
    ring = Ring(count)
    row_index = lax.axis_index("row")
    col_index = lax.axis_index("col")
    per_block = row_block // BLK
    own_mask = lax.dynamic_slice(block_mask, (row_index * per_block, col_index), (per_block, 1))
    blocks = jnp.broadcast_to(own_mask.astype(jnp.float32), (per_block, width))
    panel = jax.ShapeDtypeStruct((row_block, width), jnp.float32)
    letter = jax.ShapeDtypeStruct((row_block + samples, width), jnp.bfloat16)
    eight = jax.ShapeDtypeStruct((8, width), jnp.float32)

    message = first_message(block_mask, weights, activations, letter)
    across = trace = None

    def load(second):
        nonlocal across
        store, across, second = load_first(ring, gram_old, activations, second)
        return store, across, second

    own, received, store = ring_apply(ring, gram_old, message, load)
    grad, message = call_whole(turn_kernel, [panel, letter], own, received, blocks, activations)

    def add_trace(second):
        nonlocal trace
        trace = trace_part(ring, store, activations, second)
        return store, across, second

    own, received, _ = ring_apply(ring, None, message, add_trace)
    curve, sums = call_whole(curve_kernel, [panel, eight], trace, grad, own, received, blocks)
    sums = sum_part(sums, count)
    last = functools.partial(last_kernel, float(count * row_block))
    return call_whole(last, [panel], sums, grad, curve, weights, blocks)[0]


def solution(mesh):
    placed = (
        P(("groups", "row"), "col"),
        P("groups", "row"),
        P("row", ("groups", "col")),
        P(None, "groups"),
    )
    return jax.shard_map(
        per_device,
        mesh=mesh,
        in_specs=placed,
        out_specs=P("row", ("groups", "col")),
        check_vma=False,
    )
```

```python
import functools

import jax
import jax.numpy as jnp
from jax import lax
from jax.experimental import pallas as pl
from jax.experimental.pallas import tpu as pltpu
from jax.sharding import PartitionSpec as P

BLK = 128
TILE = 896
PART = 448
LIMIT = 8 * 1024 * 1024
HEAD_LIMIT = 60 * 1024 * 1024
AXES = ("row", "col")

damping_ratio = 0.3
epsilon = 1e-06


def swap(value, axis, distance):
    return lax.ppermute(value, axis, [(i, i ^ distance) for i in range(lax.axis_size(axis))])


def sum_part(value, count):
    devices = 2 * count
    shifts = [[(i, i ^ k) for i in range(devices)] for k in (1, 2, 3)]
    value += sum(lax.ppermute(value, AXES, pairs) for pairs in shifts)
    shifts = [[(i, (i + k) % devices) for i in range(devices)] for k in range(4, devices, 4)]
    return value + sum(lax.ppermute(value, AXES, pairs) for pairs in shifts)


def expand_local(block_mask, row_index, row_block, col_index, width_cols):
    if width_cols != BLK:
        row_ids = (row_index * row_block + jnp.arange(row_block, dtype=jnp.int32)) // BLK
        col_ids = (col_index * width_cols + jnp.arange(width_cols, dtype=jnp.int32)) // BLK
        return block_mask[row_ids][:, col_ids].astype(jnp.float32)
    piece = BLK
    while row_block % piece:
        piece //= 2
    column = lax.dynamic_index_in_dim(block_mask, col_index, 1, keepdims=False)
    column = jnp.repeat(column, BLK // piece) if piece != BLK else column
    count = row_block // piece
    own = lax.dynamic_slice_in_dim(column, row_index * count, count, 0).astype(jnp.float32)
    return jnp.broadcast_to(own[:, None, None], (count, piece, width_cols)).reshape(
        row_block, width_cols
    )


class Ring:
    def __init__(self, count):
        self.count = count
        self.order = list(range(0, count, 2)) + list(range(count - 1, 0, -2))
        self.last = count // 2 - 1

    def row(self, place):
        return self.order[place % self.count]

    def half(self, place):
        return self.row(place) * 2 // self.count

    def ahead(self, place):
        return int(place % self.count >= self.count // 2)

    def device(self, place, core):
        return self.row(place) * 2 + core

    def source(self, place, core, step):
        return place - 1 - step if core == self.ahead(place) else place + 1 + step

    def first_column(self, place, core, step):
        origin = self.ahead(self.source(place, core, step))
        return origin if core == self.ahead(place) else 1 - origin

    def places(self):
        return [(place, core) for place in range(self.count) for core in range(2)]

    def shift(self):
        pairs = []
        for place in range(self.count):
            pairs.append(
                (self.device(place, self.ahead(place)), self.device(place + 1, self.ahead(place + 1)))
            )
            pairs.append(
                (
                    self.device(place, 1 - self.ahead(place)),
                    self.device(place - 1, 1 - self.ahead(place - 1)),
                )
            )
        return pairs

    def hand_over(self, step):
        return [
            (self.device(place, core), self.device(place, 1 - core))
            for place, core in self.places()
            if self.half(self.source(place, core, step)) != core
        ]

    def slots(self):
        found = []
        for step in range(self.last):
            found.append((True, step))
            if self.hand_over(step):
                found.append((False, step))
        return found + [(True, self.last)]

    def loads(self, slot):
        base = 3 * (1 + len(self.slots()))
        return [base + slot + 1] if slot + 1 < self.count // 2 else []

    def entry(self, place, core, carrier, step):
        source = self.source(place, carrier, step)
        return [
            self.row(source) % (self.count // 2),
            int(self.half(source) == core),
            int(self.first_column(place, carrier, step) != core),
        ]

    def table(self):
        half = self.count // 2
        lines = [None] * (2 * self.count)
        for place, core in self.places():
            line = [self.row(place) % half, int(self.half(place) == core), 0]
            for carrier, step in self.slots():
                line += self.entry(place, core, core if carrier else 1 - core, step)
            needed = [line[k] for k in range(0, len(line), 3) if line[k + 1]]
            line += needed
            lines[self.device(place, core)] = line
        return lines


def pick(ring, entry):
    device = lax.axis_index("row") * 2 + lax.axis_index("col")
    values = [line[entry] for line in ring.table()]
    picked = jnp.int32(values[0])
    for index, value in enumerate(values):
        if value != values[0]:
            picked = jnp.where(device == index, jnp.int32(value), picked)
    return picked


def block_copies(ring, load, gram, store, sems):
    rows = gram.shape[0]
    there = pl.ds(pl.multiple_of(pick(ring, load) * rows, BLK), rows)
    parts = [pl.ds(part * PART, PART) for part in range(rows // PART)]
    return [
        pltpu.make_async_copy(gram.at[here, there], store.at[here, there], sems.at[part])
        for part, here in enumerate(parts)
    ]


def load_kernel(ring, load, gram, acts, second, store, across, passed, sems):
    copies = block_copies(ring, load, gram, store, sems)
    for copy in copies:
        copy.start()
    across[...] = acts[...].astype(jnp.float32).T.astype(across.dtype)
    for copy in copies:
        copy.wait()


def load_first(ring, gram, acts, second):
    whole = pl.BlockSpec(memory_space=pltpu.VMEM)
    return pl.pallas_call(
        functools.partial(load_kernel, ring, ring.loads(-1)[0]),
        in_specs=[pl.BlockSpec(memory_space=pltpu.HBM), whole, whole],
        out_specs=[whole] * 3,
        out_shape=[
            jax.ShapeDtypeStruct(gram.shape, gram.dtype),
            jax.ShapeDtypeStruct(acts.shape[::-1], acts.dtype),
            jax.ShapeDtypeStruct(second.shape, second.dtype),
        ],
        scratch_shapes=[pltpu.SemaphoreType.DMA((gram.shape[0] // PART,))],
        input_output_aliases={2: 2},
        compiler_params=pltpu.CompilerParams(vmem_limit_bytes=LIMIT),
    )(gram, acts, second)


def product_kernel(ring, slot, loads, gram, first, second, across, *refs):
    copies = []
    if loads and slot == 0:
        acts, _, own, other, store, trace, sems = refs
        copies = block_copies(ring, loads[0], gram, store, sems)
        trace[...] = jnp.zeros_like(trace)
    elif loads:
        own, other, store, sems = refs[-4:]
        copies = block_copies(ring, loads[0], gram, store, sems)
    else:
        store = gram
        own, other = refs[-2:]
    for copy in copies:
        copy.start()
    rows, width = own.shape
    start = pl.multiple_of(pick(ring, 3 * slot) * rows, BLK)
    flip = pick(ring, 3 * slot + 2) == 1
    if slot == 0:
        own[...] = jnp.zeros_like(own)
        other[...] = jnp.zeros_like(other)

    @pl.when(pick(ring, 3 * slot + 1) == 1)
    def _():
        @pl.loop(0, rows // TILE)
        def _(tile):
            here = pl.ds(pl.multiple_of(tile * TILE, TILE), TILE)
            lines = jnp.concatenate([store[here, pl.ds(start, rows)], across[here, :]], axis=1)
            panel = jnp.concatenate([first[...], second[...]], axis=1)
            result = jnp.dot(lines, panel, preferred_element_type=jnp.float32)
            left, right = result[:, :width], result[:, width:]
            own[here, :] += jnp.where(flip, right, left)
            other[here, :] += jnp.where(flip, left, right)

        if loads and slot == 0:
            add_diagonal(store, start, acts, trace)

    for copy in copies:
        copy.wait()


def add_diagonal(store, start, acts, trace):
    lines = lax.broadcasted_iota(jnp.int32, (BLK, BLK), 0)
    same = lines == lax.broadcasted_iota(jnp.int32, (BLK, BLK), 1)
    for block in range(acts.shape[1] // BLK):
        here = slice(block * BLK, (block + 1) * BLK)
        there = pl.ds(pl.multiple_of(start + block * BLK, BLK), BLK)
        square = store[here, there].astype(jnp.float32)
        diag = jnp.sum(jnp.where(same, square, 0.0), axis=0, keepdims=True)
        part = acts[:, here].astype(jnp.float32)
        diag += jnp.sum(part * part, axis=0, keepdims=True)
        trace[0:1, :] += diag.astype(jnp.bfloat16).astype(jnp.float32)


def product(ring, slot, loads, gram, store, message, across, acts, acc):
    rows = across.shape[0]
    width = message[0].shape[1]
    whole = pl.BlockSpec(memory_space=pltpu.VMEM)
    out_shape = [jax.ShapeDtypeStruct((rows, width), jnp.float32)] * 2
    operands = [store, *message, across, *acc]
    aliases = {4 + k: k for k in range(len(acc))}
    scratch = []
    with_trace = bool(loads) and slot == 0
    if loads:
        operands = [gram, *message, across, *([acts] if with_trace else acc), store]
        aliases[len(operands) - 1] = 2
        out_shape.append(jax.ShapeDtypeStruct(gram.shape, gram.dtype))
        scratch = [pltpu.SemaphoreType.DMA((rows // PART,))]
    if with_trace:
        out_shape.append(jax.ShapeDtypeStruct((8, width), jnp.float32))
    in_specs = [whole] * len(operands)
    if loads:
        in_specs[0] = pl.BlockSpec(memory_space=pltpu.HBM)
    results = pl.pallas_call(
        functools.partial(product_kernel, ring, slot, loads),
        in_specs=in_specs,
        out_specs=[whole] * len(out_shape),
        out_shape=out_shape,
        scratch_shapes=scratch,
        input_output_aliases=aliases,
        compiler_params=pltpu.CompilerParams(vmem_limit_bytes=LIMIT),
        cost_estimate=pl.CostEstimate(
            flops=4 * rows * rows * width, bytes_accessed=2 * rows * rows, transcendentals=0
        ),
    )(*operands)
    return results[:2], results[2] if loads else store, results[3:]


def after(value, others):
    return lax.optimization_barrier((value, *others))[0]


def ring_apply(ring, gram, message, acts, early):
    first = message
    trace = []
    store, across, second = early(swap(message, "col", 1))
    ready = [(first, second)]
    acc = []
    slot = 0

    def work(others=()):
        nonlocal acc, store, slot, trace
        if not ready:
            return
        parts = ready.pop(0)
        parts = (after(parts[0], others), parts[1])
        loads = [] if gram is None else ring.loads(slot)
        acc, store, added = product(ring, slot, loads, gram, store, parts, across, acts, acc)
        trace = trace or added
        slot += 1

    def hand_over(step):
        if ring.hand_over(step):
            ready.append(tuple(swap(after(part, acc[:1]), "col", 1) for part in held))

    for step in range(ring.last):
        came = lax.ppermute(after(first, acc[:1]), AXES, ring.shift())
        if step:
            work([first])
        second = lax.ppermute(after(second, acc[:1]), AXES, ring.shift())
        if step:
            hand_over(step - 1)
            work()
        first = came
        held = (first, second)
        ready.append(held)
    first = lax.ppermute(after(first, acc[:1]), AXES, ring.shift())
    hand_over(ring.last - 1)
    work()
    last = (first, swap(after(first, acc[:1]), "col", 1))
    while ready:
        work()
    ready.append(last)
    work()
    return acc[0], swap(acc[1], "col", 1), store, trace


def put_message(message, acts, rows):
    message[rows:, :] = jnp.dot(
        acts[...], message[:rows, :], preferred_element_type=jnp.float32
    ).astype(message.dtype)


def head_kernel(mask, weights, acts, message, kept, dense, samples, sems):
    copies = [
        pltpu.make_async_copy(mask, kept, sems.at[0]),
        pltpu.make_async_copy(weights, dense, sems.at[1]),
        pltpu.make_async_copy(acts, samples, sems.at[2]),
    ]
    for copy in copies:
        copy.start()
    for copy in copies:
        copy.wait()
    rows = weights.shape[0]
    top, column = lax.axis_index("row") * (rows // BLK), lax.axis_index("col")
    for block in range(rows // BLK):
        here = slice(block * BLK, (block + 1) * BLK)
        factor = kept[column, top + block].astype(jnp.float32)
        message[here, :] = (factor * dense[here, :] - dense[here, :]).astype(message.dtype)
    put_message(message, samples, rows)


def first_message(block_mask, weights, acts, letter):
    mask = block_mask.T
    return pl.pallas_call(
        head_kernel,
        in_specs=[pl.BlockSpec(memory_space=pltpu.HBM)] * 3,
        out_specs=pl.BlockSpec(memory_space=pltpu.VMEM),
        out_shape=letter,
        scratch_shapes=[
            pltpu.SMEM(mask.shape, mask.dtype),
            pltpu.VMEM(weights.shape, weights.dtype),
            pltpu.VMEM(acts.shape, acts.dtype),
            pltpu.SemaphoreType.DMA((3,)),
        ],
        compiler_params=pltpu.CompilerParams(vmem_limit_bytes=HEAD_LIMIT),
    )(mask, weights, acts)


def turn_kernel(own, received, blocks, acts, grad, message):
    rows = own.shape[0]
    for block in range(rows // BLK):
        here = slice(block * BLK, (block + 1) * BLK)
        grad_first = own[here, :] + received[here, :]
        grad[here, :] = grad_first
        message[here, :] = (blocks[block : block + 1, :] * grad_first).astype(message.dtype)
    put_message(message, acts, rows)


def lane_sums(value):
    return jnp.sum(value, axis=0, keepdims=True)


def curve_kernel(trace, grad, own, received, blocks, curve_ref, sums_ref):
    rows = grad.shape[0]
    sums_ref[...] = jnp.zeros_like(sums_ref)
    sums_ref[0:1, :] = trace[0:1, :]
    for block in range(rows // BLK):
        here = slice(block * BLK, (block + 1) * BLK)
        kept = blocks[block : block + 1, :]
        curve = own[here, :] + received[here, :]
        curve_ref[here, :] = curve
        step_dir = kept * grad[here, :]
        masked = kept * curve
        sums_ref[1:2, :] += lane_sums(step_dir * step_dir)
        sums_ref[2:3, :] += lane_sums(step_dir * curve)
        sums_ref[3:4, :] += lane_sums(masked * masked)


def last_kernel(units, sums, grad, curve, weights, blocks, out_ref):
    totals = jnp.sum(sums[...], axis=1, keepdims=True)
    trace_total, grad_square = totals[0:1, :], totals[1:2, :]
    grad_curve, curve_square = totals[2:3, :], totals[3:4, :]
    damping = damping_ratio * trace_total / units
    step_first = grad_square / (grad_curve + damping * grad_square + epsilon)
    step_second = (grad_curve + damping * grad_square) / (
        curve_square + 2.0 * damping * grad_curve + damping * damping * grad_square + epsilon
    )
    rows = grad.shape[0]
    for block in range(rows // BLK):
        here = slice(block * BLK, (block + 1) * BLK)
        kept = blocks[block : block + 1, :]
        grad_first = grad[here, :]
        step_dir = kept * grad_first
        grad_second = grad_first - step_first * curve[here, :]
        out_ref[here, :] = (
            kept * weights[here, :] - step_first * step_dir - step_second * (kept * grad_second)
        )


def gather_apply(gram, activations, panel, col_index):
    half = gram.shape[1]
    full = lax.all_gather(panel, "row", axis=0, tiled=True)
    own_half = lax.dynamic_slice_in_dim(full, col_index * half, half, 0)
    need = lax.dynamic_slice_in_dim(full, (1 - col_index) * half, half, 0)
    other_half = swap(need, "col", 1)
    own = jnp.dot(gram, own_half, preferred_element_type=jnp.float32)
    partial = jnp.dot(gram, other_half, preferred_element_type=jnp.float32)
    low = lax.psum(jnp.dot(activations, panel, preferred_element_type=jnp.float32), "row")
    update = lax.dot_general(
        activations.astype(jnp.float32),
        low,
        (((0,), (0,)), ((), ())),
        precision=lax.Precision.HIGHEST,
        preferred_element_type=jnp.float32,
    )
    return own + swap(partial, "col", 1) + update


def per_device_general(gram_old, activations, weights, block_mask):
    row_block, half_width = gram_old.shape
    width_cols = weights.shape[1]
    units = lax.axis_size("row") * row_block
    row_index = lax.axis_index("row")
    col_index = lax.axis_index("col")
    mask_local = expand_local(block_mask, row_index, row_block, col_index, width_cols)
    kept_weights = mask_local * weights
    diff_low = (kept_weights - weights).astype(jnp.bfloat16)
    acts = activations.astype(jnp.float32)
    column_squares = jnp.sum(acts * acts, axis=0)
    grad_first = gather_apply(gram_old, activations, diff_low, col_index)
    place = row_index * row_block + jnp.arange(row_block, dtype=jnp.int32)
    place = place - col_index * half_width
    on_diagonal = jnp.arange(half_width, dtype=jnp.int32)[None, :] == place[:, None]
    new_gram = gram_old.astype(jnp.float32) + column_squares[:, None]
    new_gram = new_gram.astype(jnp.bfloat16).astype(jnp.float32)
    trace_part = jnp.sum(jnp.where(on_diagonal, new_gram, 0.0))
    step_dir = mask_local * grad_first
    curvature = gather_apply(gram_old, activations, step_dir.astype(jnp.bfloat16), col_index)
    masked_curve = mask_local * curvature
    sums = jnp.stack(
        [
            trace_part,
            jnp.sum(step_dir * step_dir),
            jnp.sum(step_dir * curvature),
            jnp.sum(masked_curve * masked_curve),
        ]
    )
    sums = lax.psum(sums, ("row", "col"))
    trace_total, grad_square, grad_curve, curve_square = sums[0], sums[1], sums[2], sums[3]
    damping = damping_ratio * trace_total / units
    step_first = grad_square / (grad_curve + damping * grad_square + epsilon)
    step_second = (grad_curve + damping * grad_square) / (
        curve_square + 2.0 * damping * grad_curve + damping * damping * grad_square + epsilon
    )
    grad_second = grad_first - step_first * curvature
    return kept_weights - step_first * step_dir - step_second * (mask_local * grad_second)


def call_whole(kernel, out_shape, *operands):
    whole = pl.BlockSpec(memory_space=pltpu.VMEM)
    return pl.pallas_call(
        kernel,
        in_specs=[whole] * len(operands),
        out_specs=[whole] * len(out_shape),
        out_shape=out_shape,
        compiler_params=pltpu.CompilerParams(vmem_limit_bytes=LIMIT),
    )(*operands)


def per_device(gram_old, activations, weights, block_mask):
    row_block, _ = gram_old.shape
    width = weights.shape[1]
    samples = activations.shape[0]
    count = lax.axis_size("row")
    if row_block % TILE or count not in (4, 8, 16) or width != BLK or samples % 16:
        return per_device_general(gram_old, activations, weights, block_mask)
    ring = Ring(count)
    row_index = lax.axis_index("row")
    col_index = lax.axis_index("col")
    per_block = row_block // BLK
    own_mask = lax.dynamic_slice(block_mask, (row_index * per_block, col_index), (per_block, 1))
    blocks = jnp.broadcast_to(own_mask.astype(jnp.float32), (per_block, width))
    panel = jax.ShapeDtypeStruct((row_block, width), jnp.float32)
    letter = jax.ShapeDtypeStruct((row_block + samples, width), jnp.bfloat16)
    eight = jax.ShapeDtypeStruct((8, width), jnp.float32)

    message = first_message(block_mask, weights, activations, letter)
    across = None

    def load(second):
        nonlocal across
        store, across, second = load_first(ring, gram_old, activations, second)
        return store, across, second

    own, received, store, (trace,) = ring_apply(ring, gram_old, message, activations, load)
    grad, message = call_whole(turn_kernel, [panel, letter], own, received, blocks, activations)

    def keep(second):
        return store, across, second

    own, received, _, _ = ring_apply(ring, None, message, activations, keep)
    curve, sums = call_whole(curve_kernel, [panel, eight], trace, grad, own, received, blocks)
    sums = sum_part(sums, count)
    last = functools.partial(last_kernel, float(count * row_block))
    return call_whole(last, [panel], sums, grad, curve, weights, blocks)[0]


def solution(mesh):
    placed = (
        P(("groups", "row"), "col"),
        P("groups", "row"),
        P("row", ("groups", "col")),
        P(None, "groups"),
    )
    return jax.shard_map(
        per_device,
        mesh=mesh,
        in_specs=placed,
        out_specs=P("row", ("groups", "col")),
        check_vma=False,
    )
```

```python
import functools

import jax
import jax.numpy as jnp
from jax import lax
from jax.experimental import pallas as pl
from jax.experimental.pallas import tpu as pltpu
from jax.sharding import PartitionSpec as P

BLK = 128
TILE = 896
PART = 448
LIMIT = 8 * 1024 * 1024
AXES = ("row", "col")

damping_ratio = 0.3
epsilon = 1e-06


def swap(value, axis, distance):
    return lax.ppermute(value, axis, [(i, i ^ distance) for i in range(lax.axis_size(axis))])


def sum_part(value, count):
    devices = 2 * count
    shifts = [[(i, i ^ k) for i in range(devices)] for k in (1, 2, 3)]
    value += sum(lax.ppermute(value, AXES, pairs) for pairs in shifts)
    shifts = [[(i, (i + k) % devices) for i in range(devices)] for k in range(4, devices, 4)]
    return value + sum(lax.ppermute(value, AXES, pairs) for pairs in shifts)


def expand_local(block_mask, row_index, row_block, col_index, width_cols):
    if width_cols != BLK:
        row_ids = (row_index * row_block + jnp.arange(row_block, dtype=jnp.int32)) // BLK
        col_ids = (col_index * width_cols + jnp.arange(width_cols, dtype=jnp.int32)) // BLK
        return block_mask[row_ids][:, col_ids].astype(jnp.float32)
    piece = BLK
    while row_block % piece:
        piece //= 2
    column = lax.dynamic_index_in_dim(block_mask, col_index, 1, keepdims=False)
    column = jnp.repeat(column, BLK // piece) if piece != BLK else column
    count = row_block // piece
    own = lax.dynamic_slice_in_dim(column, row_index * count, count, 0).astype(jnp.float32)
    return jnp.broadcast_to(own[:, None, None], (count, piece, width_cols)).reshape(
        row_block, width_cols
    )


class Ring:
    def __init__(self, count):
        self.count = count
        self.order = list(range(0, count, 2)) + list(range(count - 1, 0, -2))
        self.last = count // 2 - 1

    def row(self, place):
        return self.order[place % self.count]

    def half(self, place):
        return self.row(place) * 2 // self.count

    def ahead(self, place):
        return int(place % self.count >= self.count // 2)

    def device(self, place, core):
        return self.row(place) * 2 + core

    def source(self, place, core, step):
        return place - 1 - step if core == self.ahead(place) else place + 1 + step

    def first_column(self, place, core, step):
        origin = self.ahead(self.source(place, core, step))
        return origin if core == self.ahead(place) else 1 - origin

    def places(self):
        return [(place, core) for place in range(self.count) for core in range(2)]

    def shift(self):
        pairs = []
        for place in range(self.count):
            pairs.append(
                (self.device(place, self.ahead(place)), self.device(place + 1, self.ahead(place + 1)))
            )
            pairs.append(
                (
                    self.device(place, 1 - self.ahead(place)),
                    self.device(place - 1, 1 - self.ahead(place - 1)),
                )
            )
        return pairs

    def hand_over(self, step):
        return [
            (self.device(place, core), self.device(place, 1 - core))
            for place, core in self.places()
            if self.half(self.source(place, core, step)) != core
        ]

    def slots(self):
        found = []
        for step in range(self.last):
            found.append((True, step))
            if self.hand_over(step):
                found.append((False, step))
        return found + [(True, self.last)]

    def loads(self, slot):
        base = 3 * (1 + len(self.slots()))
        return [base + slot + 1] if slot + 1 < self.count // 2 else []

    def entry(self, place, core, carrier, step):
        source = self.source(place, carrier, step)
        return [
            self.row(source) % (self.count // 2),
            int(self.half(source) == core),
            int(self.first_column(place, carrier, step) != core),
        ]

    def table(self):
        half = self.count // 2
        lines = [None] * (2 * self.count)
        for place, core in self.places():
            line = [self.row(place) % half, int(self.half(place) == core), 0]
            for carrier, step in self.slots():
                line += self.entry(place, core, core if carrier else 1 - core, step)
            needed = [line[k] for k in range(0, len(line), 3) if line[k + 1]]
            line += needed
            lines[self.device(place, core)] = line
        return lines


def pick(ring, entry):
    device = lax.axis_index("row") * 2 + lax.axis_index("col")
    values = [line[entry] for line in ring.table()]
    picked = jnp.int32(values[0])
    for index, value in enumerate(values):
        if value != values[0]:
            picked = jnp.where(device == index, jnp.int32(value), picked)
    return picked


def block_copies(ring, load, gram, store, sems):
    rows = gram.shape[0]
    there = pl.ds(pl.multiple_of(pick(ring, load) * rows, BLK), rows)
    parts = [pl.ds(part * PART, PART) for part in range(rows // PART)]
    return [
        pltpu.make_async_copy(gram.at[here, there], store.at[here, there], sems.at[part])
        for part, here in enumerate(parts)
    ]


def load_kernel(ring, load, gram, acts, second, store, across, passed, sems):
    copies = block_copies(ring, load, gram, store, sems)
    for copy in copies:
        copy.start()
    across[...] = acts[...].astype(jnp.float32).T.astype(across.dtype)
    for copy in copies:
        copy.wait()


def load_first(ring, gram, acts, second):
    whole = pl.BlockSpec(memory_space=pltpu.VMEM)
    return pl.pallas_call(
        functools.partial(load_kernel, ring, ring.loads(-1)[0]),
        in_specs=[pl.BlockSpec(memory_space=pltpu.HBM), whole, whole],
        out_specs=[whole] * 3,
        out_shape=[
            jax.ShapeDtypeStruct(gram.shape, gram.dtype),
            jax.ShapeDtypeStruct(acts.shape[::-1], acts.dtype),
            jax.ShapeDtypeStruct(second.shape, second.dtype),
        ],
        scratch_shapes=[pltpu.SemaphoreType.DMA((gram.shape[0] // PART,))],
        input_output_aliases={2: 2},
        compiler_params=pltpu.CompilerParams(vmem_limit_bytes=LIMIT),
    )(gram, acts, second)


def product_kernel(ring, slot, loads, with_trace, first, second, across, *refs):
    copies = []
    if with_trace:
        acts, gram, _, own, other, store, trace, sems = refs
        trace[...] = jnp.zeros_like(trace)
    elif loads:
        gram, _, own, other, store, sems = refs[-6:]
    else:
        own, other, store = refs[-3:]
    if loads:
        copies = block_copies(ring, loads[0], gram, store, sems)
    for copy in copies:
        copy.start()
    rows, width = own.shape
    start = pl.multiple_of(pick(ring, 3 * slot) * rows, BLK)
    flip = pick(ring, 3 * slot + 2) == 1
    if slot == 0:
        own[...] = jnp.zeros_like(own)
        other[...] = jnp.zeros_like(other)

    @pl.when(pick(ring, 3 * slot + 1) == 1)
    def _():
        @pl.loop(0, rows // TILE)
        def _(tile):
            here = pl.ds(pl.multiple_of(tile * TILE, TILE), TILE)
            lines = jnp.concatenate([store[here, pl.ds(start, rows)], across[here, :]], axis=1)
            panel = jnp.concatenate([first[...], second[...]], axis=1)
            result = jnp.dot(lines, panel, preferred_element_type=jnp.float32)
            left, right = result[:, :width], result[:, width:]
            own[here, :] += jnp.where(flip, right, left)
            other[here, :] += jnp.where(flip, left, right)

        if with_trace:
            add_diagonal(store, start, acts, trace)

    for copy in copies:
        copy.wait()


def add_diagonal(store, start, acts, trace):
    lines = lax.broadcasted_iota(jnp.int32, (BLK, BLK), 0)
    same = lines == lax.broadcasted_iota(jnp.int32, (BLK, BLK), 1)
    for block in range(acts.shape[1] // BLK):
        here = slice(block * BLK, (block + 1) * BLK)
        there = pl.ds(pl.multiple_of(start + block * BLK, BLK), BLK)
        square = store[here, there].astype(jnp.float32)
        diag = jnp.sum(jnp.where(same, square, 0.0), axis=0, keepdims=True)
        part = acts[:, here].astype(jnp.float32)
        diag += jnp.sum(part * part, axis=0, keepdims=True)
        trace[0:1, :] += diag.astype(jnp.bfloat16).astype(jnp.float32)


def product(ring, slot, loads, gram, store, message, across, acts, acc):
    rows = across.shape[0]
    width = message[0].shape[1]
    whole = pl.BlockSpec(memory_space=pltpu.VMEM)
    with_trace = bool(loads) and slot == 0
    operands = [*message, across]
    aliases = {len(operands) + k: k for k in range(len(acc))}
    operands += acc
    in_specs = [whole] * (len(operands) + 1)
    out_shape = [jax.ShapeDtypeStruct((rows, width), jnp.float32)] * 2
    out_shape.append(jax.ShapeDtypeStruct(store.shape, store.dtype))
    scratch = []
    if with_trace:
        operands.append(acts)
        in_specs.append(whole)
        out_shape.append(jax.ShapeDtypeStruct((8, width), jnp.float32))
    aliases[len(operands) + bool(loads)] = 2
    if loads:
        operands.append(gram)
        in_specs.insert(len(operands) - 1, pl.BlockSpec(memory_space=pltpu.HBM))
        scratch = [pltpu.SemaphoreType.DMA((rows // PART,))]
    operands.append(store)
    results = pl.pallas_call(
        functools.partial(product_kernel, ring, slot, loads, with_trace),
        in_specs=in_specs,
        out_specs=[whole] * len(out_shape),
        out_shape=out_shape,
        scratch_shapes=scratch,
        input_output_aliases=aliases,
        compiler_params=pltpu.CompilerParams(vmem_limit_bytes=LIMIT),
        cost_estimate=pl.CostEstimate(
            flops=4 * rows * rows * width, bytes_accessed=2 * rows * rows, transcendentals=0
        ),
    )(*operands)
    return results[:2], results[2], results[3:]


def after(value, others):
    return lax.optimization_barrier((value, *others))[0]


def ring_apply(ring, gram, message, acts, early):
    first = message
    trace = []
    store, across, second = early(swap(message, "col", 1))
    ready = [(first, second)]
    acc = []
    slot = 0

    def work(others=()):
        nonlocal acc, store, slot, trace
        if not ready:
            return
        parts = ready.pop(0)
        parts = (after(parts[0], others), parts[1])
        loads = [] if gram is None else ring.loads(slot)
        acc, store, added = product(ring, slot, loads, gram, store, parts, across, acts, acc)
        trace = trace or added
        slot += 1

    def hand_over(step):
        if ring.hand_over(step):
            ready.append(tuple(swap(after(part, acc[:1]), "col", 1) for part in held))

    for step in range(ring.last):
        came = lax.ppermute(after(first, acc[:1]), AXES, ring.shift())
        if step:
            work([first])
        second = lax.ppermute(after(second, acc[:1]), AXES, ring.shift())
        if step:
            hand_over(step - 1)
            work()
        first = came
        held = (first, second)
        ready.append(held)
    first = lax.ppermute(after(first, acc[:1]), AXES, ring.shift())
    hand_over(ring.last - 1)
    work()
    last = (first, swap(after(first, acc[:1]), "col", 1))
    while ready:
        work()
    ready.append(last)
    work()
    return acc[0], swap(acc[1], "col", 1), store, trace


def put_message(message, acts, rows):
    message[rows:, :] = jnp.dot(
        acts[...], message[:rows, :], preferred_element_type=jnp.float32
    ).astype(message.dtype)


def head_kernel(weights, blocks, acts, message):
    rows = weights.shape[0]
    for block in range(rows // BLK):
        here = slice(block * BLK, (block + 1) * BLK)
        dense = weights[here, :]
        message[here, :] = (blocks[block : block + 1, :] * dense - dense).astype(message.dtype)
    put_message(message, acts, rows)


def turn_kernel(own, received, blocks, acts, _, grad, message, __):
    rows = own.shape[0]
    for block in range(rows // BLK):
        here = slice(block * BLK, (block + 1) * BLK)
        grad_first = own[here, :] + received[here, :]
        grad[here, :] = grad_first
        message[here, :] = (blocks[block : block + 1, :] * grad_first).astype(message.dtype)
    put_message(message, acts, rows)


def lane_sums(value):
    return jnp.sum(value, axis=0, keepdims=True)


def curve_kernel(trace, grad, own, received, blocks, curve_ref, sums_ref):
    rows = grad.shape[0]
    sums_ref[...] = jnp.zeros_like(sums_ref)
    sums_ref[0:1, :] = trace[0:1, :]
    for block in range(rows // BLK):
        here = slice(block * BLK, (block + 1) * BLK)
        kept = blocks[block : block + 1, :]
        curve = own[here, :] + received[here, :]
        curve_ref[here, :] = curve
        step_dir = kept * grad[here, :]
        masked = kept * curve
        sums_ref[1:2, :] += lane_sums(step_dir * step_dir)
        sums_ref[2:3, :] += lane_sums(step_dir * curve)
        sums_ref[3:4, :] += lane_sums(masked * masked)


def last_kernel(units, sums, grad, curve, weights, blocks, out_ref):
    totals = jnp.sum(sums[...], axis=1, keepdims=True)
    trace_total, grad_square = totals[0:1, :], totals[1:2, :]
    grad_curve, curve_square = totals[2:3, :], totals[3:4, :]
    damping = damping_ratio * trace_total / units
    step_first = grad_square / (grad_curve + damping * grad_square + epsilon)
    step_second = (grad_curve + damping * grad_square) / (
        curve_square + 2.0 * damping * grad_curve + damping * damping * grad_square + epsilon
    )
    rows = grad.shape[0]
    for block in range(rows // BLK):
        here = slice(block * BLK, (block + 1) * BLK)
        kept = blocks[block : block + 1, :]
        grad_first = grad[here, :]
        step_dir = kept * grad_first
        grad_second = grad_first - step_first * curve[here, :]
        out_ref[here, :] = (
            kept * weights[here, :] - step_first * step_dir - step_second * (kept * grad_second)
        )


def gather_apply(gram, activations, panel, col_index):
    half = gram.shape[1]
    full = lax.all_gather(panel, "row", axis=0, tiled=True)
    own_half = lax.dynamic_slice_in_dim(full, col_index * half, half, 0)
    need = lax.dynamic_slice_in_dim(full, (1 - col_index) * half, half, 0)
    other_half = swap(need, "col", 1)
    own = jnp.dot(gram, own_half, preferred_element_type=jnp.float32)
    partial = jnp.dot(gram, other_half, preferred_element_type=jnp.float32)
    low = lax.psum(jnp.dot(activations, panel, preferred_element_type=jnp.float32), "row")
    update = lax.dot_general(
        activations.astype(jnp.float32),
        low,
        (((0,), (0,)), ((), ())),
        precision=lax.Precision.HIGHEST,
        preferred_element_type=jnp.float32,
    )
    return own + swap(partial, "col", 1) + update


def per_device_general(gram_old, activations, weights, block_mask):
    row_block, half_width = gram_old.shape
    width_cols = weights.shape[1]
    units = lax.axis_size("row") * row_block
    row_index = lax.axis_index("row")
    col_index = lax.axis_index("col")
    mask_local = expand_local(block_mask, row_index, row_block, col_index, width_cols)
    kept_weights = mask_local * weights
    diff_low = (kept_weights - weights).astype(jnp.bfloat16)
    acts = activations.astype(jnp.float32)
    column_squares = jnp.sum(acts * acts, axis=0)
    grad_first = gather_apply(gram_old, activations, diff_low, col_index)
    place = row_index * row_block + jnp.arange(row_block, dtype=jnp.int32)
    place = place - col_index * half_width
    on_diagonal = jnp.arange(half_width, dtype=jnp.int32)[None, :] == place[:, None]
    new_gram = gram_old.astype(jnp.float32) + column_squares[:, None]
    new_gram = new_gram.astype(jnp.bfloat16).astype(jnp.float32)
    trace_part = jnp.sum(jnp.where(on_diagonal, new_gram, 0.0))
    step_dir = mask_local * grad_first
    curvature = gather_apply(gram_old, activations, step_dir.astype(jnp.bfloat16), col_index)
    masked_curve = mask_local * curvature
    sums = jnp.stack(
        [
            trace_part,
            jnp.sum(step_dir * step_dir),
            jnp.sum(step_dir * curvature),
            jnp.sum(masked_curve * masked_curve),
        ]
    )
    sums = lax.psum(sums, ("row", "col"))
    trace_total, grad_square, grad_curve, curve_square = sums[0], sums[1], sums[2], sums[3]
    damping = damping_ratio * trace_total / units
    step_first = grad_square / (grad_curve + damping * grad_square + epsilon)
    step_second = (grad_curve + damping * grad_square) / (
        curve_square + 2.0 * damping * grad_curve + damping * damping * grad_square + epsilon
    )
    grad_second = grad_first - step_first * curvature
    return kept_weights - step_first * step_dir - step_second * (mask_local * grad_second)


def call_whole(kernel, out_shape, *operands, alias={}):
    whole = pl.BlockSpec(memory_space=pltpu.VMEM)
    return pl.pallas_call(
        kernel,
        in_specs=[whole] * len(operands),
        out_specs=[whole] * len(out_shape),
        out_shape=out_shape,
        input_output_aliases=alias,
        compiler_params=pltpu.CompilerParams(vmem_limit_bytes=LIMIT),
    )(*operands)


def per_device(gram_old, activations, weights, block_mask):
    row_block, _ = gram_old.shape
    width = weights.shape[1]
    samples = activations.shape[0]
    count = lax.axis_size("row")
    if row_block % TILE or count not in (4, 8, 16) or width != BLK or samples % 16:
        return per_device_general(gram_old, activations, weights, block_mask)
    ring = Ring(count)
    row_index = lax.axis_index("row")
    col_index = lax.axis_index("col")
    per_block = row_block // BLK
    own_mask = lax.dynamic_slice(block_mask, (row_index * per_block, col_index), (per_block, 1))
    blocks = jnp.broadcast_to(own_mask.astype(jnp.float32), (per_block, width))
    panel = jax.ShapeDtypeStruct((row_block, width), jnp.float32)
    letter = jax.ShapeDtypeStruct((row_block + samples, width), jnp.bfloat16)
    eight = jax.ShapeDtypeStruct((8, width), jnp.float32)

    (message,) = call_whole(head_kernel, [letter], weights, blocks, activations)
    across = None

    def load(second):
        nonlocal across
        store, across, second = load_first(ring, gram_old, activations, second)
        return store, across, second

    own, received, store, (trace,) = ring_apply(ring, gram_old, message, activations, load)
    held = jax.ShapeDtypeStruct(store.shape, store.dtype)
    grad, message, store = call_whole(
        turn_kernel, [panel, letter, held], own, received, blocks, activations, store, alias={4: 2}
    )

    def keep(second):
        return store, across, second

    own, received, _, _ = ring_apply(ring, None, message, activations, keep)
    curve, sums = call_whole(curve_kernel, [panel, eight], trace, grad, own, received, blocks)
    sums = sum_part(sums, count)
    last = functools.partial(last_kernel, float(count * row_block))
    return call_whole(last, [panel], sums, grad, curve, weights, blocks)[0]


def solution(mesh):
    placed = (
        P(("groups", "row"), "col"),
        P("groups", "row"),
        P("row", ("groups", "col")),
        P(None, "groups"),
    )
    return jax.shard_map(
        per_device,
        mesh=mesh,
        in_specs=placed,
        out_specs=P("row", ("groups", "col")),
        check_vma=False,
    )
```

```python
import functools

import jax
import jax.numpy as jnp
from jax import lax
from jax.experimental import pallas as pl
from jax.experimental.pallas import tpu as pltpu
from jax.sharding import PartitionSpec as P

BLK = 128
TILE = 896
PART = 448
LIMIT = 8 * 1024 * 1024
AXES = ("row", "col")
WEIGHTS = ((1, 1, 0.3, 0.3, 8, 0.02, 0.02), (1, 0.02, 0.3, 2, 4, 0.3, 4))

damping_ratio = 0.3
epsilon = 1e-06


def swap(value, axis, distance):
    return lax.ppermute(value, axis, [(i, i ^ distance) for i in range(lax.axis_size(axis))])


def sum_part(value, count):
    value = value + swap(value, "col", 1)
    distance = 1
    while distance < count:
        value = value + swap(value, "row", distance)
        distance *= 2
    return value


def expand_local(block_mask, row_index, row_block, col_index, width_cols):
    if width_cols != BLK:
        row_ids = (row_index * row_block + jnp.arange(row_block, dtype=jnp.int32)) // BLK
        col_ids = (col_index * width_cols + jnp.arange(width_cols, dtype=jnp.int32)) // BLK
        return block_mask[row_ids][:, col_ids].astype(jnp.float32)
    piece = BLK
    while row_block % piece:
        piece //= 2
    column = lax.dynamic_index_in_dim(block_mask, col_index, 1, keepdims=False)
    column = jnp.repeat(column, BLK // piece) if piece != BLK else column
    count = row_block // piece
    own = lax.dynamic_slice_in_dim(column, row_index * count, count, 0).astype(jnp.float32)
    return jnp.broadcast_to(own[:, None, None], (count, piece, width_cols)).reshape(
        row_block, width_cols
    )


class Ring:
    def __init__(self, count):
        self.count = count
        self.order = list(range(0, count, 2)) + list(range(count - 1, 0, -2))
        self.last = count // 2 - 1

    def row(self, place):
        return self.order[place % self.count]

    def half(self, place):
        return self.row(place) * 2 // self.count

    def ahead(self, place):
        return int(place % self.count >= self.count // 2)

    def device(self, place, core):
        return self.row(place) * 2 + core

    def source(self, place, core, step):
        return place - 1 - step if core == self.ahead(place) else place + 1 + step

    def first_column(self, place, core, step):
        origin = self.ahead(self.source(place, core, step))
        return origin if core == self.ahead(place) else 1 - origin

    def places(self):
        return [(place, core) for place in range(self.count) for core in range(2)]

    def shift(self):
        pairs = []
        for place in range(self.count):
            pairs.append(
                (self.device(place, self.ahead(place)), self.device(place + 1, self.ahead(place + 1)))
            )
            pairs.append(
                (
                    self.device(place, 1 - self.ahead(place)),
                    self.device(place - 1, 1 - self.ahead(place - 1)),
                )
            )
        return pairs

    def hand_over(self, step):
        return [
            (self.device(place, core), self.device(place, 1 - core))
            for place, core in self.places()
            if self.half(self.source(place, core, step)) != core
        ]

    def close(self, sign):
        pairs = []
        for place in range(self.count):
            core = self.ahead(place - sign)
            core = core if sign > 0 else 1 - core
            target = self.half(place + self.count // 2)
            pairs.append((self.device(place - sign, core), self.device(place, target)))
        return pairs

    def slots(self):
        found = []
        for step in range(self.last):
            found.append((True, step))
            if self.hand_over(step):
                found.append((False, step))
        return found

    def loads(self, slot):
        base = 3 * (2 + len(self.slots()))
        return [base + slot + 1] if slot + 1 < self.count // 2 else []

    def entry(self, place, core, carrier, step):
        source = self.source(place, carrier, step)
        return [
            self.row(source) % (self.count // 2),
            int(self.half(source) == core),
            int(self.first_column(place, carrier, step) != core),
        ]

    def table(self):
        half = self.count // 2
        lines = [None] * (2 * self.count)
        for place, core in self.places():
            line = [self.row(place) % half, int(self.half(place) == core), 0]
            for carrier, step in self.slots():
                line += self.entry(place, core, core if carrier else 1 - core, step)
            far = place + half
            line += [self.row(far) % half, int(self.half(far) == core), int(self.ahead(far) != core)]
            needed = [line[k] for k in range(0, len(line), 3) if line[k + 1]]
            line += needed
            lines[self.device(place, core)] = line
        return lines


def pick(ring, entry):
    device = lax.axis_index("row") * 2 + lax.axis_index("col")
    values = [line[entry] for line in ring.table()]
    picked = jnp.int32(values[0])
    for index, value in enumerate(values):
        if value != values[0]:
            picked = jnp.where(device == index, jnp.int32(value), picked)
    return picked


def block_copies(ring, load, gram, store, sems):
    rows = gram.shape[0]
    there = pl.ds(pl.multiple_of(pick(ring, load) * rows, BLK), rows)
    parts = [pl.ds(part * PART, PART) for part in range(rows // PART)]
    return [
        pltpu.make_async_copy(gram.at[here, there], store.at[here, there], sems.at[part])
        for part, here in enumerate(parts)
    ]


def load_kernel(ring, load, gram, acts, second, store, across, passed, sems):
    copies = block_copies(ring, load, gram, store, sems)
    for copy in copies:
        copy.start()
    across[...] = acts[...].astype(jnp.float32).T.astype(across.dtype)
    for copy in copies:
        copy.wait()


def load_first(ring, gram, acts, second):
    whole = pl.BlockSpec(memory_space=pltpu.VMEM)
    return pl.pallas_call(
        functools.partial(load_kernel, ring, ring.loads(-1)[0]),
        in_specs=[pl.BlockSpec(memory_space=pltpu.HBM), whole, whole],
        out_specs=[whole] * 3,
        out_shape=[
            jax.ShapeDtypeStruct(gram.shape, gram.dtype),
            jax.ShapeDtypeStruct(acts.shape[::-1], acts.dtype),
            jax.ShapeDtypeStruct(second.shape, second.dtype),
        ],
        scratch_shapes=[pltpu.SemaphoreType.DMA((gram.shape[0] // PART,))],
        input_output_aliases={2: 2},
        compiler_params=pltpu.CompilerParams(vmem_limit_bytes=LIMIT),
    )(gram, acts, second)


def product_kernel(ring, slot, loads, with_trace, first, second, across, *refs):
    copies = []
    if with_trace:
        acts, gram, _, own, other, store, trace, sems = refs
        trace[...] = jnp.zeros_like(trace)
    elif loads:
        gram, _, own, other, store, sems = refs[-6:]
    else:
        own, other, store = refs[-3:]
    if loads:
        copies = block_copies(ring, loads[0], gram, store, sems)
    for copy in copies:
        copy.start()
    rows, width = own.shape
    start = pl.multiple_of(pick(ring, 3 * slot) * rows, BLK)
    flip = pick(ring, 3 * slot + 2) == 1
    if slot == 0:
        own[...] = jnp.zeros_like(own)
        other[...] = jnp.zeros_like(other)

    @pl.when(pick(ring, 3 * slot + 1) == 1)
    def _():
        @pl.loop(0, rows // TILE)
        def _(tile):
            here = pl.ds(pl.multiple_of(tile * TILE, TILE), TILE)
            lines = jnp.concatenate([store[here, pl.ds(start, rows)], across[here, :]], axis=1)
            panel = jnp.concatenate([first[...], second[...]], axis=1)
            result = jnp.dot(lines, panel, preferred_element_type=jnp.float32)
            left, right = result[:, :width], result[:, width:]
            own[here, :] += jnp.where(flip, right, left)
            other[here, :] += jnp.where(flip, left, right)

        if with_trace:
            add_diagonal(store, start, acts, trace)

    for copy in copies:
        copy.wait()


def add_diagonal(store, start, acts, trace):
    lines = lax.broadcasted_iota(jnp.int32, (BLK, BLK), 0)
    same = lines == lax.broadcasted_iota(jnp.int32, (BLK, BLK), 1)
    for block in range(acts.shape[1] // BLK):
        here = slice(block * BLK, (block + 1) * BLK)
        there = pl.ds(pl.multiple_of(start + block * BLK, BLK), BLK)
        square = store[here, there].astype(jnp.float32)
        diag = jnp.sum(jnp.where(same, square, 0.0), axis=0, keepdims=True)
        part = acts[:, here].astype(jnp.float32)
        diag += jnp.sum(part * part, axis=0, keepdims=True)
        trace[0:1, :] += diag.astype(jnp.bfloat16).astype(jnp.float32)


def product(ring, slot, loads, gram, store, message, across, acts, acc):
    rows = across.shape[0]
    width = message[0].shape[1]
    weight = WEIGHTS[gram is None][slot]
    whole = pl.BlockSpec(memory_space=pltpu.VMEM)
    with_trace = bool(loads) and slot == 0
    operands = [*message, across]
    aliases = {len(operands) + k: k for k in range(len(acc))}
    operands += acc
    in_specs = [whole] * (len(operands) + 1)
    out_shape = [jax.ShapeDtypeStruct((rows, width), jnp.float32)] * 2
    out_shape.append(jax.ShapeDtypeStruct(store.shape, store.dtype))
    scratch = []
    if with_trace:
        operands.append(acts)
        in_specs.append(whole)
        out_shape.append(jax.ShapeDtypeStruct((8, width), jnp.float32))
    aliases[len(operands) + bool(loads)] = 2
    if loads:
        operands.append(gram)
        in_specs.insert(len(operands) - 1, pl.BlockSpec(memory_space=pltpu.HBM))
        scratch = [pltpu.SemaphoreType.DMA((rows // PART,))]
    operands.append(store)
    results = pl.pallas_call(
        functools.partial(product_kernel, ring, slot, loads, with_trace),
        in_specs=in_specs,
        out_specs=[whole] * len(out_shape),
        out_shape=out_shape,
        scratch_shapes=scratch,
        input_output_aliases=aliases,
        compiler_params=pltpu.CompilerParams(vmem_limit_bytes=LIMIT),
        cost_estimate=pl.CostEstimate(
            flops=int(weight * 4 * rows * rows * width),
            bytes_accessed=int(weight * 2 * rows * rows),
            transcendentals=0,
        ),
    )(*operands)
    return results[:2], results[2], results[3:]


def after(value, others):
    return lax.optimization_barrier((value, *others))[0]


def ring_apply(ring, gram, message, acts, early):
    first = message
    trace = []
    store, across, second = early(swap(message, "col", 1))
    ready = [(first, second)]
    acc = []
    slot = 0

    def work(others=()):
        nonlocal acc, store, slot, trace
        if not ready:
            return
        parts = ready.pop(0)
        parts = (after(parts[0], others), parts[1])
        loads = [] if gram is None else ring.loads(slot)
        acc, store, added = product(ring, slot, loads, gram, store, parts, across, acts, acc)
        trace = trace or added
        slot += 1

    def hand_over(step):
        if ring.hand_over(step):
            ready.append(tuple(swap(after(part, acc[:1]), "col", 1) for part in held))

    for step in range(ring.last):
        came = lax.ppermute(after(first, acc[:1]), AXES, ring.shift())
        if step:
            work([first])
        second = lax.ppermute(after(second, acc[:1]), AXES, ring.shift())
        if step:
            hand_over(step - 1)
            work()
        first = came
        held = (first, second)
        ready.append(held)
    last = tuple(lax.ppermute(after(first, acc[:1]), AXES, ring.close(sign)) for sign in (1, -1))
    hand_over(ring.last - 1)
    while ready:
        work()
    (own, other), store, _ = product(ring, slot, [], gram, store, last, across, acts, acc)
    return own, swap(other, "col", 1), store, trace


def put_message(message, acts, rows):
    message[rows:, :] = jnp.dot(
        acts[...], message[:rows, :], preferred_element_type=jnp.float32
    ).astype(message.dtype)


def head_kernel(weights, blocks, acts, message):
    rows = weights.shape[0]
    for block in range(rows // BLK):
        here = slice(block * BLK, (block + 1) * BLK)
        dense = weights[here, :]
        message[here, :] = (blocks[block : block + 1, :] * dense - dense).astype(message.dtype)
    put_message(message, acts, rows)


def turn_kernel(own, received, blocks, acts, _, grad, message, __):
    rows = own.shape[0]
    for block in range(rows // BLK):
        here = slice(block * BLK, (block + 1) * BLK)
        grad_first = own[here, :] + received[here, :]
        grad[here, :] = grad_first
        message[here, :] = (blocks[block : block + 1, :] * grad_first).astype(message.dtype)
    put_message(message, acts, rows)


def lane_sums(value):
    return jnp.sum(value, axis=0, keepdims=True)


def curve_kernel(trace, grad, own, received, blocks, curve_ref, sums_ref):
    rows = grad.shape[0]
    sums_ref[...] = jnp.zeros_like(sums_ref)
    sums_ref[0:1, :] = trace[0:1, :]
    for block in range(rows // BLK):
        here = slice(block * BLK, (block + 1) * BLK)
        kept = blocks[block : block + 1, :]
        curve = own[here, :] + received[here, :]
        curve_ref[here, :] = curve
        step_dir = kept * grad[here, :]
        masked = kept * curve
        sums_ref[1:2, :] += lane_sums(step_dir * step_dir)
        sums_ref[2:3, :] += lane_sums(step_dir * curve)
        sums_ref[3:4, :] += lane_sums(masked * masked)


def last_kernel(units, sums, grad, curve, weights, blocks, out_ref):
    totals = jnp.sum(sums[...], axis=1, keepdims=True)
    trace_total, grad_square = totals[0:1, :], totals[1:2, :]
    grad_curve, curve_square = totals[2:3, :], totals[3:4, :]
    damping = damping_ratio * trace_total / units
    step_first = grad_square / (grad_curve + damping * grad_square + epsilon)
    step_second = (grad_curve + damping * grad_square) / (
        curve_square + 2.0 * damping * grad_curve + damping * damping * grad_square + epsilon
    )
    rows = grad.shape[0]
    for block in range(rows // BLK):
        here = slice(block * BLK, (block + 1) * BLK)
        kept = blocks[block : block + 1, :]
        grad_first = grad[here, :]
        step_dir = kept * grad_first
        grad_second = grad_first - step_first * curve[here, :]
        out_ref[here, :] = (
            kept * weights[here, :] - step_first * step_dir - step_second * (kept * grad_second)
        )


def gather_apply(gram, activations, panel, col_index):
    half = gram.shape[1]
    full = lax.all_gather(panel, "row", axis=0, tiled=True)
    own_half = lax.dynamic_slice_in_dim(full, col_index * half, half, 0)
    need = lax.dynamic_slice_in_dim(full, (1 - col_index) * half, half, 0)
    other_half = swap(need, "col", 1)
    own = jnp.dot(gram, own_half, preferred_element_type=jnp.float32)
    partial = jnp.dot(gram, other_half, preferred_element_type=jnp.float32)
    low = lax.psum(jnp.dot(activations, panel, preferred_element_type=jnp.float32), "row")
    update = lax.dot_general(
        activations.astype(jnp.float32),
        low,
        (((0,), (0,)), ((), ())),
        precision=lax.Precision.HIGHEST,
        preferred_element_type=jnp.float32,
    )
    return own + swap(partial, "col", 1) + update


def per_device_general(gram_old, activations, weights, block_mask):
    row_block, half_width = gram_old.shape
    width_cols = weights.shape[1]
    units = lax.axis_size("row") * row_block
    row_index = lax.axis_index("row")
    col_index = lax.axis_index("col")
    mask_local = expand_local(block_mask, row_index, row_block, col_index, width_cols)
    kept_weights = mask_local * weights
    diff_low = (kept_weights - weights).astype(jnp.bfloat16)
    acts = activations.astype(jnp.float32)
    column_squares = jnp.sum(acts * acts, axis=0)
    grad_first = gather_apply(gram_old, activations, diff_low, col_index)
    place = row_index * row_block + jnp.arange(row_block, dtype=jnp.int32)
    place = place - col_index * half_width
    on_diagonal = jnp.arange(half_width, dtype=jnp.int32)[None, :] == place[:, None]
    new_gram = gram_old.astype(jnp.float32) + column_squares[:, None]
    new_gram = new_gram.astype(jnp.bfloat16).astype(jnp.float32)
    trace_part = jnp.sum(jnp.where(on_diagonal, new_gram, 0.0))
    step_dir = mask_local * grad_first
    curvature = gather_apply(gram_old, activations, step_dir.astype(jnp.bfloat16), col_index)
    masked_curve = mask_local * curvature
    sums = jnp.stack(
        [
            trace_part,
            jnp.sum(step_dir * step_dir),
            jnp.sum(step_dir * curvature),
            jnp.sum(masked_curve * masked_curve),
        ]
    )
    sums = lax.psum(sums, ("row", "col"))
    trace_total, grad_square, grad_curve, curve_square = sums[0], sums[1], sums[2], sums[3]
    damping = damping_ratio * trace_total / units
    step_first = grad_square / (grad_curve + damping * grad_square + epsilon)
    step_second = (grad_curve + damping * grad_square) / (
        curve_square + 2.0 * damping * grad_curve + damping * damping * grad_square + epsilon
    )
    grad_second = grad_first - step_first * curvature
    return kept_weights - step_first * step_dir - step_second * (mask_local * grad_second)


def call_whole(kernel, out_shape, *operands, alias={}):
    whole = pl.BlockSpec(memory_space=pltpu.VMEM)
    return pl.pallas_call(
        kernel,
        in_specs=[whole] * len(operands),
        out_specs=[whole] * len(out_shape),
        out_shape=out_shape,
        input_output_aliases=alias,
        compiler_params=pltpu.CompilerParams(vmem_limit_bytes=LIMIT),
    )(*operands)


def per_device(gram_old, activations, weights, block_mask):
    row_block, _ = gram_old.shape
    width = weights.shape[1]
    samples = activations.shape[0]
    count = lax.axis_size("row")
    if row_block % TILE or count not in (4, 8, 16) or width != BLK or samples % 16:
        return per_device_general(gram_old, activations, weights, block_mask)
    ring = Ring(count)
    row_index = lax.axis_index("row")
    col_index = lax.axis_index("col")
    per_block = row_block // BLK
    own_mask = lax.dynamic_slice(block_mask, (row_index * per_block, col_index), (per_block, 1))
    blocks = jnp.broadcast_to(own_mask.astype(jnp.float32), (per_block, width))
    panel = jax.ShapeDtypeStruct((row_block, width), jnp.float32)
    letter = jax.ShapeDtypeStruct((row_block + samples, width), jnp.bfloat16)
    eight = jax.ShapeDtypeStruct((8, width), jnp.float32)

    (message,) = call_whole(head_kernel, [letter], weights, blocks, activations)
    across = None

    def load(second):
        nonlocal across
        store, across, second = load_first(ring, gram_old, activations, second)
        return store, across, second

    own, received, store, (trace,) = ring_apply(ring, gram_old, message, activations, load)
    held = jax.ShapeDtypeStruct(store.shape, store.dtype)
    grad, message, store = call_whole(
        turn_kernel, [panel, letter, held], own, received, blocks, activations, store, alias={4: 2}
    )

    def keep(second):
        return store, across, second

    own, received, _, _ = ring_apply(ring, None, message, activations, keep)
    curve, sums = call_whole(curve_kernel, [panel, eight], trace, grad, own, received, blocks)
    sums = sum_part(sums, count)
    last = functools.partial(last_kernel, float(count * row_block))
    return call_whole(last, [panel], sums, grad, curve, weights, blocks)[0]


def solution(mesh):
    placed = (
        P(("groups", "row"), "col"),
        P("groups", "row"),
        P("row", ("groups", "col")),
        P(None, "groups"),
    )
    return jax.shard_map(
        per_device,
        mesh=mesh,
        in_specs=placed,
        out_specs=P("row", ("groups", "col")),
        check_vma=False,
    )
```

```python
import functools

import jax
import jax.numpy as jnp
from jax import lax
from jax.experimental import pallas as pl
from jax.experimental.pallas import tpu as pltpu
from jax.sharding import PartitionSpec as P

BLK = 128
TILE = 896
PART = 448
LIMIT = 8 * 1024 * 1024
AXES = ("row", "col")
WEIGHTS = ((1, 1, 0.3, 0.3, 8, 0.02, 0.02), (1, 0.02, 0.3, 2, 4, 0.3, 4))

damping_ratio = 0.3
epsilon = 1e-06


def swap(value, axis, distance):
    return lax.ppermute(value, axis, [(i, i ^ distance) for i in range(lax.axis_size(axis))])


def sum_part(value, count):
    devices = 2 * count
    unit = 1
    while unit < devices:
        size = min(4, devices // unit)
        swaps = [[(i, i ^ k * unit) for i in range(devices)] for k in range(1, size)]
        value += sum(lax.ppermute(value, AXES, pairs) for pairs in swaps)
        unit *= size
    return value


def expand_local(block_mask, row_index, row_block, col_index, width_cols):
    if width_cols != BLK:
        row_ids = (row_index * row_block + jnp.arange(row_block, dtype=jnp.int32)) // BLK
        col_ids = (col_index * width_cols + jnp.arange(width_cols, dtype=jnp.int32)) // BLK
        return block_mask[row_ids][:, col_ids].astype(jnp.float32)
    piece = BLK
    while row_block % piece:
        piece //= 2
    column = lax.dynamic_index_in_dim(block_mask, col_index, 1, keepdims=False)
    column = jnp.repeat(column, BLK // piece) if piece != BLK else column
    count = row_block // piece
    own = lax.dynamic_slice_in_dim(column, row_index * count, count, 0).astype(jnp.float32)
    return jnp.broadcast_to(own[:, None, None], (count, piece, width_cols)).reshape(
        row_block, width_cols
    )


class Ring:
    def __init__(self, count):
        self.count = count
        self.order = list(range(0, count, 2)) + list(range(count - 1, 0, -2))
        self.last = count // 2 - 1

    def row(self, place):
        return self.order[place % self.count]

    def half(self, place):
        return self.row(place) * 2 // self.count

    def ahead(self, place):
        return int(place % self.count >= self.count // 2)

    def device(self, place, core):
        return self.row(place) * 2 + core

    def source(self, place, core, step):
        return place - 1 - step if core == self.ahead(place) else place + 1 + step

    def first_column(self, place, core, step):
        origin = self.ahead(self.source(place, core, step))
        return origin if core == self.ahead(place) else 1 - origin

    def places(self):
        return [(place, core) for place in range(self.count) for core in range(2)]

    def shift(self):
        pairs = []
        for place in range(self.count):
            pairs.append(
                (self.device(place, self.ahead(place)), self.device(place + 1, self.ahead(place + 1)))
            )
            pairs.append(
                (
                    self.device(place, 1 - self.ahead(place)),
                    self.device(place - 1, 1 - self.ahead(place - 1)),
                )
            )
        return pairs

    def hand_over(self, step):
        return [
            (self.device(place, core), self.device(place, 1 - core))
            for place, core in self.places()
            if self.half(self.source(place, core, step)) != core
        ]

    def slots(self):
        found = []
        for step in range(self.last):
            found.append((True, step))
            if self.hand_over(step):
                found.append((False, step))
        return found

    def loads(self, slot):
        base = 3 * (2 + len(self.slots()))
        return [base + slot + 1] if slot + 1 < self.count // 2 else []

    def entry(self, place, core, carrier, step):
        source = self.source(place, carrier, step)
        return [
            self.row(source) % (self.count // 2),
            int(self.half(source) == core),
            int(self.first_column(place, carrier, step) != core),
        ]

    def table(self):
        half = self.count // 2
        lines = [None] * (2 * self.count)
        for place, core in self.places():
            line = [self.row(place) % half, int(self.half(place) == core), 0]
            for carrier, step in self.slots():
                line += self.entry(place, core, core if carrier else 1 - core, step)
            line += self.entry(place, core, core, self.last)
            needed = [line[k] for k in range(0, len(line), 3) if line[k + 1]]
            line += needed
            lines[self.device(place, core)] = line
        return lines


def pick(ring, entry):
    device = lax.axis_index("row") * 2 + lax.axis_index("col")
    values = [line[entry] for line in ring.table()]
    picked = jnp.int32(values[0])
    for index, value in enumerate(values):
        if value != values[0]:
            picked = jnp.where(device == index, jnp.int32(value), picked)
    return picked


def block_copies(ring, load, gram, store, sems):
    rows = gram.shape[0]
    there = pl.ds(pl.multiple_of(pick(ring, load) * rows, BLK), rows)
    parts = [pl.ds(part * PART, PART) for part in range(rows // PART)]
    return [
        pltpu.make_async_copy(gram.at[here, there], store.at[here, there], sems.at[part])
        for part, here in enumerate(parts)
    ]


def load_kernel(ring, load, gram, acts, second, store, across, passed, sems):
    copies = block_copies(ring, load, gram, store, sems)
    for copy in copies:
        copy.start()
    across[...] = acts[...].astype(jnp.float32).T.astype(across.dtype)
    for copy in copies:
        copy.wait()


def load_first(ring, gram, acts, second):
    whole = pl.BlockSpec(memory_space=pltpu.VMEM)
    return pl.pallas_call(
        functools.partial(load_kernel, ring, ring.loads(-1)[0]),
        in_specs=[pl.BlockSpec(memory_space=pltpu.HBM), whole, whole],
        out_specs=[whole] * 3,
        out_shape=[
            jax.ShapeDtypeStruct(gram.shape, gram.dtype),
            jax.ShapeDtypeStruct(acts.shape[::-1], acts.dtype),
            jax.ShapeDtypeStruct(second.shape, second.dtype),
        ],
        scratch_shapes=[pltpu.SemaphoreType.DMA((gram.shape[0] // PART,))],
        input_output_aliases={2: 2},
        compiler_params=pltpu.CompilerParams(vmem_limit_bytes=LIMIT),
    )(gram, acts, second)


def product_kernel(ring, slot, loads, with_trace, first, second, across, *refs):
    copies = []
    if with_trace:
        acts, gram, _, own, other, store, trace, sems = refs
        trace[...] = jnp.zeros_like(trace)
    elif loads:
        gram, _, own, other, store, sems = refs[-6:]
    else:
        own, other, store = refs[-3:]
    if loads:
        copies = block_copies(ring, loads[0], gram, store, sems)
    for copy in copies:
        copy.start()
    rows, width = own.shape
    start = pl.multiple_of(pick(ring, 3 * slot) * rows, BLK)
    flip = pick(ring, 3 * slot + 2) == 1
    if slot == 0:
        own[...] = jnp.zeros_like(own)
        other[...] = jnp.zeros_like(other)

    @pl.when(pick(ring, 3 * slot + 1) == 1)
    def _():
        @pl.loop(0, rows // TILE)
        def _(tile):
            here = pl.ds(pl.multiple_of(tile * TILE, TILE), TILE)
            lines = jnp.concatenate([store[here, pl.ds(start, rows)], across[here, :]], axis=1)
            panel = jnp.concatenate([first[...], second[...]], axis=1)
            result = jnp.dot(lines, panel, preferred_element_type=jnp.float32)
            left, right = result[:, :width], result[:, width:]
            own[here, :] += jnp.where(flip, right, left)
            other[here, :] += jnp.where(flip, left, right)

        if with_trace:
            add_diagonal(store, start, acts, trace)

    for copy in copies:
        copy.wait()


def add_diagonal(store, start, acts, trace):
    lines = lax.broadcasted_iota(jnp.int32, (BLK, BLK), 0)
    same = lines == lax.broadcasted_iota(jnp.int32, (BLK, BLK), 1)
    for block in range(acts.shape[1] // BLK):
        here = slice(block * BLK, (block + 1) * BLK)
        there = pl.ds(pl.multiple_of(start + block * BLK, BLK), BLK)
        square = store[here, there].astype(jnp.float32)
        diag = jnp.sum(jnp.where(same, square, 0.0), axis=0, keepdims=True)
        part = acts[:, here].astype(jnp.float32)
        diag += jnp.sum(part * part, axis=0, keepdims=True)
        trace[0:1, :] += diag.astype(jnp.bfloat16).astype(jnp.float32)


def product(ring, slot, loads, gram, store, message, across, acts, acc):
    rows = across.shape[0]
    width = message[0].shape[1]
    weight = WEIGHTS[gram is None][slot]
    whole = pl.BlockSpec(memory_space=pltpu.VMEM)
    with_trace = bool(loads) and slot == 0
    operands = [*message, across]
    aliases = {len(operands) + k: k for k in range(len(acc))}
    operands += acc
    in_specs = [whole] * (len(operands) + 1)
    out_shape = [jax.ShapeDtypeStruct((rows, width), jnp.float32)] * 2
    out_shape.append(jax.ShapeDtypeStruct(store.shape, store.dtype))
    scratch = []
    if with_trace:
        operands.append(acts)
        in_specs.append(whole)
        out_shape.append(jax.ShapeDtypeStruct((8, width), jnp.float32))
    aliases[len(operands) + bool(loads)] = 2
    if loads:
        operands.append(gram)
        in_specs.insert(len(operands) - 1, pl.BlockSpec(memory_space=pltpu.HBM))
        scratch = [pltpu.SemaphoreType.DMA((rows // PART,))]
    operands.append(store)
    results = pl.pallas_call(
        functools.partial(product_kernel, ring, slot, loads, with_trace),
        in_specs=in_specs,
        out_specs=[whole] * len(out_shape),
        out_shape=out_shape,
        scratch_shapes=scratch,
        input_output_aliases=aliases,
        compiler_params=pltpu.CompilerParams(vmem_limit_bytes=LIMIT),
        cost_estimate=pl.CostEstimate(
            flops=int(weight * 4 * rows * rows * width),
            bytes_accessed=int(weight * 2 * rows * rows),
            transcendentals=0,
        ),
    )(*operands)
    return results[:2], results[2], results[3:]


def after(value, others):
    return lax.optimization_barrier((value, *others))[0]


def ring_apply(ring, gram, message, acts, early):
    first = message
    trace = []
    store, across, second = early(swap(message, "col", 1))
    ready = [(first, second)]
    acc = []
    slot = 0

    def work(others=()):
        nonlocal acc, store, slot, trace
        if not ready:
            return
        parts = ready.pop(0)
        parts = (after(parts[0], others), parts[1])
        loads = [] if gram is None else ring.loads(slot)
        acc, store, added = product(ring, slot, loads, gram, store, parts, across, acts, acc)
        trace = trace or added
        slot += 1

    def hand_over(step):
        if ring.hand_over(step):
            ready.append(tuple(swap(after(part, acc[:1]), "col", 1) for part in held))

    for step in range(ring.last):
        came = lax.ppermute(after(first, acc[:1]), AXES, ring.shift())
        if step:
            work([first])
        second = lax.ppermute(after(second, acc[:1]), AXES, ring.shift())
        if step:
            hand_over(step - 1)
            work()
        first = came
        held = (first, second)
        ready.append(held)
    first = lax.ppermute(after(first, acc[:1]), AXES, ring.shift())
    hand_over(ring.last - 1)
    while ready:
        work()
    last = (first, swap(after(first, acc[:1]), "col", 1))
    (own, other), store, _ = product(ring, slot, [], gram, store, last, across, acts, acc)
    return own, swap(other, "col", 1), store, trace


def put_message(message, acts, rows):
    message[rows:, :] = jnp.dot(
        acts[...], message[:rows, :], preferred_element_type=jnp.float32
    ).astype(message.dtype)


def head_kernel(weights, blocks, acts, message):
    rows = weights.shape[0]
    for block in range(rows // BLK):
        here = slice(block * BLK, (block + 1) * BLK)
        dense = weights[here, :]
        message[here, :] = (blocks[block : block + 1, :] * dense - dense).astype(message.dtype)
    put_message(message, acts, rows)


def turn_kernel(own, received, blocks, acts, _, grad, message, __):
    rows = own.shape[0]
    for block in range(rows // BLK):
        here = slice(block * BLK, (block + 1) * BLK)
        grad_first = own[here, :] + received[here, :]
        grad[here, :] = grad_first
        message[here, :] = (blocks[block : block + 1, :] * grad_first).astype(message.dtype)
    put_message(message, acts, rows)


def lane_sums(value):
    return jnp.sum(value, axis=0, keepdims=True)


def curve_kernel(trace, grad, own, received, blocks, curve_ref, sums_ref):
    rows = grad.shape[0]
    sums_ref[...] = jnp.zeros_like(sums_ref)
    sums_ref[0:1, :] = trace[0:1, :]
    for block in range(rows // BLK):
        here = slice(block * BLK, (block + 1) * BLK)
        kept = blocks[block : block + 1, :]
        curve = own[here, :] + received[here, :]
        curve_ref[here, :] = curve
        step_dir = kept * grad[here, :]
        masked = kept * curve
        sums_ref[1:2, :] += lane_sums(step_dir * step_dir)
        sums_ref[2:3, :] += lane_sums(step_dir * curve)
        sums_ref[3:4, :] += lane_sums(masked * masked)


def last_kernel(units, sums, grad, curve, weights, blocks, out_ref):
    totals = jnp.sum(sums[...], axis=1, keepdims=True)
    trace_total, grad_square = totals[0:1, :], totals[1:2, :]
    grad_curve, curve_square = totals[2:3, :], totals[3:4, :]
    damping = damping_ratio * trace_total / units
    step_first = grad_square / (grad_curve + damping * grad_square + epsilon)
    step_second = (grad_curve + damping * grad_square) / (
        curve_square + 2.0 * damping * grad_curve + damping * damping * grad_square + epsilon
    )
    rows = grad.shape[0]
    for block in range(rows // BLK):
        here = slice(block * BLK, (block + 1) * BLK)
        kept = blocks[block : block + 1, :]
        grad_first = grad[here, :]
        step_dir = kept * grad_first
        grad_second = grad_first - step_first * curve[here, :]
        out_ref[here, :] = (
            kept * weights[here, :] - step_first * step_dir - step_second * (kept * grad_second)
        )


def gather_apply(gram, activations, panel, col_index):
    half = gram.shape[1]
    full = lax.all_gather(panel, "row", axis=0, tiled=True)
    own_half = lax.dynamic_slice_in_dim(full, col_index * half, half, 0)
    need = lax.dynamic_slice_in_dim(full, (1 - col_index) * half, half, 0)
    other_half = swap(need, "col", 1)
    own = jnp.dot(gram, own_half, preferred_element_type=jnp.float32)
    partial = jnp.dot(gram, other_half, preferred_element_type=jnp.float32)
    low = lax.psum(jnp.dot(activations, panel, preferred_element_type=jnp.float32), "row")
    update = lax.dot_general(
        activations.astype(jnp.float32),
        low,
        (((0,), (0,)), ((), ())),
        precision=lax.Precision.HIGHEST,
        preferred_element_type=jnp.float32,
    )
    return own + swap(partial, "col", 1) + update


def per_device_general(gram_old, activations, weights, block_mask):
    row_block, half_width = gram_old.shape
    width_cols = weights.shape[1]
    units = lax.axis_size("row") * row_block
    row_index = lax.axis_index("row")
    col_index = lax.axis_index("col")
    mask_local = expand_local(block_mask, row_index, row_block, col_index, width_cols)
    kept_weights = mask_local * weights
    diff_low = (kept_weights - weights).astype(jnp.bfloat16)
    acts = activations.astype(jnp.float32)
    column_squares = jnp.sum(acts * acts, axis=0)
    grad_first = gather_apply(gram_old, activations, diff_low, col_index)
    place = row_index * row_block + jnp.arange(row_block, dtype=jnp.int32)
    place = place - col_index * half_width
    on_diagonal = jnp.arange(half_width, dtype=jnp.int32)[None, :] == place[:, None]
    new_gram = gram_old.astype(jnp.float32) + column_squares[:, None]
    new_gram = new_gram.astype(jnp.bfloat16).astype(jnp.float32)
    trace_part = jnp.sum(jnp.where(on_diagonal, new_gram, 0.0))
    step_dir = mask_local * grad_first
    curvature = gather_apply(gram_old, activations, step_dir.astype(jnp.bfloat16), col_index)
    masked_curve = mask_local * curvature
    sums = jnp.stack(
        [
            trace_part,
            jnp.sum(step_dir * step_dir),
            jnp.sum(step_dir * curvature),
            jnp.sum(masked_curve * masked_curve),
        ]
    )
    sums = lax.psum(sums, ("row", "col"))
    trace_total, grad_square, grad_curve, curve_square = sums[0], sums[1], sums[2], sums[3]
    damping = damping_ratio * trace_total / units
    step_first = grad_square / (grad_curve + damping * grad_square + epsilon)
    step_second = (grad_curve + damping * grad_square) / (
        curve_square + 2.0 * damping * grad_curve + damping * damping * grad_square + epsilon
    )
    grad_second = grad_first - step_first * curvature
    return kept_weights - step_first * step_dir - step_second * (mask_local * grad_second)


def call_whole(kernel, out_shape, *operands, alias={}):
    whole = pl.BlockSpec(memory_space=pltpu.VMEM)
    return pl.pallas_call(
        kernel,
        in_specs=[whole] * len(operands),
        out_specs=[whole] * len(out_shape),
        out_shape=out_shape,
        input_output_aliases=alias,
        compiler_params=pltpu.CompilerParams(vmem_limit_bytes=LIMIT),
    )(*operands)


def per_device(gram_old, activations, weights, block_mask):
    row_block, _ = gram_old.shape
    width = weights.shape[1]
    samples = activations.shape[0]
    count = lax.axis_size("row")
    if row_block % TILE or count not in (4, 8, 16) or width != BLK or samples % 16:
        return per_device_general(gram_old, activations, weights, block_mask)
    ring = Ring(count)
    row_index = lax.axis_index("row")
    col_index = lax.axis_index("col")
    per_block = row_block // BLK
    own_mask = lax.dynamic_slice(block_mask, (row_index * per_block, col_index), (per_block, 1))
    blocks = jnp.broadcast_to(own_mask.astype(jnp.float32), (per_block, width))
    panel = jax.ShapeDtypeStruct((row_block, width), jnp.float32)
    letter = jax.ShapeDtypeStruct((row_block + samples, width), jnp.bfloat16)
    eight = jax.ShapeDtypeStruct((8, width), jnp.float32)

    (message,) = call_whole(head_kernel, [letter], weights, blocks, activations)
    across = None

    def load(second):
        nonlocal across
        store, across, second = load_first(ring, gram_old, activations, second)
        return store, across, second

    own, received, store, (trace,) = ring_apply(ring, gram_old, message, activations, load)
    held = jax.ShapeDtypeStruct(store.shape, store.dtype)
    grad, message, store = call_whole(
        turn_kernel, [panel, letter, held], own, received, blocks, activations, store, alias={4: 2}
    )

    def keep(second):
        return store, across, second

    own, received, _, _ = ring_apply(ring, None, message, activations, keep)
    curve, sums = call_whole(curve_kernel, [panel, eight], trace, grad, own, received, blocks)
    sums = sum_part(sums, count)
    last = functools.partial(last_kernel, float(count * row_block))
    return call_whole(last, [panel], sums, grad, curve, weights, blocks)[0]


def solution(mesh):
    placed = (
        P(("groups", "row"), "col"),
        P("groups", "row"),
        P("row", ("groups", "col")),
        P(None, "groups"),
    )
    return jax.shard_map(
        per_device,
        mesh=mesh,
        in_specs=placed,
        out_specs=P("row", ("groups", "col")),
        check_vma=False,
    )
```

```python
import functools

import jax
import jax.numpy as jnp
from jax import lax
from jax.experimental import pallas as pl
from jax.experimental.pallas import tpu as pltpu
from jax.sharding import PartitionSpec as P

BLK = 128
TILES = 1
PARTS = 4
LIMIT = 8 * 1024 * 1024
AXES = ("row", "col")
WEIGHTS = ((1, 1, 0.3, 0.3, 8, 0.02, 0.02), (1, 0.02, 0.3, 2, 4, 0.3, 4))

damping_ratio = 0.3
epsilon = 1e-06


def swap(value, axis, distance):
    return lax.ppermute(value, axis, [(i, i ^ distance) for i in range(lax.axis_size(axis))])


def sum_part(value, count):
    devices = 2 * count
    unit = 1
    while unit < devices:
        size = 2 if unit == 1 else min(4, devices // unit)
        swaps = [[(i, i ^ k * unit) for i in range(devices)] for k in range(1, size)]
        value += sum(lax.ppermute(value, AXES, pairs) for pairs in swaps)
        unit *= size
    return value


def expand_local(block_mask, row_index, row_block, col_index, width_cols):
    if width_cols != BLK:
        row_ids = (row_index * row_block + jnp.arange(row_block, dtype=jnp.int32)) // BLK
        col_ids = (col_index * width_cols + jnp.arange(width_cols, dtype=jnp.int32)) // BLK
        return block_mask[row_ids][:, col_ids].astype(jnp.float32)
    piece = BLK
    while row_block % piece:
        piece //= 2
    column = lax.dynamic_index_in_dim(block_mask, col_index, 1, keepdims=False)
    column = jnp.repeat(column, BLK // piece) if piece != BLK else column
    count = row_block // piece
    own = lax.dynamic_slice_in_dim(column, row_index * count, count, 0).astype(jnp.float32)
    return jnp.broadcast_to(own[:, None, None], (count, piece, width_cols)).reshape(
        row_block, width_cols
    )


class Ring:
    def __init__(self, count):
        self.count = count
        self.order = list(range(0, count, 2)) + list(range(count - 1, 0, -2))
        self.last = count // 2 - 1

    def row(self, place):
        return self.order[place % self.count]

    def half(self, place):
        return self.row(place) * 2 // self.count

    def ahead(self, place):
        return int(place % self.count >= self.count // 2)

    def device(self, place, core):
        return self.row(place) * 2 + core

    def source(self, place, core, step):
        return place - 1 - step if core == self.ahead(place) else place + 1 + step

    def first_column(self, place, core, step):
        origin = self.ahead(self.source(place, core, step))
        return origin if core == self.ahead(place) else 1 - origin

    def places(self):
        return [(place, core) for place in range(self.count) for core in range(2)]

    def shift(self):
        pairs = []
        for place in range(self.count):
            pairs.append(
                (self.device(place, self.ahead(place)), self.device(place + 1, self.ahead(place + 1)))
            )
            pairs.append(
                (
                    self.device(place, 1 - self.ahead(place)),
                    self.device(place - 1, 1 - self.ahead(place - 1)),
                )
            )
        return pairs

    def hand_over(self, step):
        return [
            (self.device(place, core), self.device(place, 1 - core))
            for place, core in self.places()
            if self.half(self.source(place, core, step)) != core
        ]

    def slots(self):
        found = []
        for step in range(self.last):
            found.append((True, step))
            if self.hand_over(step):
                found.append((False, step))
        return found

    def loads(self, slot):
        base = 3 * (2 + len(self.slots()))
        return [base + slot + 1] if slot + 1 < self.count // 2 else []

    def entry(self, place, core, carrier, step):
        source = self.source(place, carrier, step)
        return [
            self.row(source) % (self.count // 2),
            int(self.half(source) == core),
            int(self.first_column(place, carrier, step) != core),
        ]

    def table(self):
        half = self.count // 2
        lines = [None] * (2 * self.count)
        for place, core in self.places():
            line = [self.row(place) % half, int(self.half(place) == core), 0]
            for carrier, step in self.slots():
                line += self.entry(place, core, core if carrier else 1 - core, step)
            line += self.entry(place, core, core, self.last)
            needed = [line[k] for k in range(0, len(line), 3) if line[k + 1]]
            line += needed
            lines[self.device(place, core)] = line
        return lines


def pick(ring, entry):
    device = lax.axis_index("row") * 2 + lax.axis_index("col")
    values = [line[entry] for line in ring.table()]
    picked = jnp.int32(values[0])
    for index, value in enumerate(values):
        if value != values[0]:
            picked = jnp.where(device == index, jnp.int32(value), picked)
    return picked


def block_copies(ring, load, gram, store, sems):
    rows = gram.shape[0]
    there = pl.ds(pl.multiple_of(pick(ring, load) * rows, BLK), rows)
    parts = [pl.ds(part * rows // PARTS, rows // PARTS) for part in range(PARTS)]
    return [
        pltpu.make_async_copy(gram.at[here, there], store.at[here, there], sems.at[part])
        for part, here in enumerate(parts)
    ]


def load_kernel(ring, load, gram, acts, second, store, across, passed, sems):
    copies = block_copies(ring, load, gram, store, sems)
    for copy in copies:
        copy.start()
    across[...] = acts[...].astype(jnp.float32).T.astype(across.dtype)
    for copy in copies:
        copy.wait()


def load_first(ring, gram, acts, second):
    whole = pl.BlockSpec(memory_space=pltpu.VMEM)
    return pl.pallas_call(
        functools.partial(load_kernel, ring, ring.loads(-1)[0]),
        in_specs=[pl.BlockSpec(memory_space=pltpu.HBM), whole, whole],
        out_specs=[whole] * 3,
        out_shape=[
            jax.ShapeDtypeStruct(gram.shape, gram.dtype),
            jax.ShapeDtypeStruct(acts.shape[::-1], acts.dtype),
            jax.ShapeDtypeStruct(second.shape, second.dtype),
        ],
        scratch_shapes=[pltpu.SemaphoreType.DMA((PARTS,))],
        input_output_aliases={2: 2},
        compiler_params=pltpu.CompilerParams(vmem_limit_bytes=LIMIT),
    )(gram, acts, second)


def product_kernel(ring, slot, loads, with_trace, first, second, across, *refs):
    copies = []
    if with_trace:
        acts, gram, _, own, other, store, trace, sems = refs
        trace[...] = jnp.zeros_like(trace)
    elif loads:
        gram, _, own, other, store, sems = refs[-6:]
    else:
        own, other, store = refs[-3:]
    if loads:
        copies = block_copies(ring, loads[0], gram, store, sems)
    for copy in copies:
        copy.start()
    rows, width = own.shape
    start = pl.multiple_of(pick(ring, 3 * slot) * rows, BLK)
    flip = pick(ring, 3 * slot + 2) == 1
    if slot == 0:
        own[...] = jnp.zeros_like(own)
        other[...] = jnp.zeros_like(other)

    @pl.when(pick(ring, 3 * slot + 1) == 1)
    def _():
        @pl.loop(0, TILES)
        def _(tile):
            size = rows // TILES
            here = pl.ds(pl.multiple_of(tile * size, size), size)
            lines = jnp.concatenate([store[here, pl.ds(start, rows)], across[here, :]], axis=1)
            panel = jnp.concatenate([first[...], second[...]], axis=1)
            result = jnp.dot(lines, panel, preferred_element_type=jnp.float32)
            left, right = result[:, :width], result[:, width:]
            own[here, :] += jnp.where(flip, right, left)
            other[here, :] += jnp.where(flip, left, right)

        if with_trace:
            add_diagonal(store, start, acts, trace)

    for copy in copies:
        copy.wait()


def add_diagonal(store, start, acts, trace):
    lines = lax.broadcasted_iota(jnp.int32, (BLK, BLK), 0)
    same = lines == lax.broadcasted_iota(jnp.int32, (BLK, BLK), 1)
    for block in range(acts.shape[1] // BLK):
        here = slice(block * BLK, (block + 1) * BLK)
        there = pl.ds(pl.multiple_of(start + block * BLK, BLK), BLK)
        square = store[here, there].astype(jnp.float32)
        diag = jnp.sum(jnp.where(same, square, 0.0), axis=0, keepdims=True)
        part = acts[:, here].astype(jnp.float32)
        diag += jnp.sum(part * part, axis=0, keepdims=True)
        trace[0:1, :] += diag.astype(jnp.bfloat16).astype(jnp.float32)


def product(ring, slot, loads, gram, store, message, across, acts, acc):
    rows = across.shape[0]
    width = message[0].shape[1]
    weight = WEIGHTS[gram is None][slot]
    whole = pl.BlockSpec(memory_space=pltpu.VMEM)
    with_trace = bool(loads) and slot == 0
    operands = [*message, across]
    aliases = {len(operands) + k: k for k in range(len(acc))}
    operands += acc
    in_specs = [whole] * (len(operands) + 1)
    out_shape = [jax.ShapeDtypeStruct((rows, width), jnp.float32)] * 2
    out_shape.append(jax.ShapeDtypeStruct(store.shape, store.dtype))
    scratch = []
    if with_trace:
        operands.append(acts)
        in_specs.append(whole)
        out_shape.append(jax.ShapeDtypeStruct((8, width), jnp.float32))
    aliases[len(operands) + bool(loads)] = 2
    if loads:
        operands.append(gram)
        in_specs.insert(len(operands) - 1, pl.BlockSpec(memory_space=pltpu.HBM))
        scratch = [pltpu.SemaphoreType.DMA((PARTS,))]
    operands.append(store)
    results = pl.pallas_call(
        functools.partial(product_kernel, ring, slot, loads, with_trace),
        in_specs=in_specs,
        out_specs=[whole] * len(out_shape),
        out_shape=out_shape,
        scratch_shapes=scratch,
        input_output_aliases=aliases,
        compiler_params=pltpu.CompilerParams(vmem_limit_bytes=LIMIT),
        cost_estimate=pl.CostEstimate(
            flops=int(weight * 4 * rows * rows * width),
            bytes_accessed=int(weight * 2 * rows * rows),
            transcendentals=0,
        ),
    )(*operands)
    return results[:2], results[2], results[3:]


def after(value, others):
    return lax.optimization_barrier((value, *others))[0]


def ring_apply(ring, gram, message, acts, early):
    first = message
    trace = []
    store, across, second = early(swap(message, "col", 1))
    ready = [(first, second)]
    acc = []
    slot = 0

    def work(others=()):
        nonlocal acc, store, slot, trace
        if not ready:
            return
        parts = ready.pop(0)
        parts = (after(parts[0], others), parts[1])
        loads = [] if gram is None else ring.loads(slot)
        acc, store, added = product(ring, slot, loads, gram, store, parts, across, acts, acc)
        trace = trace or added
        slot += 1

    def hand_over(step):
        if ring.hand_over(step):
            ready.append(tuple(swap(after(part, acc[:1]), "col", 1) for part in held))

    for step in range(ring.last):
        came = lax.ppermute(after(first, acc[:1]), AXES, ring.shift())
        if step:
            work([first])
        second = lax.ppermute(after(second, acc[:1]), AXES, ring.shift())
        if step:
            hand_over(step - 1)
            work()
        first = came
        held = (first, second)
        ready.append(held)
    first = lax.ppermute(after(first, acc[:1]), AXES, ring.shift())
    hand_over(ring.last - 1)
    while ready:
        work()
    last = (first, swap(after(first, acc[:1]), "col", 1))
    (own, other), store, _ = product(ring, slot, [], gram, store, last, across, acts, acc)
    return own, swap(other, "col", 1), store, trace


def put_message(message, acts, rows):
    message[rows:, :] = jnp.dot(
        acts[...], message[:rows, :], preferred_element_type=jnp.float32
    ).astype(message.dtype)


def head_kernel(weights, blocks, acts, message):
    rows = weights.shape[0]
    for block in range(rows // BLK):
        here = slice(block * BLK, (block + 1) * BLK)
        dense = weights[here, :]
        message[here, :] = (blocks[block : block + 1, :] * dense - dense).astype(message.dtype)
    put_message(message, acts, rows)


def turn_kernel(own, received, blocks, acts, _, grad, message, __):
    rows = own.shape[0]
    for block in range(rows // BLK):
        here = slice(block * BLK, (block + 1) * BLK)
        grad_first = own[here, :] + received[here, :]
        grad[here, :] = grad_first
        message[here, :] = (blocks[block : block + 1, :] * grad_first).astype(message.dtype)
    put_message(message, acts, rows)


def lane_sums(value):
    return jnp.sum(value, axis=0, keepdims=True)


def curve_kernel(trace, grad, own, received, blocks, curve_ref, sums_ref):
    rows = grad.shape[0]
    sums_ref[...] = jnp.zeros_like(sums_ref)
    sums_ref[0:1, :] = trace[0:1, :]
    for block in range(rows // BLK):
        here = slice(block * BLK, (block + 1) * BLK)
        kept = blocks[block : block + 1, :]
        curve = own[here, :] + received[here, :]
        curve_ref[here, :] = curve
        step_dir = kept * grad[here, :]
        masked = kept * curve
        sums_ref[1:2, :] += lane_sums(step_dir * step_dir)
        sums_ref[2:3, :] += lane_sums(step_dir * curve)
        sums_ref[3:4, :] += lane_sums(masked * masked)


def last_kernel(units, sums, grad, curve, weights, blocks, out_ref):
    totals = jnp.sum(sums[...], axis=1, keepdims=True)
    trace_total, grad_square = totals[0:1, :], totals[1:2, :]
    grad_curve, curve_square = totals[2:3, :], totals[3:4, :]
    damping = damping_ratio * trace_total / units
    step_first = grad_square / (grad_curve + damping * grad_square + epsilon)
    step_second = (grad_curve + damping * grad_square) / (
        curve_square + 2.0 * damping * grad_curve + damping * damping * grad_square + epsilon
    )
    rows = grad.shape[0]
    for block in range(rows // BLK):
        here = slice(block * BLK, (block + 1) * BLK)
        kept = blocks[block : block + 1, :]
        grad_first = grad[here, :]
        step_dir = kept * grad_first
        grad_second = grad_first - step_first * curve[here, :]
        out_ref[here, :] = (
            kept * weights[here, :] - step_first * step_dir - step_second * (kept * grad_second)
        )


def gather_apply(gram, activations, panel, col_index):
    half = gram.shape[1]
    full = lax.all_gather(panel, "row", axis=0, tiled=True)
    own_half = lax.dynamic_slice_in_dim(full, col_index * half, half, 0)
    need = lax.dynamic_slice_in_dim(full, (1 - col_index) * half, half, 0)
    other_half = swap(need, "col", 1)
    own = jnp.dot(gram, own_half, preferred_element_type=jnp.float32)
    partial = jnp.dot(gram, other_half, preferred_element_type=jnp.float32)
    low = lax.psum(jnp.dot(activations, panel, preferred_element_type=jnp.float32), "row")
    update = lax.dot_general(
        activations.astype(jnp.float32),
        low,
        (((0,), (0,)), ((), ())),
        precision=lax.Precision.HIGHEST,
        preferred_element_type=jnp.float32,
    )
    return own + swap(partial, "col", 1) + update


def per_device_general(gram_old, activations, weights, block_mask):
    row_block, half_width = gram_old.shape
    width_cols = weights.shape[1]
    units = lax.axis_size("row") * row_block
    row_index = lax.axis_index("row")
    col_index = lax.axis_index("col")
    mask_local = expand_local(block_mask, row_index, row_block, col_index, width_cols)
    kept_weights = mask_local * weights
    diff_low = (kept_weights - weights).astype(jnp.bfloat16)
    acts = activations.astype(jnp.float32)
    column_squares = jnp.sum(acts * acts, axis=0)
    grad_first = gather_apply(gram_old, activations, diff_low, col_index)
    place = row_index * row_block + jnp.arange(row_block, dtype=jnp.int32)
    place = place - col_index * half_width
    on_diagonal = jnp.arange(half_width, dtype=jnp.int32)[None, :] == place[:, None]
    new_gram = gram_old.astype(jnp.float32) + column_squares[:, None]
    new_gram = new_gram.astype(jnp.bfloat16).astype(jnp.float32)
    trace_part = jnp.sum(jnp.where(on_diagonal, new_gram, 0.0))
    step_dir = mask_local * grad_first
    curvature = gather_apply(gram_old, activations, step_dir.astype(jnp.bfloat16), col_index)
    masked_curve = mask_local * curvature
    sums = jnp.stack(
        [
            trace_part,
            jnp.sum(step_dir * step_dir),
            jnp.sum(step_dir * curvature),
            jnp.sum(masked_curve * masked_curve),
        ]
    )
    sums = lax.psum(sums, ("row", "col"))
    trace_total, grad_square, grad_curve, curve_square = sums[0], sums[1], sums[2], sums[3]
    damping = damping_ratio * trace_total / units
    step_first = grad_square / (grad_curve + damping * grad_square + epsilon)
    step_second = (grad_curve + damping * grad_square) / (
        curve_square + 2.0 * damping * grad_curve + damping * damping * grad_square + epsilon
    )
    grad_second = grad_first - step_first * curvature
    return kept_weights - step_first * step_dir - step_second * (mask_local * grad_second)


def call_whole(kernel, out_shape, *operands, alias={}):
    whole = pl.BlockSpec(memory_space=pltpu.VMEM)
    return pl.pallas_call(
        kernel,
        in_specs=[whole] * len(operands),
        out_specs=[whole] * len(out_shape),
        out_shape=out_shape,
        input_output_aliases=alias,
        compiler_params=pltpu.CompilerParams(vmem_limit_bytes=LIMIT),
    )(*operands)


def per_device(gram_old, activations, weights, block_mask):
    row_block, _ = gram_old.shape
    width = weights.shape[1]
    samples = activations.shape[0]
    count = lax.axis_size("row")
    if row_block % (BLK * TILES) or row_block % (16 * PARTS) or count not in (4, 8, 16) or width != BLK or samples % 16:
        return per_device_general(gram_old, activations, weights, block_mask)
    ring = Ring(count)
    row_index = lax.axis_index("row")
    col_index = lax.axis_index("col")
    per_block = row_block // BLK
    own_mask = lax.dynamic_slice(block_mask, (row_index * per_block, col_index), (per_block, 1))
    blocks = jnp.broadcast_to(own_mask.astype(jnp.float32), (per_block, width))
    panel = jax.ShapeDtypeStruct((row_block, width), jnp.float32)
    letter = jax.ShapeDtypeStruct((row_block + samples, width), jnp.bfloat16)
    eight = jax.ShapeDtypeStruct((8, width), jnp.float32)

    (message,) = call_whole(head_kernel, [letter], weights, blocks, activations)
    across = None

    def load(second):
        nonlocal across
        store, across, second = load_first(ring, gram_old, activations, second)
        return store, across, second

    own, received, store, (trace,) = ring_apply(ring, gram_old, message, activations, load)
    held = jax.ShapeDtypeStruct(store.shape, store.dtype)
    grad, message, store = call_whole(
        turn_kernel, [panel, letter, held], own, received, blocks, activations, store, alias={4: 2}
    )

    def keep(second):
        return store, across, second

    own, received, _, _ = ring_apply(ring, None, message, activations, keep)
    curve, sums = call_whole(curve_kernel, [panel, eight], trace, grad, own, received, blocks)
    sums = sum_part(sums, count)
    last = functools.partial(last_kernel, float(count * row_block))
    return call_whole(last, [panel], sums, grad, curve, weights, blocks)[0]


def solution(mesh):
    placed = (
        P(("groups", "row"), "col"),
        P("groups", "row"),
        P("row", ("groups", "col")),
        P(None, "groups"),
    )
    return jax.shard_map(
        per_device,
        mesh=mesh,
        in_specs=placed,
        out_specs=P("row", ("groups", "col")),
        check_vma=False,
    )
```

```python
import functools

import jax
import jax.numpy as jnp
from jax import lax
from jax.experimental import pallas as pl
from jax.experimental.pallas import tpu as pltpu
from jax.sharding import PartitionSpec as P

BLK = 128
TILES = 1
PARTS = 4
LIMIT = 8 * 1024 * 1024
AXES = ("row", "col")
WEIGHTS = ((1, 1, 0.3, 0.3, 8, 0.02, 0.02, 0.02), (1, 1, 0.3, 0.3, 8, 0.02, 0.02, 0.02))

damping_ratio = 0.3
epsilon = 1e-06


def swap(value, axis, distance):
    return lax.ppermute(value, axis, [(i, i ^ distance) for i in range(lax.axis_size(axis))])


def sum_part(value, count):
    devices = 2 * count
    unit = 1
    while unit < devices:
        size = 2 if unit == 1 else min(4, devices // unit)
        swaps = [[(i, i ^ k * unit) for i in range(devices)] for k in range(1, size)]
        value += sum(lax.ppermute(value, AXES, pairs) for pairs in swaps)
        unit *= size
    return value


def expand_local(block_mask, row_index, row_block, col_index, width_cols):
    if width_cols != BLK:
        row_ids = (row_index * row_block + jnp.arange(row_block, dtype=jnp.int32)) // BLK
        col_ids = (col_index * width_cols + jnp.arange(width_cols, dtype=jnp.int32)) // BLK
        return block_mask[row_ids][:, col_ids].astype(jnp.float32)
    piece = BLK
    while row_block % piece:
        piece //= 2
    column = lax.dynamic_index_in_dim(block_mask, col_index, 1, keepdims=False)
    column = jnp.repeat(column, BLK // piece) if piece != BLK else column
    count = row_block // piece
    own = lax.dynamic_slice_in_dim(column, row_index * count, count, 0).astype(jnp.float32)
    return jnp.broadcast_to(own[:, None, None], (count, piece, width_cols)).reshape(
        row_block, width_cols
    )


class Ring:
    def __init__(self, count):
        self.count = count
        self.order = list(range(0, count, 2)) + list(range(count - 1, 0, -2))
        self.last = count // 2 - 1

    def row(self, place):
        return self.order[place % self.count]

    def half(self, place):
        return self.row(place) * 2 // self.count

    def ahead(self, place):
        return int(place % self.count >= self.count // 2)

    def device(self, place, core):
        return self.row(place) * 2 + core

    def source(self, place, core, step):
        return place - 1 - step if core == self.ahead(place) else place + 1 + step

    def first_column(self, place, core, step):
        origin = self.ahead(self.source(place, core, step))
        return origin if core == self.ahead(place) else 1 - origin

    def places(self):
        return [(place, core) for place in range(self.count) for core in range(2)]

    def shift(self):
        pairs = []
        for place in range(self.count):
            pairs.append(
                (self.device(place, self.ahead(place)), self.device(place + 1, self.ahead(place + 1)))
            )
            pairs.append(
                (
                    self.device(place, 1 - self.ahead(place)),
                    self.device(place - 1, 1 - self.ahead(place - 1)),
                )
            )
        return pairs

    def hand_over(self, step):
        return [
            (self.device(place, core), self.device(place, 1 - core))
            for place, core in self.places()
            if self.half(self.source(place, core, step)) != core
        ]

    def slots(self):
        found = []
        for step in range(self.last):
            found.append((True, step))
            if self.hand_over(step):
                found.append((False, step))
        return found

    def loads(self, slot):
        base = 3 * (2 + len(self.slots()))
        return [base + slot + 1] if slot + 1 < self.count // 2 else []

    def entry(self, place, core, carrier, step):
        source = self.source(place, carrier, step)
        return [
            self.row(source) % (self.count // 2),
            int(self.half(source) == core),
            int(self.first_column(place, carrier, step) != core),
        ]

    def table(self):
        half = self.count // 2
        lines = [None] * (2 * self.count)
        for place, core in self.places():
            line = [self.row(place) % half, int(self.half(place) == core), 0]
            for carrier, step in self.slots():
                line += self.entry(place, core, core if carrier else 1 - core, step)
            line += self.entry(place, core, core, self.last)
            needed = [line[k] for k in range(0, len(line), 3) if line[k + 1]]
            line += needed
            lines[self.device(place, core)] = line
        return lines


def pick(ring, entry):
    device = lax.axis_index("row") * 2 + lax.axis_index("col")
    values = [line[entry] for line in ring.table()]
    picked = jnp.int32(values[0])
    for index, value in enumerate(values):
        if value != values[0]:
            picked = jnp.where(device == index, jnp.int32(value), picked)
    return picked


def block_copies(ring, load, gram, store, sems):
    rows = gram.shape[0]
    there = pl.ds(pl.multiple_of(pick(ring, load) * rows, BLK), rows)
    parts = [pl.ds(part * rows // PARTS, rows // PARTS) for part in range(PARTS)]
    return [
        pltpu.make_async_copy(gram.at[here, there], store.at[here, there], sems.at[part])
        for part, here in enumerate(parts)
    ]


def load_kernel(ring, load, gram, acts, second, store, across, passed, sems):
    copies = block_copies(ring, load, gram, store, sems)
    for copy in copies:
        copy.start()
    across[...] = acts[...].astype(jnp.float32).T.astype(across.dtype)
    for copy in copies:
        copy.wait()


def load_first(ring, gram, acts, second):
    whole = pl.BlockSpec(memory_space=pltpu.VMEM)
    return pl.pallas_call(
        functools.partial(load_kernel, ring, ring.loads(-1)[0]),
        in_specs=[pl.BlockSpec(memory_space=pltpu.HBM), whole, whole],
        out_specs=[whole] * 3,
        out_shape=[
            jax.ShapeDtypeStruct(gram.shape, gram.dtype),
            jax.ShapeDtypeStruct(acts.shape[::-1], acts.dtype),
            jax.ShapeDtypeStruct(second.shape, second.dtype),
        ],
        scratch_shapes=[pltpu.SemaphoreType.DMA((PARTS,))],
        input_output_aliases={2: 2},
        compiler_params=pltpu.CompilerParams(vmem_limit_bytes=LIMIT),
    )(gram, acts, second)


def product_kernel(ring, slot, loads, with_trace, begin, first, second, across, *refs):
    copies = []
    if with_trace:
        acts, gram, _, own, other, store, trace, sems = refs
        trace[...] = jnp.zeros_like(trace)
    elif loads:
        gram, _, own, other, store, sems = refs[-6:]
    else:
        own, other, store = refs[-3:]
    if loads:
        copies = block_copies(ring, loads[0], gram, store, sems)
    for copy in copies:
        copy.start()
    rows, width = own.shape
    start = pl.multiple_of(pick(ring, 3 * slot) * rows, BLK)
    flip = pick(ring, 3 * slot + 2) == 1
    if slot == 0:
        own[...] = jnp.zeros_like(own)
        other[...] = jnp.zeros_like(other)

    @pl.when(pick(ring, 3 * slot + 1) == 1)
    def _():
        @pl.loop(0, TILES)
        def _(tile):
            size = rows // TILES
            here = pl.ds(pl.multiple_of(tile * size, size), size)
            depth = min(first.shape[0], rows - begin)
            lines = store[here, pl.ds(start + begin, depth)]
            if depth < first.shape[0]:
                lines = jnp.concatenate([lines, across[here, :]], axis=1)
            panel = jnp.concatenate([first[...], second[...]], axis=1)
            result = jnp.dot(lines, panel, preferred_element_type=jnp.float32)
            left, right = result[:, :width], result[:, width:]
            own[here, :] += jnp.where(flip, right, left)
            other[here, :] += jnp.where(flip, left, right)

        if with_trace:
            add_diagonal(store, start, acts, trace)

    for copy in copies:
        copy.wait()


def add_diagonal(store, start, acts, trace):
    lines = lax.broadcasted_iota(jnp.int32, (BLK, BLK), 0)
    same = lines == lax.broadcasted_iota(jnp.int32, (BLK, BLK), 1)
    for block in range(acts.shape[1] // BLK):
        here = slice(block * BLK, (block + 1) * BLK)
        there = pl.ds(pl.multiple_of(start + block * BLK, BLK), BLK)
        square = store[here, there].astype(jnp.float32)
        diag = jnp.sum(jnp.where(same, square, 0.0), axis=0, keepdims=True)
        part = acts[:, here].astype(jnp.float32)
        diag += jnp.sum(part * part, axis=0, keepdims=True)
        trace[0:1, :] += diag.astype(jnp.bfloat16).astype(jnp.float32)


def product(ring, slot, loads, gram, store, message, across, acts, acc, begin=0):
    rows = across.shape[0]
    width = message[0].shape[1]
    weight = WEIGHTS[gram is None][slot + (begin > 0)]
    whole = pl.BlockSpec(memory_space=pltpu.VMEM)
    with_trace = bool(loads) and slot == 0
    operands = [*message, across]
    aliases = {len(operands) + k: k for k in range(len(acc))}
    operands += acc
    in_specs = [whole] * (len(operands) + 1)
    out_shape = [jax.ShapeDtypeStruct((rows, width), jnp.float32)] * 2
    out_shape.append(jax.ShapeDtypeStruct(store.shape, store.dtype))
    scratch = []
    if with_trace:
        operands.append(acts)
        in_specs.append(whole)
        out_shape.append(jax.ShapeDtypeStruct((8, width), jnp.float32))
    aliases[len(operands) + bool(loads)] = 2
    if loads:
        operands.append(gram)
        in_specs.insert(len(operands) - 1, pl.BlockSpec(memory_space=pltpu.HBM))
        scratch = [pltpu.SemaphoreType.DMA((PARTS,))]
    operands.append(store)
    results = pl.pallas_call(
        functools.partial(product_kernel, ring, slot, loads, with_trace, begin),
        in_specs=in_specs,
        out_specs=[whole] * len(out_shape),
        out_shape=out_shape,
        scratch_shapes=scratch,
        input_output_aliases=aliases,
        compiler_params=pltpu.CompilerParams(vmem_limit_bytes=LIMIT),
        cost_estimate=pl.CostEstimate(
            flops=int(weight * 4 * rows * rows * width),
            bytes_accessed=int(weight * 2 * rows * rows),
            transcendentals=0,
        ),
    )(*operands)
    return results[:2], results[2], results[3:]


def after(value, others):
    return lax.optimization_barrier((value, *others))[0]


def ring_apply(ring, gram, message, acts, early):
    first = message
    trace = []
    store, across, second = early(swap(message, "col", 1))
    ready = [(first, second)]
    acc = []
    slot = 0

    def work(others=()):
        nonlocal acc, store, slot, trace
        if not ready:
            return
        parts = ready.pop(0)
        parts = (after(parts[0], others), parts[1])
        loads = [] if gram is None else ring.loads(slot)
        acc, store, added = product(ring, slot, loads, gram, store, parts, across, acts, acc)
        trace = trace or added
        slot += 1

    def hand_over(step):
        if ring.hand_over(step):
            ready.append(tuple(swap(after(part, acc[:1]), "col", 1) for part in held))

    for step in range(ring.last):
        came = lax.ppermute(after(first, acc[:1]), AXES, ring.shift())
        if step:
            work([first])
        second = lax.ppermute(after(second, acc[:1]), AXES, ring.shift())
        if step:
            hand_over(step - 1)
            work()
        first = came
        held = (first, second)
        ready.append(held)
    middle = store.shape[0] // 2
    came = [
        lax.ppermute(after(part, acc[:1]), AXES, ring.shift())
        for part in (first[:middle], first[middle:])
    ]
    hand_over(ring.last - 1)
    while ready:
        work()
    for begin, part in zip((0, middle), came):
        parts = (part, swap(after(part, acc[:1]), "col", 1))
        acc, store, _ = product(ring, slot, [], gram, store, parts, across, acts, acc, begin)
    own, other = acc
    return own, swap(other, "col", 1), store, trace


def put_message(message, acts, rows):
    message[rows:, :] = jnp.dot(
        acts[...], message[:rows, :], preferred_element_type=jnp.float32
    ).astype(message.dtype)


def head_kernel(weights, blocks, acts, message):
    rows = weights.shape[0]
    for block in range(rows // BLK):
        here = slice(block * BLK, (block + 1) * BLK)
        dense = weights[here, :]
        message[here, :] = (blocks[block : block + 1, :] * dense - dense).astype(message.dtype)
    put_message(message, acts, rows)


def turn_kernel(own, received, blocks, acts, _, grad, message, __):
    rows = own.shape[0]
    for block in range(rows // BLK):
        here = slice(block * BLK, (block + 1) * BLK)
        grad_first = own[here, :] + received[here, :]
        grad[here, :] = grad_first
        message[here, :] = (blocks[block : block + 1, :] * grad_first).astype(message.dtype)
    put_message(message, acts, rows)


def lane_sums(value):
    return jnp.sum(value, axis=0, keepdims=True)


def curve_kernel(trace, grad, own, received, blocks, curve_ref, sums_ref):
    rows = grad.shape[0]
    sums_ref[...] = jnp.zeros_like(sums_ref)
    sums_ref[0:1, :] = trace[0:1, :]
    for block in range(rows // BLK):
        here = slice(block * BLK, (block + 1) * BLK)
        kept = blocks[block : block + 1, :]
        curve = own[here, :] + received[here, :]
        curve_ref[here, :] = curve
        step_dir = kept * grad[here, :]
        masked = kept * curve
        sums_ref[1:2, :] += lane_sums(step_dir * step_dir)
        sums_ref[2:3, :] += lane_sums(step_dir * curve)
        sums_ref[3:4, :] += lane_sums(masked * masked)


def last_kernel(units, sums, grad, curve, weights, blocks, out_ref):
    totals = jnp.sum(sums[...], axis=1, keepdims=True)
    trace_total, grad_square = totals[0:1, :], totals[1:2, :]
    grad_curve, curve_square = totals[2:3, :], totals[3:4, :]
    damping = damping_ratio * trace_total / units
    step_first = grad_square / (grad_curve + damping * grad_square + epsilon)
    step_second = (grad_curve + damping * grad_square) / (
        curve_square + 2.0 * damping * grad_curve + damping * damping * grad_square + epsilon
    )
    rows = grad.shape[0]
    for block in range(rows // BLK):
        here = slice(block * BLK, (block + 1) * BLK)
        kept = blocks[block : block + 1, :]
        grad_first = grad[here, :]
        step_dir = kept * grad_first
        grad_second = grad_first - step_first * curve[here, :]
        out_ref[here, :] = (
            kept * weights[here, :] - step_first * step_dir - step_second * (kept * grad_second)
        )


def gather_apply(gram, activations, panel, col_index):
    half = gram.shape[1]
    full = lax.all_gather(panel, "row", axis=0, tiled=True)
    own_half = lax.dynamic_slice_in_dim(full, col_index * half, half, 0)
    need = lax.dynamic_slice_in_dim(full, (1 - col_index) * half, half, 0)
    other_half = swap(need, "col", 1)
    own = jnp.dot(gram, own_half, preferred_element_type=jnp.float32)
    partial = jnp.dot(gram, other_half, preferred_element_type=jnp.float32)
    low = lax.psum(jnp.dot(activations, panel, preferred_element_type=jnp.float32), "row")
    update = lax.dot_general(
        activations.astype(jnp.float32),
        low,
        (((0,), (0,)), ((), ())),
        precision=lax.Precision.HIGHEST,
        preferred_element_type=jnp.float32,
    )
    return own + swap(partial, "col", 1) + update


def per_device_general(gram_old, activations, weights, block_mask):
    row_block, half_width = gram_old.shape
    width_cols = weights.shape[1]
    units = lax.axis_size("row") * row_block
    row_index = lax.axis_index("row")
    col_index = lax.axis_index("col")
    mask_local = expand_local(block_mask, row_index, row_block, col_index, width_cols)
    kept_weights = mask_local * weights
    diff_low = (kept_weights - weights).astype(jnp.bfloat16)
    acts = activations.astype(jnp.float32)
    column_squares = jnp.sum(acts * acts, axis=0)
    grad_first = gather_apply(gram_old, activations, diff_low, col_index)
    place = row_index * row_block + jnp.arange(row_block, dtype=jnp.int32)
    place = place - col_index * half_width
    on_diagonal = jnp.arange(half_width, dtype=jnp.int32)[None, :] == place[:, None]
    new_gram = gram_old.astype(jnp.float32) + column_squares[:, None]
    new_gram = new_gram.astype(jnp.bfloat16).astype(jnp.float32)
    trace_part = jnp.sum(jnp.where(on_diagonal, new_gram, 0.0))
    step_dir = mask_local * grad_first
    curvature = gather_apply(gram_old, activations, step_dir.astype(jnp.bfloat16), col_index)
    masked_curve = mask_local * curvature
    sums = jnp.stack(
        [
            trace_part,
            jnp.sum(step_dir * step_dir),
            jnp.sum(step_dir * curvature),
            jnp.sum(masked_curve * masked_curve),
        ]
    )
    sums = lax.psum(sums, ("row", "col"))
    trace_total, grad_square, grad_curve, curve_square = sums[0], sums[1], sums[2], sums[3]
    damping = damping_ratio * trace_total / units
    step_first = grad_square / (grad_curve + damping * grad_square + epsilon)
    step_second = (grad_curve + damping * grad_square) / (
        curve_square + 2.0 * damping * grad_curve + damping * damping * grad_square + epsilon
    )
    grad_second = grad_first - step_first * curvature
    return kept_weights - step_first * step_dir - step_second * (mask_local * grad_second)


def call_whole(kernel, out_shape, *operands, alias={}):
    whole = pl.BlockSpec(memory_space=pltpu.VMEM)
    return pl.pallas_call(
        kernel,
        in_specs=[whole] * len(operands),
        out_specs=[whole] * len(out_shape),
        out_shape=out_shape,
        input_output_aliases=alias,
        compiler_params=pltpu.CompilerParams(vmem_limit_bytes=LIMIT),
    )(*operands)


def per_device(gram_old, activations, weights, block_mask):
    row_block, _ = gram_old.shape
    width = weights.shape[1]
    samples = activations.shape[0]
    count = lax.axis_size("row")
    if row_block % (2 * BLK * TILES) or row_block % (16 * PARTS) or count not in (4, 8, 16) or width != BLK or samples % 16:
        return per_device_general(gram_old, activations, weights, block_mask)
    ring = Ring(count)
    row_index = lax.axis_index("row")
    col_index = lax.axis_index("col")
    per_block = row_block // BLK
    own_mask = lax.dynamic_slice(block_mask, (row_index * per_block, col_index), (per_block, 1))
    blocks = jnp.broadcast_to(own_mask.astype(jnp.float32), (per_block, width))
    panel = jax.ShapeDtypeStruct((row_block, width), jnp.float32)
    letter = jax.ShapeDtypeStruct((row_block + samples, width), jnp.bfloat16)
    eight = jax.ShapeDtypeStruct((8, width), jnp.float32)

    (message,) = call_whole(head_kernel, [letter], weights, blocks, activations)
    across = None

    def load(second):
        nonlocal across
        store, across, second = load_first(ring, gram_old, activations, second)
        return store, across, second

    own, received, store, (trace,) = ring_apply(ring, gram_old, message, activations, load)
    held = jax.ShapeDtypeStruct(store.shape, store.dtype)
    grad, message, store = call_whole(
        turn_kernel, [panel, letter, held], own, received, blocks, activations, store, alias={4: 2}
    )

    def keep(second):
        return store, across, second

    own, received, _, _ = ring_apply(ring, None, message, activations, keep)
    curve, sums = call_whole(curve_kernel, [panel, eight], trace, grad, own, received, blocks)
    sums = sum_part(sums, count)
    last = functools.partial(last_kernel, float(count * row_block))
    return call_whole(last, [panel], sums, grad, curve, weights, blocks)[0]


def solution(mesh):
    placed = (
        P(("groups", "row"), "col"),
        P("groups", "row"),
        P("row", ("groups", "col")),
        P(None, "groups"),
    )
    return jax.shard_map(
        per_device,
        mesh=mesh,
        in_specs=placed,
        out_specs=P("row", ("groups", "col")),
        check_vma=False,
    )
```

```python
import functools

import jax
import jax.numpy as jnp
from jax import lax
from jax.experimental import pallas as pl
from jax.experimental.pallas import tpu as pltpu
from jax.sharding import PartitionSpec as P

BLK = 128
TILES = 1
PARTS = 4
LIMIT = 8 * 1024 * 1024
HEAD_LIMIT = 60 * 1024 * 1024
AXES = ("row", "col")
WEIGHTS = ((1, 1, 0.3, 0.3, 8, 0.02, 0.02), (1, 0.02, 0.3, 2, 4, 0.3, 4))

damping_ratio = 0.3
epsilon = 1e-06


def swap(value, axis, distance):
    return lax.ppermute(value, axis, [(i, i ^ distance) for i in range(lax.axis_size(axis))])


def sum_part(value, count):
    devices = 2 * count
    unit = 1
    while unit < devices:
        size = 2 if unit == 1 else min(4, devices // unit)
        swaps = [[(i, i ^ k * unit) for i in range(devices)] for k in range(1, size)]
        value += sum(lax.ppermute(value, AXES, pairs) for pairs in swaps)
        unit *= size
    return value


def expand_local(block_mask, row_index, row_block, col_index, width_cols):
    if width_cols != BLK:
        row_ids = (row_index * row_block + jnp.arange(row_block, dtype=jnp.int32)) // BLK
        col_ids = (col_index * width_cols + jnp.arange(width_cols, dtype=jnp.int32)) // BLK
        return block_mask[row_ids][:, col_ids].astype(jnp.float32)
    piece = BLK
    while row_block % piece:
        piece //= 2
    column = lax.dynamic_index_in_dim(block_mask, col_index, 1, keepdims=False)
    column = jnp.repeat(column, BLK // piece) if piece != BLK else column
    count = row_block // piece
    own = lax.dynamic_slice_in_dim(column, row_index * count, count, 0).astype(jnp.float32)
    return jnp.broadcast_to(own[:, None, None], (count, piece, width_cols)).reshape(
        row_block, width_cols
    )


class Ring:
    def __init__(self, count):
        self.count = count
        self.order = list(range(0, count, 2)) + list(range(count - 1, 0, -2))
        self.last = count // 2 - 1

    def row(self, place):
        return self.order[place % self.count]

    def half(self, place):
        return self.row(place) * 2 // self.count

    def ahead(self, place):
        return int(place % self.count >= self.count // 2)

    def device(self, place, core):
        return self.row(place) * 2 + core

    def source(self, place, core, step):
        return place - 1 - step if core == self.ahead(place) else place + 1 + step

    def first_column(self, place, core, step):
        origin = self.ahead(self.source(place, core, step))
        return origin if core == self.ahead(place) else 1 - origin

    def places(self):
        return [(place, core) for place in range(self.count) for core in range(2)]

    def shift(self):
        pairs = []
        for place in range(self.count):
            pairs.append(
                (self.device(place, self.ahead(place)), self.device(place + 1, self.ahead(place + 1)))
            )
            pairs.append(
                (
                    self.device(place, 1 - self.ahead(place)),
                    self.device(place - 1, 1 - self.ahead(place - 1)),
                )
            )
        return pairs

    def hand_over(self, step):
        return [
            (self.device(place, core), self.device(place, 1 - core))
            for place, core in self.places()
            if self.half(self.source(place, core, step)) != core
        ]

    def slots(self):
        found = []
        for step in range(self.last):
            found.append((True, step))
            if self.hand_over(step):
                found.append((False, step))
        return found

    def loads(self, slot):
        base = 3 * (2 + len(self.slots()))
        return [base + slot + 1] if slot + 1 < self.count // 2 else []

    def entry(self, place, core, carrier, step):
        source = self.source(place, carrier, step)
        return [
            self.row(source) % (self.count // 2),
            int(self.half(source) == core),
            int(self.first_column(place, carrier, step) != core),
        ]

    def table(self):
        half = self.count // 2
        lines = [None] * (2 * self.count)
        for place, core in self.places():
            line = [self.row(place) % half, int(self.half(place) == core), 0]
            for carrier, step in self.slots():
                line += self.entry(place, core, core if carrier else 1 - core, step)
            line += self.entry(place, core, core, self.last)
            needed = [line[k] for k in range(0, len(line), 3) if line[k + 1]]
            line += needed
            lines[self.device(place, core)] = line
        return lines


def pick(ring, entry):
    device = lax.axis_index("row") * 2 + lax.axis_index("col")
    values = [line[entry] for line in ring.table()]
    picked = jnp.int32(values[0])
    for index, value in enumerate(values):
        if value != values[0]:
            picked = jnp.where(device == index, jnp.int32(value), picked)
    return picked


def block_copies(ring, load, gram, store, sems):
    rows = gram.shape[0]
    there = pl.ds(pl.multiple_of(pick(ring, load) * rows, BLK), rows)
    parts = [pl.ds(part * rows // PARTS, rows // PARTS) for part in range(PARTS)]
    return [
        pltpu.make_async_copy(gram.at[here, there], store.at[here, there], sems.at[part])
        for part, here in enumerate(parts)
    ]


def load_kernel(ring, load, gram, acts, second, store, across, passed, sems):
    copies = block_copies(ring, load, gram, store, sems)
    for copy in copies:
        copy.start()
    across[...] = acts[...].astype(jnp.float32).T.astype(across.dtype)
    for copy in copies:
        copy.wait()


def load_first(ring, gram, acts, second):
    whole = pl.BlockSpec(memory_space=pltpu.VMEM)
    return pl.pallas_call(
        functools.partial(load_kernel, ring, ring.loads(-1)[0]),
        in_specs=[pl.BlockSpec(memory_space=pltpu.HBM), whole, whole],
        out_specs=[whole] * 3,
        out_shape=[
            jax.ShapeDtypeStruct(gram.shape, gram.dtype),
            jax.ShapeDtypeStruct(acts.shape[::-1], acts.dtype),
            jax.ShapeDtypeStruct(second.shape, second.dtype),
        ],
        scratch_shapes=[pltpu.SemaphoreType.DMA((PARTS,))],
        input_output_aliases={2: 2},
        compiler_params=pltpu.CompilerParams(vmem_limit_bytes=LIMIT),
    )(gram, acts, second)


def product_kernel(ring, slot, loads, with_trace, first, second, across, *refs):
    copies = []
    if with_trace:
        acts, gram, _, own, other, store, trace, sems = refs
        trace[...] = jnp.zeros_like(trace)
    elif loads:
        gram, _, own, other, store, sems = refs[-6:]
    else:
        own, other, store = refs[-3:]
    if loads:
        copies = block_copies(ring, loads[0], gram, store, sems)
    for copy in copies:
        copy.start()
    rows, width = own.shape
    start = pl.multiple_of(pick(ring, 3 * slot) * rows, BLK)
    flip = pick(ring, 3 * slot + 2) == 1
    if slot == 0:
        own[...] = jnp.zeros_like(own)
        other[...] = jnp.zeros_like(other)

    @pl.when(pick(ring, 3 * slot + 1) == 1)
    def _():
        @pl.loop(0, TILES)
        def _(tile):
            size = rows // TILES
            here = pl.ds(pl.multiple_of(tile * size, size), size)
            lines = jnp.concatenate([store[here, pl.ds(start, rows)], across[here, :]], axis=1)
            panel = jnp.concatenate([first[...], second[...]], axis=1)
            result = jnp.dot(lines, panel, preferred_element_type=jnp.float32)
            left, right = result[:, :width], result[:, width:]
            own[here, :] += jnp.where(flip, right, left)
            other[here, :] += jnp.where(flip, left, right)

        if with_trace:
            add_diagonal(store, start, acts, trace)

    for copy in copies:
        copy.wait()


def add_diagonal(store, start, acts, trace):
    lines = lax.broadcasted_iota(jnp.int32, (BLK, BLK), 0)
    same = lines == lax.broadcasted_iota(jnp.int32, (BLK, BLK), 1)
    for block in range(acts.shape[1] // BLK):
        here = slice(block * BLK, (block + 1) * BLK)
        there = pl.ds(pl.multiple_of(start + block * BLK, BLK), BLK)
        square = store[here, there].astype(jnp.float32)
        diag = jnp.sum(jnp.where(same, square, 0.0), axis=0, keepdims=True)
        part = acts[:, here].astype(jnp.float32)
        diag += jnp.sum(part * part, axis=0, keepdims=True)
        trace[0:1, :] += diag.astype(jnp.bfloat16).astype(jnp.float32)


def product(ring, slot, loads, gram, store, message, across, acts, acc):
    rows = across.shape[0]
    width = message[0].shape[1]
    weight = WEIGHTS[gram is None][slot]
    whole = pl.BlockSpec(memory_space=pltpu.VMEM)
    with_trace = bool(loads) and slot == 0
    operands = [*message, across]
    aliases = {len(operands) + k: k for k in range(len(acc))}
    operands += acc
    in_specs = [whole] * (len(operands) + 1)
    out_shape = [jax.ShapeDtypeStruct((rows, width), jnp.float32)] * 2
    out_shape.append(jax.ShapeDtypeStruct(store.shape, store.dtype))
    scratch = []
    if with_trace:
        operands.append(acts)
        in_specs.append(whole)
        out_shape.append(jax.ShapeDtypeStruct((8, width), jnp.float32))
    aliases[len(operands) + bool(loads)] = 2
    if loads:
        operands.append(gram)
        in_specs.insert(len(operands) - 1, pl.BlockSpec(memory_space=pltpu.HBM))
        scratch = [pltpu.SemaphoreType.DMA((PARTS,))]
    operands.append(store)
    results = pl.pallas_call(
        functools.partial(product_kernel, ring, slot, loads, with_trace),
        in_specs=in_specs,
        out_specs=[whole] * len(out_shape),
        out_shape=out_shape,
        scratch_shapes=scratch,
        input_output_aliases=aliases,
        compiler_params=pltpu.CompilerParams(vmem_limit_bytes=LIMIT),
        cost_estimate=pl.CostEstimate(
            flops=int(weight * 4 * rows * rows * width),
            bytes_accessed=int(weight * 2 * rows * rows),
            transcendentals=0,
        ),
    )(*operands)
    return results[:2], results[2], results[3:]


def after(value, others):
    return lax.optimization_barrier((value, *others))[0]


def ring_apply(ring, gram, message, acts, early):
    first = message
    trace = []
    store, across, second = early(swap(message, "col", 1))
    ready = [(first, second)]
    acc = []
    slot = 0

    def work(others=()):
        nonlocal acc, store, slot, trace
        if not ready:
            return
        parts = ready.pop(0)
        parts = (after(parts[0], others), parts[1])
        loads = [] if gram is None else ring.loads(slot)
        acc, store, added = product(ring, slot, loads, gram, store, parts, across, acts, acc)
        trace = trace or added
        slot += 1

    def hand_over(step):
        if ring.hand_over(step):
            ready.append(tuple(swap(after(part, acc[:1]), "col", 1) for part in held))

    for step in range(ring.last):
        came = lax.ppermute(after(first, acc[:1]), AXES, ring.shift())
        if step:
            work([first])
        second = lax.ppermute(after(second, acc[:1]), AXES, ring.shift())
        if step:
            hand_over(step - 1)
            work()
        first = came
        held = (first, second)
        ready.append(held)
    first = lax.ppermute(after(first, acc[:1]), AXES, ring.shift())
    hand_over(ring.last - 1)
    while ready:
        work()
    last = (first, swap(after(first, acc[:1]), "col", 1))
    (own, other), store, _ = product(ring, slot, [], gram, store, last, across, acts, acc)
    return own, swap(other, "col", 1), store, trace


def put_message(message, acts, rows):
    message[rows:, :] = jnp.dot(
        acts[...], message[:rows, :], preferred_element_type=jnp.float32
    ).astype(message.dtype)


def head_kernel(mask, weights, acts, message, kept, dense, samples, sems):
    copies = [
        pltpu.make_async_copy(mask, kept, sems.at[0]),
        pltpu.make_async_copy(weights, dense, sems.at[1]),
        pltpu.make_async_copy(acts, samples, sems.at[2]),
    ]
    for copy in copies:
        copy.start()
    for copy in copies:
        copy.wait()
    rows = weights.shape[0]
    top, column = lax.axis_index("row") * (rows // BLK), lax.axis_index("col")
    for block in range(rows // BLK):
        here = slice(block * BLK, (block + 1) * BLK)
        factor = kept[column, top + block].astype(jnp.float32)
        message[here, :] = (factor * dense[here, :] - dense[here, :]).astype(message.dtype)
    put_message(message, samples, rows)


def first_message(block_mask, weights, acts, letter):
    mask = block_mask.T
    return pl.pallas_call(
        head_kernel,
        in_specs=[pl.BlockSpec(memory_space=pltpu.HBM)] * 3,
        out_specs=pl.BlockSpec(memory_space=pltpu.VMEM),
        out_shape=letter,
        scratch_shapes=[
            pltpu.SMEM(mask.shape, mask.dtype),
            pltpu.VMEM(weights.shape, weights.dtype),
            pltpu.VMEM(acts.shape, acts.dtype),
            pltpu.SemaphoreType.DMA((3,)),
        ],
        compiler_params=pltpu.CompilerParams(vmem_limit_bytes=HEAD_LIMIT),
    )(mask, weights, acts)


def turn_kernel(own, received, blocks, acts, _, grad, message, __):
    rows = own.shape[0]
    for block in range(rows // BLK):
        here = slice(block * BLK, (block + 1) * BLK)
        grad_first = own[here, :] + received[here, :]
        grad[here, :] = grad_first
        message[here, :] = (blocks[block : block + 1, :] * grad_first).astype(message.dtype)
    put_message(message, acts, rows)


def lane_sums(value):
    return jnp.sum(value, axis=0, keepdims=True)


def curve_kernel(trace, grad, own, received, blocks, curve_ref, sums_ref):
    rows = grad.shape[0]
    sums_ref[...] = jnp.zeros_like(sums_ref)
    sums_ref[0:1, :] = trace[0:1, :]
    for block in range(rows // BLK):
        here = slice(block * BLK, (block + 1) * BLK)
        kept = blocks[block : block + 1, :]
        curve = own[here, :] + received[here, :]
        curve_ref[here, :] = curve
        step_dir = kept * grad[here, :]
        masked = kept * curve
        sums_ref[1:2, :] += lane_sums(step_dir * step_dir)
        sums_ref[2:3, :] += lane_sums(step_dir * curve)
        sums_ref[3:4, :] += lane_sums(masked * masked)


def last_kernel(units, sums, grad, curve, weights, blocks, out_ref):
    totals = jnp.sum(sums[...], axis=1, keepdims=True)
    trace_total, grad_square = totals[0:1, :], totals[1:2, :]
    grad_curve, curve_square = totals[2:3, :], totals[3:4, :]
    damping = damping_ratio * trace_total / units
    step_first = grad_square / (grad_curve + damping * grad_square + epsilon)
    step_second = (grad_curve + damping * grad_square) / (
        curve_square + 2.0 * damping * grad_curve + damping * damping * grad_square + epsilon
    )
    rows = grad.shape[0]
    for block in range(rows // BLK):
        here = slice(block * BLK, (block + 1) * BLK)
        kept = blocks[block : block + 1, :]
        grad_first = grad[here, :]
        step_dir = kept * grad_first
        grad_second = grad_first - step_first * curve[here, :]
        out_ref[here, :] = (
            kept * weights[here, :] - step_first * step_dir - step_second * (kept * grad_second)
        )


def gather_apply(gram, activations, panel, col_index):
    half = gram.shape[1]
    full = lax.all_gather(panel, "row", axis=0, tiled=True)
    own_half = lax.dynamic_slice_in_dim(full, col_index * half, half, 0)
    need = lax.dynamic_slice_in_dim(full, (1 - col_index) * half, half, 0)
    other_half = swap(need, "col", 1)
    own = jnp.dot(gram, own_half, preferred_element_type=jnp.float32)
    partial = jnp.dot(gram, other_half, preferred_element_type=jnp.float32)
    low = lax.psum(jnp.dot(activations, panel, preferred_element_type=jnp.float32), "row")
    update = lax.dot_general(
        activations.astype(jnp.float32),
        low,
        (((0,), (0,)), ((), ())),
        precision=lax.Precision.HIGHEST,
        preferred_element_type=jnp.float32,
    )
    return own + swap(partial, "col", 1) + update


def per_device_general(gram_old, activations, weights, block_mask):
    row_block, half_width = gram_old.shape
    width_cols = weights.shape[1]
    units = lax.axis_size("row") * row_block
    row_index = lax.axis_index("row")
    col_index = lax.axis_index("col")
    mask_local = expand_local(block_mask, row_index, row_block, col_index, width_cols)
    kept_weights = mask_local * weights
    diff_low = (kept_weights - weights).astype(jnp.bfloat16)
    acts = activations.astype(jnp.float32)
    column_squares = jnp.sum(acts * acts, axis=0)
    grad_first = gather_apply(gram_old, activations, diff_low, col_index)
    place = row_index * row_block + jnp.arange(row_block, dtype=jnp.int32)
    place = place - col_index * half_width
    on_diagonal = jnp.arange(half_width, dtype=jnp.int32)[None, :] == place[:, None]
    new_gram = gram_old.astype(jnp.float32) + column_squares[:, None]
    new_gram = new_gram.astype(jnp.bfloat16).astype(jnp.float32)
    trace_part = jnp.sum(jnp.where(on_diagonal, new_gram, 0.0))
    step_dir = mask_local * grad_first
    curvature = gather_apply(gram_old, activations, step_dir.astype(jnp.bfloat16), col_index)
    masked_curve = mask_local * curvature
    sums = jnp.stack(
        [
            trace_part,
            jnp.sum(step_dir * step_dir),
            jnp.sum(step_dir * curvature),
            jnp.sum(masked_curve * masked_curve),
        ]
    )
    sums = lax.psum(sums, ("row", "col"))
    trace_total, grad_square, grad_curve, curve_square = sums[0], sums[1], sums[2], sums[3]
    damping = damping_ratio * trace_total / units
    step_first = grad_square / (grad_curve + damping * grad_square + epsilon)
    step_second = (grad_curve + damping * grad_square) / (
        curve_square + 2.0 * damping * grad_curve + damping * damping * grad_square + epsilon
    )
    grad_second = grad_first - step_first * curvature
    return kept_weights - step_first * step_dir - step_second * (mask_local * grad_second)


def call_whole(kernel, out_shape, *operands, alias={}):
    whole = pl.BlockSpec(memory_space=pltpu.VMEM)
    return pl.pallas_call(
        kernel,
        in_specs=[whole] * len(operands),
        out_specs=[whole] * len(out_shape),
        out_shape=out_shape,
        input_output_aliases=alias,
        compiler_params=pltpu.CompilerParams(vmem_limit_bytes=LIMIT),
    )(*operands)


def per_device(gram_old, activations, weights, block_mask):
    row_block, _ = gram_old.shape
    width = weights.shape[1]
    samples = activations.shape[0]
    count = lax.axis_size("row")
    if row_block % (BLK * TILES) or row_block % (16 * PARTS) or count not in (4, 8, 16) or width != BLK or samples % 16:
        return per_device_general(gram_old, activations, weights, block_mask)
    ring = Ring(count)
    row_index = lax.axis_index("row")
    col_index = lax.axis_index("col")
    per_block = row_block // BLK
    own_mask = lax.dynamic_slice(block_mask, (row_index * per_block, col_index), (per_block, 1))
    blocks = jnp.broadcast_to(own_mask.astype(jnp.float32), (per_block, width))
    panel = jax.ShapeDtypeStruct((row_block, width), jnp.float32)
    letter = jax.ShapeDtypeStruct((row_block + samples, width), jnp.bfloat16)
    eight = jax.ShapeDtypeStruct((8, width), jnp.float32)

    message = first_message(block_mask, weights, activations, letter)
    across = None

    def load(second):
        nonlocal across
        store, across, second = load_first(ring, gram_old, activations, second)
        return store, across, second

    own, received, store, (trace,) = ring_apply(ring, gram_old, message, activations, load)
    held = jax.ShapeDtypeStruct(store.shape, store.dtype)
    grad, message, store = call_whole(
        turn_kernel, [panel, letter, held], own, received, blocks, activations, store, alias={4: 2}
    )

    def keep(second):
        return store, across, second

    own, received, _, _ = ring_apply(ring, None, message, activations, keep)
    curve, sums = call_whole(curve_kernel, [panel, eight], trace, grad, own, received, blocks)
    sums = sum_part(sums, count)
    last = functools.partial(last_kernel, float(count * row_block))
    return call_whole(last, [panel], sums, grad, curve, weights, blocks)[0]


def solution(mesh):
    placed = (
        P(("groups", "row"), "col"),
        P("groups", "row"),
        P("row", ("groups", "col")),
        P(None, "groups"),
    )
    return jax.shard_map(
        per_device,
        mesh=mesh,
        in_specs=placed,
        out_specs=P("row", ("groups", "col")),
        check_vma=False,
    )
```

```python
import functools

import jax
import jax.numpy as jnp
from jax import lax
from jax.experimental import pallas as pl
from jax.experimental.pallas import tpu as pltpu
from jax.sharding import PartitionSpec as P

BLK = 128
TILES = 1
PARTS = 4
LIMIT = 8 * 1024 * 1024
AXES = ("row", "col")
WEIGHTS = ((1, 1, 0.3, 0.3, 8, 0.02, 0.02), (1, 0.02, 0.3, 2, 4, 0.3, 4))

damping_ratio = 0.3
epsilon = 1e-06


def swap(value, axis, distance):
    return lax.ppermute(value, axis, [(i, i ^ distance) for i in range(lax.axis_size(axis))])


def sum_part(value, count):
    devices = 2 * count
    unit = 1
    while unit < devices:
        value += lax.ppermute(value, AXES, [(i, i ^ unit) for i in range(devices)])
        unit *= 2
    return value


def expand_local(block_mask, row_index, row_block, col_index, width_cols):
    if width_cols != BLK:
        row_ids = (row_index * row_block + jnp.arange(row_block, dtype=jnp.int32)) // BLK
        col_ids = (col_index * width_cols + jnp.arange(width_cols, dtype=jnp.int32)) // BLK
        return block_mask[row_ids][:, col_ids].astype(jnp.float32)
    piece = BLK
    while row_block % piece:
        piece //= 2
    column = lax.dynamic_index_in_dim(block_mask, col_index, 1, keepdims=False)
    column = jnp.repeat(column, BLK // piece) if piece != BLK else column
    count = row_block // piece
    own = lax.dynamic_slice_in_dim(column, row_index * count, count, 0).astype(jnp.float32)
    return jnp.broadcast_to(own[:, None, None], (count, piece, width_cols)).reshape(
        row_block, width_cols
    )


class Ring:
    def __init__(self, count):
        self.count = count
        self.order = list(range(0, count, 2)) + list(range(count - 1, 0, -2))
        self.last = count // 2 - 1

    def row(self, place):
        return self.order[place % self.count]

    def half(self, place):
        return self.row(place) * 2 // self.count

    def ahead(self, place):
        return int(place % self.count >= self.count // 2)

    def device(self, place, core):
        return self.row(place) * 2 + core

    def source(self, place, core, step):
        return place - 1 - step if core == self.ahead(place) else place + 1 + step

    def first_column(self, place, core, step):
        origin = self.ahead(self.source(place, core, step))
        return origin if core == self.ahead(place) else 1 - origin

    def places(self):
        return [(place, core) for place in range(self.count) for core in range(2)]

    def shift(self):
        pairs = []
        for place in range(self.count):
            pairs.append(
                (self.device(place, self.ahead(place)), self.device(place + 1, self.ahead(place + 1)))
            )
            pairs.append(
                (
                    self.device(place, 1 - self.ahead(place)),
                    self.device(place - 1, 1 - self.ahead(place - 1)),
                )
            )
        return pairs

    def hand_over(self, step):
        return [
            (self.device(place, core), self.device(place, 1 - core))
            for place, core in self.places()
            if self.half(self.source(place, core, step)) != core
        ]

    def slots(self):
        found = []
        for step in range(self.last):
            found.append((True, step))
            if self.hand_over(step):
                found.append((False, step))
        return found

    def loads(self, slot):
        base = 3 * (2 + len(self.slots()))
        return [base + slot + 1] if slot + 1 < self.count // 2 else []

    def entry(self, place, core, carrier, step):
        source = self.source(place, carrier, step)
        return [
            self.row(source) % (self.count // 2),
            int(self.half(source) == core),
            int(self.first_column(place, carrier, step) != core),
        ]

    def table(self):
        half = self.count // 2
        lines = [None] * (2 * self.count)
        for place, core in self.places():
            line = [self.row(place) % half, int(self.half(place) == core), 0]
            for carrier, step in self.slots():
                line += self.entry(place, core, core if carrier else 1 - core, step)
            line += self.entry(place, core, core, self.last)
            needed = [line[k] for k in range(0, len(line), 3) if line[k + 1]]
            line += needed
            lines[self.device(place, core)] = line
        return lines


def pick(ring, entry):
    device = lax.axis_index("row") * 2 + lax.axis_index("col")
    values = [line[entry] for line in ring.table()]
    picked = jnp.int32(values[0])
    for index, value in enumerate(values):
        if value != values[0]:
            picked = jnp.where(device == index, jnp.int32(value), picked)
    return picked


def block_copies(ring, load, gram, store, sems):
    rows = gram.shape[0]
    there = pl.ds(pl.multiple_of(pick(ring, load) * rows, BLK), rows)
    parts = [pl.ds(part * rows // PARTS, rows // PARTS) for part in range(PARTS)]
    return [
        pltpu.make_async_copy(gram.at[here, there], store.at[here, there], sems.at[part])
        for part, here in enumerate(parts)
    ]


def load_kernel(ring, load, gram, acts, second, store, across, passed, sems):
    copies = block_copies(ring, load, gram, store, sems)
    for copy in copies:
        copy.start()
    across[...] = acts[...].astype(jnp.float32).T.astype(across.dtype)
    for copy in copies:
        copy.wait()


def load_first(ring, gram, acts, second):
    whole = pl.BlockSpec(memory_space=pltpu.VMEM)
    return pl.pallas_call(
        functools.partial(load_kernel, ring, ring.loads(-1)[0]),
        in_specs=[pl.BlockSpec(memory_space=pltpu.HBM), whole, whole],
        out_specs=[whole] * 3,
        out_shape=[
            jax.ShapeDtypeStruct(gram.shape, gram.dtype),
            jax.ShapeDtypeStruct(acts.shape[::-1], acts.dtype),
            jax.ShapeDtypeStruct(second.shape, second.dtype),
        ],
        scratch_shapes=[pltpu.SemaphoreType.DMA((PARTS,))],
        input_output_aliases={2: 2},
        compiler_params=pltpu.CompilerParams(vmem_limit_bytes=LIMIT),
    )(gram, acts, second)


def product_kernel(ring, slot, loads, with_trace, first, second, across, *refs):
    copies = []
    if with_trace:
        acts, gram, _, own, other, store, trace, sems = refs
        trace[...] = jnp.zeros_like(trace)
    elif loads:
        gram, _, own, other, store, sems = refs[-6:]
    else:
        own, other, store = refs[-3:]
    if loads:
        copies = block_copies(ring, loads[0], gram, store, sems)
    for copy in copies:
        copy.start()
    rows, width = own.shape
    start = pl.multiple_of(pick(ring, 3 * slot) * rows, BLK)
    flip = pick(ring, 3 * slot + 2) == 1
    if slot == 0:
        own[...] = jnp.zeros_like(own)
        other[...] = jnp.zeros_like(other)

    @pl.when(pick(ring, 3 * slot + 1) == 1)
    def _():
        @pl.loop(0, TILES)
        def _(tile):
            size = rows // TILES
            here = pl.ds(pl.multiple_of(tile * size, size), size)
            lines = jnp.concatenate([store[here, pl.ds(start, rows)], across[here, :]], axis=1)
            panel = jnp.concatenate([first[...], second[...]], axis=1)
            result = jnp.dot(lines, panel, preferred_element_type=jnp.float32)
            left, right = result[:, :width], result[:, width:]
            own[here, :] += jnp.where(flip, right, left)
            other[here, :] += jnp.where(flip, left, right)

        if with_trace:
            add_diagonal(store, start, acts, trace)

    for copy in copies:
        copy.wait()


def add_diagonal(store, start, acts, trace):
    lines = lax.broadcasted_iota(jnp.int32, (BLK, BLK), 0)
    same = lines == lax.broadcasted_iota(jnp.int32, (BLK, BLK), 1)
    for block in range(acts.shape[1] // BLK):
        here = slice(block * BLK, (block + 1) * BLK)
        there = pl.ds(pl.multiple_of(start + block * BLK, BLK), BLK)
        square = store[here, there].astype(jnp.float32)
        diag = jnp.sum(jnp.where(same, square, 0.0), axis=0, keepdims=True)
        part = acts[:, here].astype(jnp.float32)
        diag += jnp.sum(part * part, axis=0, keepdims=True)
        trace[0:1, :] += diag.astype(jnp.bfloat16).astype(jnp.float32)


def product(ring, slot, loads, gram, store, message, across, acts, acc):
    rows = across.shape[0]
    width = message[0].shape[1]
    weight = WEIGHTS[gram is None][slot]
    whole = pl.BlockSpec(memory_space=pltpu.VMEM)
    with_trace = bool(loads) and slot == 0
    operands = [*message, across]
    aliases = {len(operands) + k: k for k in range(len(acc))}
    operands += acc
    in_specs = [whole] * (len(operands) + 1)
    out_shape = [jax.ShapeDtypeStruct((rows, width), jnp.float32)] * 2
    out_shape.append(jax.ShapeDtypeStruct(store.shape, store.dtype))
    scratch = []
    if with_trace:
        operands.append(acts)
        in_specs.append(whole)
        out_shape.append(jax.ShapeDtypeStruct((8, width), jnp.float32))
    aliases[len(operands) + bool(loads)] = 2
    if loads:
        operands.append(gram)
        in_specs.insert(len(operands) - 1, pl.BlockSpec(memory_space=pltpu.HBM))
        scratch = [pltpu.SemaphoreType.DMA((PARTS,))]
    operands.append(store)
    results = pl.pallas_call(
        functools.partial(product_kernel, ring, slot, loads, with_trace),
        in_specs=in_specs,
        out_specs=[whole] * len(out_shape),
        out_shape=out_shape,
        scratch_shapes=scratch,
        input_output_aliases=aliases,
        compiler_params=pltpu.CompilerParams(vmem_limit_bytes=LIMIT),
        cost_estimate=pl.CostEstimate(
            flops=int(weight * 4 * rows * rows * width),
            bytes_accessed=int(weight * 2 * rows * rows),
            transcendentals=0,
        ),
    )(*operands)
    return results[:2], results[2], results[3:]


def after(value, others):
    return lax.optimization_barrier((value, *others))[0]


def ring_apply(ring, gram, message, acts, early):
    first = message
    trace = []
    store, across, second = early(swap(message, "col", 1))
    ready = [(first, second)]
    acc = []
    slot = 0

    def work(others=()):
        nonlocal acc, store, slot, trace
        if not ready:
            return
        parts = ready.pop(0)
        parts = (after(parts[0], others), parts[1])
        loads = [] if gram is None else ring.loads(slot)
        acc, store, added = product(ring, slot, loads, gram, store, parts, across, acts, acc)
        trace = trace or added
        slot += 1

    def hand_over(step):
        if ring.hand_over(step):
            ready.append(tuple(swap(after(part, acc[:1]), "col", 1) for part in held))

    for step in range(ring.last):
        came = lax.ppermute(after(first, acc[:1]), AXES, ring.shift())
        if step:
            work([first])
        second = lax.ppermute(after(second, acc[:1]), AXES, ring.shift())
        if step:
            hand_over(step - 1)
            work()
        first = came
        held = (first, second)
        ready.append(held)
    first = lax.ppermute(after(first, acc[:1]), AXES, ring.shift())
    hand_over(ring.last - 1)
    while ready:
        work()
    last = (first, swap(after(first, acc[:1]), "col", 1))
    (own, other), store, _ = product(ring, slot, [], gram, store, last, across, acts, acc)
    return own, swap(other, "col", 1), store, trace


def put_message(message, acts, rows):
    message[rows:, :] = jnp.dot(
        acts[...], message[:rows, :], preferred_element_type=jnp.float32
    ).astype(message.dtype)


def head_kernel(weights, blocks, acts, message):
    rows = weights.shape[0]
    for block in range(rows // BLK):
        here = slice(block * BLK, (block + 1) * BLK)
        dense = weights[here, :]
        message[here, :] = (blocks[block : block + 1, :] * dense - dense).astype(message.dtype)
    put_message(message, acts, rows)


def turn_kernel(own, received, blocks, acts, _, grad, message, __):
    rows = own.shape[0]
    for block in range(rows // BLK):
        here = slice(block * BLK, (block + 1) * BLK)
        grad_first = own[here, :] + received[here, :]
        grad[here, :] = grad_first
        message[here, :] = (blocks[block : block + 1, :] * grad_first).astype(message.dtype)
    put_message(message, acts, rows)


def lane_sums(value):
    return jnp.sum(value, axis=0, keepdims=True)


def curve_kernel(trace, grad, own, received, blocks, curve_ref, sums_ref):
    rows = grad.shape[0]
    sums_ref[...] = jnp.zeros_like(sums_ref)
    sums_ref[0:1, :] = trace[0:1, :]
    for block in range(rows // BLK):
        here = slice(block * BLK, (block + 1) * BLK)
        kept = blocks[block : block + 1, :]
        curve = own[here, :] + received[here, :]
        curve_ref[here, :] = curve
        step_dir = kept * grad[here, :]
        masked = kept * curve
        sums_ref[1:2, :] += lane_sums(step_dir * step_dir)
        sums_ref[2:3, :] += lane_sums(step_dir * curve)
        sums_ref[3:4, :] += lane_sums(masked * masked)


def last_kernel(units, sums, grad, curve, weights, blocks, out_ref):
    totals = jnp.sum(sums[...], axis=1, keepdims=True)
    trace_total, grad_square = totals[0:1, :], totals[1:2, :]
    grad_curve, curve_square = totals[2:3, :], totals[3:4, :]
    damping = damping_ratio * trace_total / units
    step_first = grad_square / (grad_curve + damping * grad_square + epsilon)
    step_second = (grad_curve + damping * grad_square) / (
        curve_square + 2.0 * damping * grad_curve + damping * damping * grad_square + epsilon
    )
    rows = grad.shape[0]
    for block in range(rows // BLK):
        here = slice(block * BLK, (block + 1) * BLK)
        kept = blocks[block : block + 1, :]
        grad_first = grad[here, :]
        step_dir = kept * grad_first
        grad_second = grad_first - step_first * curve[here, :]
        out_ref[here, :] = (
            kept * weights[here, :] - step_first * step_dir - step_second * (kept * grad_second)
        )


def gather_apply(gram, activations, panel, col_index):
    half = gram.shape[1]
    full = lax.all_gather(panel, "row", axis=0, tiled=True)
    own_half = lax.dynamic_slice_in_dim(full, col_index * half, half, 0)
    need = lax.dynamic_slice_in_dim(full, (1 - col_index) * half, half, 0)
    other_half = swap(need, "col", 1)
    own = jnp.dot(gram, own_half, preferred_element_type=jnp.float32)
    partial = jnp.dot(gram, other_half, preferred_element_type=jnp.float32)
    low = lax.psum(jnp.dot(activations, panel, preferred_element_type=jnp.float32), "row")
    update = lax.dot_general(
        activations.astype(jnp.float32),
        low,
        (((0,), (0,)), ((), ())),
        precision=lax.Precision.HIGHEST,
        preferred_element_type=jnp.float32,
    )
    return own + swap(partial, "col", 1) + update


def per_device_general(gram_old, activations, weights, block_mask):
    row_block, half_width = gram_old.shape
    width_cols = weights.shape[1]
    units = lax.axis_size("row") * row_block
    row_index = lax.axis_index("row")
    col_index = lax.axis_index("col")
    mask_local = expand_local(block_mask, row_index, row_block, col_index, width_cols)
    kept_weights = mask_local * weights
    diff_low = (kept_weights - weights).astype(jnp.bfloat16)
    acts = activations.astype(jnp.float32)
    column_squares = jnp.sum(acts * acts, axis=0)
    grad_first = gather_apply(gram_old, activations, diff_low, col_index)
    place = row_index * row_block + jnp.arange(row_block, dtype=jnp.int32)
    place = place - col_index * half_width
    on_diagonal = jnp.arange(half_width, dtype=jnp.int32)[None, :] == place[:, None]
    new_gram = gram_old.astype(jnp.float32) + column_squares[:, None]
    new_gram = new_gram.astype(jnp.bfloat16).astype(jnp.float32)
    trace_part = jnp.sum(jnp.where(on_diagonal, new_gram, 0.0))
    step_dir = mask_local * grad_first
    curvature = gather_apply(gram_old, activations, step_dir.astype(jnp.bfloat16), col_index)
    masked_curve = mask_local * curvature
    sums = jnp.stack(
        [
            trace_part,
            jnp.sum(step_dir * step_dir),
            jnp.sum(step_dir * curvature),
            jnp.sum(masked_curve * masked_curve),
        ]
    )
    sums = lax.psum(sums, ("row", "col"))
    trace_total, grad_square, grad_curve, curve_square = sums[0], sums[1], sums[2], sums[3]
    damping = damping_ratio * trace_total / units
    step_first = grad_square / (grad_curve + damping * grad_square + epsilon)
    step_second = (grad_curve + damping * grad_square) / (
        curve_square + 2.0 * damping * grad_curve + damping * damping * grad_square + epsilon
    )
    grad_second = grad_first - step_first * curvature
    return kept_weights - step_first * step_dir - step_second * (mask_local * grad_second)


def call_whole(kernel, out_shape, *operands, alias={}):
    whole = pl.BlockSpec(memory_space=pltpu.VMEM)
    return pl.pallas_call(
        kernel,
        in_specs=[whole] * len(operands),
        out_specs=[whole] * len(out_shape),
        out_shape=out_shape,
        input_output_aliases=alias,
        compiler_params=pltpu.CompilerParams(vmem_limit_bytes=LIMIT),
    )(*operands)


def per_device(gram_old, activations, weights, block_mask):
    row_block, _ = gram_old.shape
    width = weights.shape[1]
    samples = activations.shape[0]
    count = lax.axis_size("row")
    if row_block % (BLK * TILES) or row_block % (16 * PARTS) or count not in (4, 8, 16) or width != BLK or samples % 16:
        return per_device_general(gram_old, activations, weights, block_mask)
    ring = Ring(count)
    row_index = lax.axis_index("row")
    col_index = lax.axis_index("col")
    per_block = row_block // BLK
    own_mask = lax.dynamic_slice(block_mask, (row_index * per_block, col_index), (per_block, 1))
    blocks = jnp.broadcast_to(own_mask.astype(jnp.float32), (per_block, width))
    panel = jax.ShapeDtypeStruct((row_block, width), jnp.float32)
    letter = jax.ShapeDtypeStruct((row_block + samples, width), jnp.bfloat16)
    eight = jax.ShapeDtypeStruct((8, width), jnp.float32)

    (message,) = call_whole(head_kernel, [letter], weights, blocks, activations)
    across = None

    def load(second):
        nonlocal across
        store, across, second = load_first(ring, gram_old, activations, second)
        return store, across, second

    own, received, store, (trace,) = ring_apply(ring, gram_old, message, activations, load)
    held = jax.ShapeDtypeStruct(store.shape, store.dtype)
    grad, message, store = call_whole(
        turn_kernel, [panel, letter, held], own, received, blocks, activations, store, alias={4: 2}
    )

    def keep(second):
        return store, across, second

    own, received, _, _ = ring_apply(ring, None, message, activations, keep)
    curve, sums = call_whole(curve_kernel, [panel, eight], trace, grad, own, received, blocks)
    sums = sum_part(sums, count)
    last = functools.partial(last_kernel, float(count * row_block))
    return call_whole(last, [panel], sums, grad, curve, weights, blocks)[0]


def solution(mesh):
    placed = (
        P(("groups", "row"), "col"),
        P("groups", "row"),
        P("row", ("groups", "col")),
        P(None, "groups"),
    )
    return jax.shard_map(
        per_device,
        mesh=mesh,
        in_specs=placed,
        out_specs=P("row", ("groups", "col")),
        check_vma=False,
    )
```

```python
import functools

import jax
import jax.numpy as jnp
from jax import lax
from jax.experimental import pallas as pl
from jax.experimental.pallas import tpu as pltpu
from jax.sharding import PartitionSpec as P

BLK = 128
TILES = 1
PARTS = 4
LIMIT = 8 * 1024 * 1024
AXES = ("row", "col")
WEIGHTS = ((1, 1, 0.3, 0.3, 8, 0.02, 0.02), (1, 0.02, 0.3, 2, 4, 0.3, 4))

damping_ratio = 0.3
epsilon = 1e-06


def swap(value, axis, distance):
    return lax.ppermute(value, axis, [(i, i ^ distance) for i in range(lax.axis_size(axis))])


def sum_part(value, count):
    devices = 2 * count
    unit = 1
    while unit < devices:
        value += lax.ppermute(value, AXES, [(i, i ^ unit) for i in range(devices)])
        unit *= 2
    return value


def expand_local(block_mask, row_index, row_block, col_index, width_cols):
    if width_cols != BLK:
        row_ids = (row_index * row_block + jnp.arange(row_block, dtype=jnp.int32)) // BLK
        col_ids = (col_index * width_cols + jnp.arange(width_cols, dtype=jnp.int32)) // BLK
        return block_mask[row_ids][:, col_ids].astype(jnp.float32)
    piece = BLK
    while row_block % piece:
        piece //= 2
    column = lax.dynamic_index_in_dim(block_mask, col_index, 1, keepdims=False)
    column = jnp.repeat(column, BLK // piece) if piece != BLK else column
    count = row_block // piece
    own = lax.dynamic_slice_in_dim(column, row_index * count, count, 0).astype(jnp.float32)
    return jnp.broadcast_to(own[:, None, None], (count, piece, width_cols)).reshape(
        row_block, width_cols
    )


class Ring:
    def __init__(self, count):
        self.count = count
        self.order = list(range(0, count, 2)) + list(range(count - 1, 0, -2))
        self.last = count // 2 - 1

    def row(self, place):
        return self.order[place % self.count]

    def half(self, place):
        return self.row(place) * 2 // self.count

    def ahead(self, place):
        return int(place % self.count >= self.count // 2)

    def device(self, place, core):
        return self.row(place) * 2 + core

    def source(self, place, core, step):
        return place - 1 - step if core == self.ahead(place) else place + 1 + step

    def first_column(self, place, core, step):
        origin = self.ahead(self.source(place, core, step))
        return origin if core == self.ahead(place) else 1 - origin

    def places(self):
        return [(place, core) for place in range(self.count) for core in range(2)]

    def shift(self):
        pairs = []
        for place in range(self.count):
            pairs.append(
                (self.device(place, self.ahead(place)), self.device(place + 1, self.ahead(place + 1)))
            )
            pairs.append(
                (
                    self.device(place, 1 - self.ahead(place)),
                    self.device(place - 1, 1 - self.ahead(place - 1)),
                )
            )
        return pairs

    def hand_over(self, step):
        return [
            (self.device(place, core), self.device(place, 1 - core))
            for place, core in self.places()
            if self.half(self.source(place, core, step)) != core
        ]

    def slots(self):
        found = []
        for step in range(self.last):
            found.append((True, step))
            if self.hand_over(step):
                found.append((False, step))
        return found

    def loads(self, slot):
        base = 3 * (2 + len(self.slots()))
        return [base + slot + 1] if slot + 1 < self.count // 2 else []

    def entry(self, place, core, carrier, step):
        source = self.source(place, carrier, step)
        return [
            self.row(source) % (self.count // 2),
            int(self.half(source) == core),
            int(self.first_column(place, carrier, step) != core),
        ]

    def table(self):
        half = self.count // 2
        lines = [None] * (2 * self.count)
        for place, core in self.places():
            line = [self.row(place) % half, int(self.half(place) == core), 0]
            for carrier, step in self.slots():
                line += self.entry(place, core, core if carrier else 1 - core, step)
            line += self.entry(place, core, core, self.last)
            needed = [line[k] for k in range(0, len(line), 3) if line[k + 1]]
            line += needed
            lines[self.device(place, core)] = line
        return lines


def pick(ring, entry):
    device = lax.axis_index("row") * 2 + lax.axis_index("col")
    values = [line[entry] for line in ring.table()]
    picked = jnp.int32(values[0])
    for index, value in enumerate(values):
        if value != values[0]:
            picked = jnp.where(device == index, jnp.int32(value), picked)
    return picked


def block_copies(ring, load, gram, store, sems):
    rows = gram.shape[0]
    there = pl.ds(pl.multiple_of(pick(ring, load) * rows, BLK), rows)
    parts = [pl.ds(part * rows // PARTS, rows // PARTS) for part in range(PARTS)]
    return [
        pltpu.make_async_copy(gram.at[here, there], store.at[here, there], sems.at[part])
        for part, here in enumerate(parts)
    ]


def load_kernel(ring, load, gram, acts, second, store, across, passed, sems):
    copies = block_copies(ring, load, gram, store, sems)
    for copy in copies:
        copy.start()
    across[...] = acts[...].astype(jnp.float32).T.astype(across.dtype)
    for copy in copies:
        copy.wait()


def load_first(ring, gram, acts, second):
    whole = pl.BlockSpec(memory_space=pltpu.VMEM)
    return pl.pallas_call(
        functools.partial(load_kernel, ring, ring.loads(-1)[0]),
        in_specs=[pl.BlockSpec(memory_space=pltpu.HBM), whole, whole],
        out_specs=[whole] * 3,
        out_shape=[
            jax.ShapeDtypeStruct(gram.shape, gram.dtype),
            jax.ShapeDtypeStruct(acts.shape[::-1], acts.dtype),
            jax.ShapeDtypeStruct(second.shape, second.dtype),
        ],
        scratch_shapes=[pltpu.SemaphoreType.DMA((PARTS,))],
        input_output_aliases={2: 2},
        compiler_params=pltpu.CompilerParams(vmem_limit_bytes=LIMIT),
    )(gram, acts, second)


def product_kernel(ring, slot, loads, with_trace, first, second, across, *refs):
    copies = []
    if with_trace:
        acts, gram, _, own, other, store, trace, sems = refs
        trace[...] = jnp.zeros_like(trace)
    elif loads:
        gram, _, own, other, store, sems = refs[-6:]
    else:
        own, other, store = refs[-3:]
    if loads:
        copies = block_copies(ring, loads[0], gram, store, sems)
    for copy in copies:
        copy.start()
    rows, width = own.shape
    start = pl.multiple_of(pick(ring, 3 * slot) * rows, BLK)
    flip = pick(ring, 3 * slot + 2) == 1
    if slot == 0:
        own[...] = jnp.zeros_like(own)
        other[...] = jnp.zeros_like(other)

    @pl.when(pick(ring, 3 * slot + 1) == 1)
    def _():
        @pl.loop(0, TILES)
        def _(tile):
            size = rows // TILES
            here = pl.ds(pl.multiple_of(tile * size, size), size)
            lines = jnp.concatenate([store[here, pl.ds(start, rows)], across[here, :]], axis=1)
            panel = jnp.concatenate([first[...], second[...]], axis=1)
            result = jnp.dot(lines, panel, preferred_element_type=jnp.float32)
            left, right = result[:, :width], result[:, width:]
            own[here, :] += jnp.where(flip, right, left)
            other[here, :] += jnp.where(flip, left, right)

        if with_trace:
            add_diagonal(store, start, acts, trace)

    for copy in copies:
        copy.wait()


def add_diagonal(store, start, acts, trace):
    lines = lax.broadcasted_iota(jnp.int32, (BLK, BLK), 0)
    same = lines == lax.broadcasted_iota(jnp.int32, (BLK, BLK), 1)
    for block in range(acts.shape[1] // BLK):
        here = slice(block * BLK, (block + 1) * BLK)
        there = pl.ds(pl.multiple_of(start + block * BLK, BLK), BLK)
        square = store[here, there].astype(jnp.float32)
        diag = jnp.sum(jnp.where(same, square, 0.0), axis=0, keepdims=True)
        part = acts[:, here].astype(jnp.float32)
        diag += jnp.sum(part * part, axis=0, keepdims=True)
        trace[0:1, :] += diag.astype(jnp.bfloat16).astype(jnp.float32)


def product(ring, slot, loads, gram, store, message, across, acts, acc):
    rows = across.shape[0]
    width = message[0].shape[1]
    weight = WEIGHTS[gram is None][slot]
    whole = pl.BlockSpec(memory_space=pltpu.VMEM)
    with_trace = bool(loads) and slot == 0
    operands = [*message, across]
    aliases = {len(operands) + k: k for k in range(len(acc))}
    operands += acc
    in_specs = [whole] * (len(operands) + 1)
    out_shape = [jax.ShapeDtypeStruct((rows, width), jnp.float32)] * 2
    out_shape.append(jax.ShapeDtypeStruct(store.shape, store.dtype))
    scratch = []
    if with_trace:
        operands.append(acts)
        in_specs.append(whole)
        out_shape.append(jax.ShapeDtypeStruct((8, width), jnp.float32))
    aliases[len(operands) + bool(loads)] = 2
    if loads:
        operands.append(gram)
        in_specs.insert(len(operands) - 1, pl.BlockSpec(memory_space=pltpu.HBM))
        scratch = [pltpu.SemaphoreType.DMA((PARTS,))]
    operands.append(store)
    results = pl.pallas_call(
        functools.partial(product_kernel, ring, slot, loads, with_trace),
        in_specs=in_specs,
        out_specs=[whole] * len(out_shape),
        out_shape=out_shape,
        scratch_shapes=scratch,
        input_output_aliases=aliases,
        compiler_params=pltpu.CompilerParams(vmem_limit_bytes=LIMIT),
        cost_estimate=pl.CostEstimate(
            flops=int(weight * 4 * rows * rows * width),
            bytes_accessed=int(weight * 2 * rows * rows),
            transcendentals=0,
        ),
    )(*operands)
    return results[:2], results[2], results[3:]


def after(value, others):
    return lax.optimization_barrier((value, *others))[0]


def ring_apply(ring, gram, message, acts, early):
    first = message
    trace = []
    store, across, second = early(swap(message, "col", 1))
    ready = [(first, second)]
    acc = []
    slot = 0

    def work(others=()):
        nonlocal acc, store, slot, trace
        if not ready:
            return
        parts = ready.pop(0)
        parts = (after(parts[0], others), parts[1])
        loads = [] if gram is None else ring.loads(slot)
        acc, store, added = product(ring, slot, loads, gram, store, parts, across, acts, acc)
        trace = trace or added
        slot += 1

    def hand_over(step):
        if ring.hand_over(step):
            ready.append(tuple(swap(after(part, acc[:1]), "col", 1) for part in held))

    for step in range(ring.last):
        came = lax.ppermute(after(first, acc[:1]), AXES, ring.shift())
        if step:
            work([first])
        second = lax.ppermute(after(second, acc[:1]), AXES, ring.shift())
        if step:
            hand_over(step - 1)
            work()
        first = came
        held = (first, second)
        ready.append(held)
    first = lax.ppermute(after(first, acc[:1]), AXES, ring.shift())
    hand_over(ring.last - 1)
    while ready:
        work()
    last = (first, swap(after(first, acc[:1]), "col", 1))
    (own, other), store, _ = product(ring, slot, [], gram, store, last, across, acts, acc)
    return own, swap(other, "col", 1), store, trace


def put_message(message, acts, rows):
    message[rows:, :] = jnp.dot(
        acts[...], message[:rows, :], preferred_element_type=jnp.float32
    ).astype(message.dtype)


def head_kernel(weights, blocks, acts, message, kept_acts):
    rows = weights.shape[0]
    for block in range(rows // BLK):
        here = slice(block * BLK, (block + 1) * BLK)
        dense = weights[here, :]
        message[here, :] = (blocks[block : block + 1, :] * dense - dense).astype(message.dtype)
    put_message(message, acts, rows)
    kept_acts[...] = acts[...]


def turn_kernel(own, received, blocks, acts, _, grad, message, __):
    rows = own.shape[0]
    for block in range(rows // BLK):
        here = slice(block * BLK, (block + 1) * BLK)
        grad_first = own[here, :] + received[here, :]
        grad[here, :] = grad_first
        message[here, :] = (blocks[block : block + 1, :] * grad_first).astype(message.dtype)
    put_message(message, acts, rows)


def lane_sums(value):
    return jnp.sum(value, axis=0, keepdims=True)


def curve_kernel(trace, grad, own, received, blocks, curve_ref, sums_ref):
    rows = grad.shape[0]
    sums_ref[...] = jnp.zeros_like(sums_ref)
    sums_ref[0:1, :] = trace[0:1, :]
    for block in range(rows // BLK):
        here = slice(block * BLK, (block + 1) * BLK)
        kept = blocks[block : block + 1, :]
        curve = own[here, :] + received[here, :]
        curve_ref[here, :] = curve
        step_dir = kept * grad[here, :]
        masked = kept * curve
        sums_ref[1:2, :] += lane_sums(step_dir * step_dir)
        sums_ref[2:3, :] += lane_sums(step_dir * curve)
        sums_ref[3:4, :] += lane_sums(masked * masked)


def last_kernel(units, sums, grad, curve, weights, blocks, out_ref):
    totals = jnp.sum(sums[...], axis=1, keepdims=True)
    trace_total, grad_square = totals[0:1, :], totals[1:2, :]
    grad_curve, curve_square = totals[2:3, :], totals[3:4, :]
    damping = damping_ratio * trace_total / units
    step_first = grad_square / (grad_curve + damping * grad_square + epsilon)
    step_second = (grad_curve + damping * grad_square) / (
        curve_square + 2.0 * damping * grad_curve + damping * damping * grad_square + epsilon
    )
    rows = grad.shape[0]
    for block in range(rows // BLK):
        here = slice(block * BLK, (block + 1) * BLK)
        kept = blocks[block : block + 1, :]
        grad_first = grad[here, :]
        step_dir = kept * grad_first
        grad_second = grad_first - step_first * curve[here, :]
        out_ref[here, :] = (
            kept * weights[here, :] - step_first * step_dir - step_second * (kept * grad_second)
        )


def gather_apply(gram, activations, panel, col_index):
    half = gram.shape[1]
    full = lax.all_gather(panel, "row", axis=0, tiled=True)
    own_half = lax.dynamic_slice_in_dim(full, col_index * half, half, 0)
    need = lax.dynamic_slice_in_dim(full, (1 - col_index) * half, half, 0)
    other_half = swap(need, "col", 1)
    own = jnp.dot(gram, own_half, preferred_element_type=jnp.float32)
    partial = jnp.dot(gram, other_half, preferred_element_type=jnp.float32)
    low = lax.psum(jnp.dot(activations, panel, preferred_element_type=jnp.float32), "row")
    update = lax.dot_general(
        activations.astype(jnp.float32),
        low,
        (((0,), (0,)), ((), ())),
        precision=lax.Precision.HIGHEST,
        preferred_element_type=jnp.float32,
    )
    return own + swap(partial, "col", 1) + update


def per_device_general(gram_old, activations, weights, block_mask):
    row_block, half_width = gram_old.shape
    width_cols = weights.shape[1]
    units = lax.axis_size("row") * row_block
    row_index = lax.axis_index("row")
    col_index = lax.axis_index("col")
    mask_local = expand_local(block_mask, row_index, row_block, col_index, width_cols)
    kept_weights = mask_local * weights
    diff_low = (kept_weights - weights).astype(jnp.bfloat16)
    acts = activations.astype(jnp.float32)
    column_squares = jnp.sum(acts * acts, axis=0)
    grad_first = gather_apply(gram_old, activations, diff_low, col_index)
    place = row_index * row_block + jnp.arange(row_block, dtype=jnp.int32)
    place = place - col_index * half_width
    on_diagonal = jnp.arange(half_width, dtype=jnp.int32)[None, :] == place[:, None]
    new_gram = gram_old.astype(jnp.float32) + column_squares[:, None]
    new_gram = new_gram.astype(jnp.bfloat16).astype(jnp.float32)
    trace_part = jnp.sum(jnp.where(on_diagonal, new_gram, 0.0))
    step_dir = mask_local * grad_first
    curvature = gather_apply(gram_old, activations, step_dir.astype(jnp.bfloat16), col_index)
    masked_curve = mask_local * curvature
    sums = jnp.stack(
        [
            trace_part,
            jnp.sum(step_dir * step_dir),
            jnp.sum(step_dir * curvature),
            jnp.sum(masked_curve * masked_curve),
        ]
    )
    sums = lax.psum(sums, ("row", "col"))
    trace_total, grad_square, grad_curve, curve_square = sums[0], sums[1], sums[2], sums[3]
    damping = damping_ratio * trace_total / units
    step_first = grad_square / (grad_curve + damping * grad_square + epsilon)
    step_second = (grad_curve + damping * grad_square) / (
        curve_square + 2.0 * damping * grad_curve + damping * damping * grad_square + epsilon
    )
    grad_second = grad_first - step_first * curvature
    return kept_weights - step_first * step_dir - step_second * (mask_local * grad_second)


def call_whole(kernel, out_shape, *operands, alias={}):
    whole = pl.BlockSpec(memory_space=pltpu.VMEM)
    return pl.pallas_call(
        kernel,
        in_specs=[whole] * len(operands),
        out_specs=[whole] * len(out_shape),
        out_shape=out_shape,
        input_output_aliases=alias,
        compiler_params=pltpu.CompilerParams(vmem_limit_bytes=LIMIT),
    )(*operands)


def per_device(gram_old, activations, weights, block_mask):
    row_block, _ = gram_old.shape
    width = weights.shape[1]
    samples = activations.shape[0]
    count = lax.axis_size("row")
    if row_block % (BLK * TILES) or row_block % (16 * PARTS) or count not in (4, 8, 16) or width != BLK or samples % 16:
        return per_device_general(gram_old, activations, weights, block_mask)
    ring = Ring(count)
    row_index = lax.axis_index("row")
    col_index = lax.axis_index("col")
    per_block = row_block // BLK
    own_mask = lax.dynamic_slice(block_mask, (row_index * per_block, col_index), (per_block, 1))
    blocks = jnp.broadcast_to(own_mask.astype(jnp.float32), (per_block, width))
    panel = jax.ShapeDtypeStruct((row_block, width), jnp.float32)
    letter = jax.ShapeDtypeStruct((row_block + samples, width), jnp.bfloat16)
    eight = jax.ShapeDtypeStruct((8, width), jnp.float32)

    samples_shape = jax.ShapeDtypeStruct(activations.shape, activations.dtype)
    message, activations = call_whole(
        head_kernel, [letter, samples_shape], weights, blocks, activations
    )
    across = None

    def load(second):
        nonlocal across
        store, across, second = load_first(ring, gram_old, activations, second)
        return store, across, second

    own, received, store, (trace,) = ring_apply(ring, gram_old, message, activations, load)
    held = jax.ShapeDtypeStruct(store.shape, store.dtype)
    grad, message, store = call_whole(
        turn_kernel, [panel, letter, held], own, received, blocks, activations, store, alias={4: 2}
    )

    def keep(second):
        return store, across, second

    own, received, _, _ = ring_apply(ring, None, message, activations, keep)
    curve, sums = call_whole(curve_kernel, [panel, eight], trace, grad, own, received, blocks)
    sums = sum_part(sums, count)
    last = functools.partial(last_kernel, float(count * row_block))
    return call_whole(last, [panel], sums, grad, curve, weights, blocks)[0]


def solution(mesh):
    placed = (
        P(("groups", "row"), "col"),
        P("groups", "row"),
        P("row", ("groups", "col")),
        P(None, "groups"),
    )
    return jax.shard_map(
        per_device,
        mesh=mesh,
        in_specs=placed,
        out_specs=P("row", ("groups", "col")),
        check_vma=False,
    )
```

```python
import functools

import jax
import jax.numpy as jnp
from jax import lax
from jax.experimental import pallas as pl
from jax.experimental.pallas import tpu as pltpu
from jax.sharding import PartitionSpec as P

BLK = 128
TILES = 1
PARTS = 4
LIMIT = 8 * 1024 * 1024
AXES = ("row", "col")
WEIGHTS = ((1, 1, 0.3, 0.3, 8, 0.02, 0.02), (1, 0.02, 0.3, 2, 4, 0.3, 4))

damping_ratio = 0.3
epsilon = 1e-06


def swap(value, axis, distance):
    return lax.ppermute(value, axis, [(i, i ^ distance) for i in range(lax.axis_size(axis))])


def sum_part(value, count):
    devices = 2 * count
    unit = devices // 2
    while unit:
        value += lax.ppermute(value, AXES, [(i, i ^ unit) for i in range(devices)])
        unit //= 2
    return value


def expand_local(block_mask, row_index, row_block, col_index, width_cols):
    if width_cols != BLK:
        row_ids = (row_index * row_block + jnp.arange(row_block, dtype=jnp.int32)) // BLK
        col_ids = (col_index * width_cols + jnp.arange(width_cols, dtype=jnp.int32)) // BLK
        return block_mask[row_ids][:, col_ids].astype(jnp.float32)
    piece = BLK
    while row_block % piece:
        piece //= 2
    column = lax.dynamic_index_in_dim(block_mask, col_index, 1, keepdims=False)
    column = jnp.repeat(column, BLK // piece) if piece != BLK else column
    count = row_block // piece
    own = lax.dynamic_slice_in_dim(column, row_index * count, count, 0).astype(jnp.float32)
    return jnp.broadcast_to(own[:, None, None], (count, piece, width_cols)).reshape(
        row_block, width_cols
    )


class Ring:
    def __init__(self, count):
        self.count = count
        self.order = list(range(0, count, 2)) + list(range(count - 1, 0, -2))
        self.last = count // 2 - 1

    def row(self, place):
        return self.order[place % self.count]

    def half(self, place):
        return self.row(place) * 2 // self.count

    def ahead(self, place):
        return int(place % self.count >= self.count // 2)

    def device(self, place, core):
        return self.row(place) * 2 + core

    def source(self, place, core, step):
        return place - 1 - step if core == self.ahead(place) else place + 1 + step

    def first_column(self, place, core, step):
        origin = self.ahead(self.source(place, core, step))
        return origin if core == self.ahead(place) else 1 - origin

    def places(self):
        return [(place, core) for place in range(self.count) for core in range(2)]

    def shift(self):
        pairs = []
        for place in range(self.count):
            pairs.append(
                (self.device(place, self.ahead(place)), self.device(place + 1, self.ahead(place + 1)))
            )
            pairs.append(
                (
                    self.device(place, 1 - self.ahead(place)),
                    self.device(place - 1, 1 - self.ahead(place - 1)),
                )
            )
        return pairs

    def hand_over(self, step):
        return [
            (self.device(place, core), self.device(place, 1 - core))
            for place, core in self.places()
            if self.half(self.source(place, core, step)) != core
        ]

    def slots(self):
        found = []
        for step in range(self.last):
            found.append((True, step))
            if self.hand_over(step):
                found.append((False, step))
        return found

    def loads(self, slot):
        base = 3 * (2 + len(self.slots()))
        return [base + slot + 1] if slot + 1 < self.count // 2 else []

    def entry(self, place, core, carrier, step):
        source = self.source(place, carrier, step)
        return [
            self.row(source) % (self.count // 2),
            int(self.half(source) == core),
            int(self.first_column(place, carrier, step) != core),
        ]

    def table(self):
        half = self.count // 2
        lines = [None] * (2 * self.count)
        for place, core in self.places():
            line = [self.row(place) % half, int(self.half(place) == core), 0]
            for carrier, step in self.slots():
                line += self.entry(place, core, core if carrier else 1 - core, step)
            line += self.entry(place, core, core, self.last)
            needed = [line[k] for k in range(0, len(line), 3) if line[k + 1]]
            line += needed
            lines[self.device(place, core)] = line
        return lines


def pick(ring, entry):
    device = lax.axis_index("row") * 2 + lax.axis_index("col")
    values = [line[entry] for line in ring.table()]
    picked = jnp.int32(values[0])
    for index, value in enumerate(values):
        if value != values[0]:
            picked = jnp.where(device == index, jnp.int32(value), picked)
    return picked


def block_copies(ring, load, gram, store, sems):
    rows = gram.shape[0]
    there = pl.ds(pl.multiple_of(pick(ring, load) * rows, BLK), rows)
    parts = [pl.ds(part * rows // PARTS, rows // PARTS) for part in range(PARTS)]
    return [
        pltpu.make_async_copy(gram.at[here, there], store.at[here, there], sems.at[part])
        for part, here in enumerate(parts)
    ]


def load_kernel(ring, load, gram, acts, second, store, across, passed, sems):
    copies = block_copies(ring, load, gram, store, sems)
    for copy in copies:
        copy.start()
    across[...] = acts[...].astype(jnp.float32).T.astype(across.dtype)
    for copy in copies:
        copy.wait()


def load_first(ring, gram, acts, second):
    whole = pl.BlockSpec(memory_space=pltpu.VMEM)
    return pl.pallas_call(
        functools.partial(load_kernel, ring, ring.loads(-1)[0]),
        in_specs=[pl.BlockSpec(memory_space=pltpu.HBM), whole, whole],
        out_specs=[whole] * 3,
        out_shape=[
            jax.ShapeDtypeStruct(gram.shape, gram.dtype),
            jax.ShapeDtypeStruct(acts.shape[::-1], acts.dtype),
            jax.ShapeDtypeStruct(second.shape, second.dtype),
        ],
        scratch_shapes=[pltpu.SemaphoreType.DMA((PARTS,))],
        input_output_aliases={2: 2},
        compiler_params=pltpu.CompilerParams(vmem_limit_bytes=LIMIT),
    )(gram, acts, second)


def product_kernel(ring, slot, loads, with_trace, first, second, across, *refs):
    copies = []
    if with_trace:
        acts, gram, _, own, other, store, trace, sems = refs
        trace[...] = jnp.zeros_like(trace)
    elif loads:
        gram, _, own, other, store, sems = refs[-6:]
    else:
        own, other, store = refs[-3:]
    if loads:
        copies = block_copies(ring, loads[0], gram, store, sems)
    for copy in copies:
        copy.start()
    rows, width = own.shape
    start = pl.multiple_of(pick(ring, 3 * slot) * rows, BLK)
    flip = pick(ring, 3 * slot + 2) == 1
    if slot == 0:
        own[...] = jnp.zeros_like(own)
        other[...] = jnp.zeros_like(other)

    @pl.when(pick(ring, 3 * slot + 1) == 1)
    def _():
        @pl.loop(0, TILES)
        def _(tile):
            size = rows // TILES
            here = pl.ds(pl.multiple_of(tile * size, size), size)
            lines = jnp.concatenate([store[here, pl.ds(start, rows)], across[here, :]], axis=1)
            panel = jnp.concatenate([first[...], second[...]], axis=1)
            result = jnp.dot(lines, panel, preferred_element_type=jnp.float32)
            left, right = result[:, :width], result[:, width:]
            own[here, :] += jnp.where(flip, right, left)
            other[here, :] += jnp.where(flip, left, right)

        if with_trace:
            add_diagonal(store, start, acts, trace)

    for copy in copies:
        copy.wait()


def add_diagonal(store, start, acts, trace):
    lines = lax.broadcasted_iota(jnp.int32, (BLK, BLK), 0)
    same = lines == lax.broadcasted_iota(jnp.int32, (BLK, BLK), 1)
    for block in range(acts.shape[1] // BLK):
        here = slice(block * BLK, (block + 1) * BLK)
        there = pl.ds(pl.multiple_of(start + block * BLK, BLK), BLK)
        square = store[here, there].astype(jnp.float32)
        diag = jnp.sum(jnp.where(same, square, 0.0), axis=0, keepdims=True)
        part = acts[:, here].astype(jnp.float32)
        diag += jnp.sum(part * part, axis=0, keepdims=True)
        trace[0:1, :] += diag.astype(jnp.bfloat16).astype(jnp.float32)


def product(ring, slot, loads, gram, store, message, across, acts, acc):
    rows = across.shape[0]
    width = message[0].shape[1]
    weight = WEIGHTS[gram is None][slot]
    whole = pl.BlockSpec(memory_space=pltpu.VMEM)
    with_trace = bool(loads) and slot == 0
    operands = [*message, across]
    aliases = {len(operands) + k: k for k in range(len(acc))}
    operands += acc
    in_specs = [whole] * (len(operands) + 1)
    out_shape = [jax.ShapeDtypeStruct((rows, width), jnp.float32)] * 2
    out_shape.append(jax.ShapeDtypeStruct(store.shape, store.dtype))
    scratch = []
    if with_trace:
        operands.append(acts)
        in_specs.append(whole)
        out_shape.append(jax.ShapeDtypeStruct((8, width), jnp.float32))
    aliases[len(operands) + bool(loads)] = 2
    if loads:
        operands.append(gram)
        in_specs.insert(len(operands) - 1, pl.BlockSpec(memory_space=pltpu.HBM))
        scratch = [pltpu.SemaphoreType.DMA((PARTS,))]
    operands.append(store)
    results = pl.pallas_call(
        functools.partial(product_kernel, ring, slot, loads, with_trace),
        in_specs=in_specs,
        out_specs=[whole] * len(out_shape),
        out_shape=out_shape,
        scratch_shapes=scratch,
        input_output_aliases=aliases,
        compiler_params=pltpu.CompilerParams(vmem_limit_bytes=LIMIT),
        cost_estimate=pl.CostEstimate(
            flops=int(weight * 4 * rows * rows * width),
            bytes_accessed=int(weight * 2 * rows * rows),
            transcendentals=0,
        ),
    )(*operands)
    return results[:2], results[2], results[3:]


def after(value, others):
    return lax.optimization_barrier((value, *others))[0]


def ring_apply(ring, gram, message, acts, early):
    first = message
    trace = []
    store, across, second = early(swap(message, "col", 1))
    ready = [(first, second)]
    acc = []
    slot = 0

    def work(others=()):
        nonlocal acc, store, slot, trace
        if not ready:
            return
        parts = ready.pop(0)
        parts = (after(parts[0], others), parts[1])
        loads = [] if gram is None else ring.loads(slot)
        acc, store, added = product(ring, slot, loads, gram, store, parts, across, acts, acc)
        trace = trace or added
        slot += 1

    def hand_over(step):
        if ring.hand_over(step):
            ready.append(tuple(swap(after(part, acc[:1]), "col", 1) for part in held))

    for step in range(ring.last):
        came = lax.ppermute(after(first, acc[:1]), AXES, ring.shift())
        if step:
            work([first])
        second = lax.ppermute(after(second, acc[:1]), AXES, ring.shift())
        if step:
            hand_over(step - 1)
            work()
        first = came
        held = (first, second)
        ready.append(held)
    first = lax.ppermute(after(first, acc[:1]), AXES, ring.shift())
    hand_over(ring.last - 1)
    while ready:
        work()
    last = (first, swap(after(first, acc[:1]), "col", 1))
    (own, other), store, _ = product(ring, slot, [], gram, store, last, across, acts, acc)
    return own, swap(other, "col", 1), store, trace


def put_message(message, acts, rows):
    message[rows:, :] = jnp.dot(
        acts[...], message[:rows, :], preferred_element_type=jnp.float32
    ).astype(message.dtype)


def head_kernel(weights, blocks, acts, message, kept_acts):
    rows = weights.shape[0]
    for block in range(rows // BLK):
        here = slice(block * BLK, (block + 1) * BLK)
        dense = weights[here, :]
        message[here, :] = (blocks[block : block + 1, :] * dense - dense).astype(message.dtype)
    put_message(message, acts, rows)
    kept_acts[...] = acts[...]


def turn_kernel(own, received, blocks, acts, _, grad, message, __):
    rows = own.shape[0]
    for block in range(rows // BLK):
        here = slice(block * BLK, (block + 1) * BLK)
        grad_first = own[here, :] + received[here, :]
        grad[here, :] = grad_first
        message[here, :] = (blocks[block : block + 1, :] * grad_first).astype(message.dtype)
    put_message(message, acts, rows)


def lane_sums(value):
    return jnp.sum(value, axis=0, keepdims=True)


def curve_kernel(trace, grad, own, received, blocks, curve_ref, sums_ref):
    rows = grad.shape[0]
    sums_ref[...] = jnp.zeros_like(sums_ref)
    sums_ref[0:1, :] = trace[0:1, :]
    for block in range(rows // BLK):
        here = slice(block * BLK, (block + 1) * BLK)
        kept = blocks[block : block + 1, :]
        curve = own[here, :] + received[here, :]
        curve_ref[here, :] = curve
        step_dir = kept * grad[here, :]
        masked = kept * curve
        sums_ref[1:2, :] += lane_sums(step_dir * step_dir)
        sums_ref[2:3, :] += lane_sums(step_dir * curve)
        sums_ref[3:4, :] += lane_sums(masked * masked)


def last_kernel(units, sums, grad, curve, weights, blocks, out_ref):
    totals = jnp.sum(sums[...], axis=1, keepdims=True)
    trace_total, grad_square = totals[0:1, :], totals[1:2, :]
    grad_curve, curve_square = totals[2:3, :], totals[3:4, :]
    damping = damping_ratio * trace_total / units
    step_first = grad_square / (grad_curve + damping * grad_square + epsilon)
    step_second = (grad_curve + damping * grad_square) / (
        curve_square + 2.0 * damping * grad_curve + damping * damping * grad_square + epsilon
    )
    rows = grad.shape[0]
    for block in range(rows // BLK):
        here = slice(block * BLK, (block + 1) * BLK)
        kept = blocks[block : block + 1, :]
        grad_first = grad[here, :]
        step_dir = kept * grad_first
        grad_second = grad_first - step_first * curve[here, :]
        out_ref[here, :] = (
            kept * weights[here, :] - step_first * step_dir - step_second * (kept * grad_second)
        )


def gather_apply(gram, activations, panel, col_index):
    half = gram.shape[1]
    full = lax.all_gather(panel, "row", axis=0, tiled=True)
    own_half = lax.dynamic_slice_in_dim(full, col_index * half, half, 0)
    need = lax.dynamic_slice_in_dim(full, (1 - col_index) * half, half, 0)
    other_half = swap(need, "col", 1)
    own = jnp.dot(gram, own_half, preferred_element_type=jnp.float32)
    partial = jnp.dot(gram, other_half, preferred_element_type=jnp.float32)
    low = lax.psum(jnp.dot(activations, panel, preferred_element_type=jnp.float32), "row")
    update = lax.dot_general(
        activations.astype(jnp.float32),
        low,
        (((0,), (0,)), ((), ())),
        precision=lax.Precision.HIGHEST,
        preferred_element_type=jnp.float32,
    )
    return own + swap(partial, "col", 1) + update


def per_device_general(gram_old, activations, weights, block_mask):
    row_block, half_width = gram_old.shape
    width_cols = weights.shape[1]
    units = lax.axis_size("row") * row_block
    row_index = lax.axis_index("row")
    col_index = lax.axis_index("col")
    mask_local = expand_local(block_mask, row_index, row_block, col_index, width_cols)
    kept_weights = mask_local * weights
    diff_low = (kept_weights - weights).astype(jnp.bfloat16)
    acts = activations.astype(jnp.float32)
    column_squares = jnp.sum(acts * acts, axis=0)
    grad_first = gather_apply(gram_old, activations, diff_low, col_index)
    place = row_index * row_block + jnp.arange(row_block, dtype=jnp.int32)
    place = place - col_index * half_width
    on_diagonal = jnp.arange(half_width, dtype=jnp.int32)[None, :] == place[:, None]
    new_gram = gram_old.astype(jnp.float32) + column_squares[:, None]
    new_gram = new_gram.astype(jnp.bfloat16).astype(jnp.float32)
    trace_part = jnp.sum(jnp.where(on_diagonal, new_gram, 0.0))
    step_dir = mask_local * grad_first
    curvature = gather_apply(gram_old, activations, step_dir.astype(jnp.bfloat16), col_index)
    masked_curve = mask_local * curvature
    sums = jnp.stack(
        [
            trace_part,
            jnp.sum(step_dir * step_dir),
            jnp.sum(step_dir * curvature),
            jnp.sum(masked_curve * masked_curve),
        ]
    )
    sums = lax.psum(sums, ("row", "col"))
    trace_total, grad_square, grad_curve, curve_square = sums[0], sums[1], sums[2], sums[3]
    damping = damping_ratio * trace_total / units
    step_first = grad_square / (grad_curve + damping * grad_square + epsilon)
    step_second = (grad_curve + damping * grad_square) / (
        curve_square + 2.0 * damping * grad_curve + damping * damping * grad_square + epsilon
    )
    grad_second = grad_first - step_first * curvature
    return kept_weights - step_first * step_dir - step_second * (mask_local * grad_second)


def call_whole(kernel, out_shape, *operands, alias={}):
    whole = pl.BlockSpec(memory_space=pltpu.VMEM)
    return pl.pallas_call(
        kernel,
        in_specs=[whole] * len(operands),
        out_specs=[whole] * len(out_shape),
        out_shape=out_shape,
        input_output_aliases=alias,
        compiler_params=pltpu.CompilerParams(vmem_limit_bytes=LIMIT),
    )(*operands)


def per_device(gram_old, activations, weights, block_mask):
    row_block, _ = gram_old.shape
    width = weights.shape[1]
    samples = activations.shape[0]
    count = lax.axis_size("row")
    if row_block % (BLK * TILES) or row_block % (16 * PARTS) or count not in (4, 8, 16) or width != BLK or samples % 16:
        return per_device_general(gram_old, activations, weights, block_mask)
    ring = Ring(count)
    row_index = lax.axis_index("row")
    col_index = lax.axis_index("col")
    per_block = row_block // BLK
    own_mask = lax.dynamic_slice(block_mask, (row_index * per_block, col_index), (per_block, 1))
    blocks = jnp.broadcast_to(own_mask.astype(jnp.float32), (per_block, width))
    panel = jax.ShapeDtypeStruct((row_block, width), jnp.float32)
    letter = jax.ShapeDtypeStruct((row_block + samples, width), jnp.bfloat16)
    eight = jax.ShapeDtypeStruct((8, width), jnp.float32)

    samples_shape = jax.ShapeDtypeStruct(activations.shape, activations.dtype)
    message, activations = call_whole(
        head_kernel, [letter, samples_shape], weights, blocks, activations
    )
    across = None

    def load(second):
        nonlocal across
        store, across, second = load_first(ring, gram_old, activations, second)
        return store, across, second

    own, received, store, (trace,) = ring_apply(ring, gram_old, message, activations, load)
    held = jax.ShapeDtypeStruct(store.shape, store.dtype)
    grad, message, store = call_whole(
        turn_kernel, [panel, letter, held], own, received, blocks, activations, store, alias={4: 2}
    )

    def keep(second):
        return store, across, second

    own, received, _, _ = ring_apply(ring, None, message, activations, keep)
    curve, sums = call_whole(curve_kernel, [panel, eight], trace, grad, own, received, blocks)
    sums = sum_part(sums, count)
    last = functools.partial(last_kernel, float(count * row_block))
    return call_whole(last, [panel], sums, grad, curve, weights, blocks)[0]


def solution(mesh):
    placed = (
        P(("groups", "row"), "col"),
        P("groups", "row"),
        P("row", ("groups", "col")),
        P(None, "groups"),
    )
    return jax.shard_map(
        per_device,
        mesh=mesh,
        in_specs=placed,
        out_specs=P("row", ("groups", "col")),
        check_vma=False,
    )
```
